512 devices in a mesh: dp: 16 (over z, core), expert: 32 (over y, x).
Axes of the slice: x: 4, y: 8, z: 8, core: 2. Of those that a mesh axis runs over, the one named last changes fastest.
Arguments:
- grad_values: bfloat16 [4096, 7168], P(('dp', 'expert')), may hold values from -6 to 6
- grad_scales: bfloat16 [4096], P(('dp', 'expert')), may hold values from 0.099609375 to 2
- hidden_act: bfloat16 [16, 128, 4096], P('dp', None, 'expert'), may hold values from -4 to 4
- down_weight: bfloat16 [4096, 7168], P('expert'), may hold values from -0.0625 to 0.0625
- slot_token: int32 [16, 2, 128], P('dp'), may hold values from 0 to 255, as said below
- slot_count: int32 [16, 2], P('dp'), may hold values from 32 to 128, as said below
- slot_gate: float32 [16, 2, 128], P('dp'), may hold values from 0.05 to 1
Outputs:
- hidden_grad: bfloat16 [16, 128, 4096], P('dp', None, 'expert')
- weight_grad: bfloat16 [4096, 7168], P('expert')
- gate_grad: float32 [4096, 2], P(('dp', 'expert'))
The draws below stay inside these ranges and needn't reach their ends.
Inputs may be any that keep to these rules, and one draw needn't show every extreme that they name: `slot_token`: within one expert and group the 128 slots name distinct tokens of the group. `slot_count`: live slots are the first ones of each expert and group; some expert of some group has all 128 slots live.
All inputs are finite; a program needn't handle non-finite values.
Results may differ from the reference program's by a relative error of at most 0.0057.
Values may be sent and summed in bfloat16 or wider, within the bound.
No kernel may reach another device: no remote copies, remote signals or barrier semaphores. Data moves between devices by JAX's collectives and lax.ppermute only.
A program may use at most 64 MiB of HBM per device.

```python
import math
import jax
import jax.numpy as jnp
from jax import lax

D = 7168
FW = 2048
EXPERTS = 2
GROUP = 256
TOKENS = 4096
CAP = 128
N_DP = 16


def draw_slot_token(key, part):
    key = jax.random.fold_in(key, 11)
    key_list = jax.random.split(key, N_DP * EXPERTS)
    orders = jax.vmap(lambda single: jax.random.permutation(single, GROUP))(key_list)
    return orders[:, :CAP].reshape(N_DP, EXPERTS, CAP).astype(jnp.int32)


def draw_slot_count(key, part):
    key = jax.random.fold_in(key, 23)
    key_list = jax.random.split(key, 5)
    counts = jax.random.randint(key_list[0], (N_DP, EXPERTS), CAP // 4, CAP + 1)
    low_group = jax.random.randint(key_list[1], (), 0, N_DP)
    full_group = (low_group + 1 + jax.random.randint(key_list[2], (), 0, N_DP - 1)) % N_DP
    low_expert = jax.random.randint(key_list[3], (), 0, EXPERTS)
    full_expert = jax.random.randint(key_list[4], (), 0, EXPERTS)
    counts = counts.at[low_group, low_expert].set(CAP // 4)
    counts = counts.at[full_group, full_expert].set(CAP)
    return counts.astype(jnp.int32)


def level_of(stream_key, extent, pieces, low, high):
    def one(dim, parts):
        heights = jax.random.uniform(jax.random.fold_in(jax.random.fold_in(stream_key, 6), dim), (parts,), jnp.float32, low / len(pieces), high / len(pieces))
        return jnp.repeat(jnp.exp(heights), extent[dim] // parts).reshape((-1,) + (1,) * (len(extent) - dim - 1))

    level = one(*pieces[0])
    for cut in pieces[1:]:
        level = level * one(*cut)
    return level


def noise(rng, extent, width, bound, pieces=(), kind=jnp.bfloat16):
    factor_of = level_of(rng, extent, pieces, -0.22, 0.18) if pieces else 1.0
    array = jax.random.normal(rng, extent, jnp.float32) * width * factor_of
    return jnp.minimum(jnp.maximum(array, -bound), bound).astype(kind)


def setup_inputs(seed: int = 0) -> dict:
    arg_keys = jax.random.split(jax.random.key(seed), 8)
    return {
        "grad_values": noise(arg_keys[0], (TOKENS, D), 1.0, 6.0, ((0, 512),)),
        "grad_scales": jnp.clip(jnp.exp(math.log(2.0) - 2.9996462 * jax.random.uniform(arg_keys[1], (TOKENS,), jnp.float32) ** level_of(arg_keys[1], (TOKENS,), ((0, 512),), -0.2, 0.2)), 0.099609375, 2.0).astype(jnp.bfloat16),
        "hidden_act": noise(arg_keys[2], (N_DP, CAP, EXPERTS * FW), 0.25, 4.0, ((0, 16), (2, 32))),
        "down_weight": noise(arg_keys[3], (EXPERTS * FW, D), D ** -0.5, 0.0625, ((0, 32),)),
        "slot_token": draw_slot_token(jax.random.fold_in(arg_keys[7], 71), 0),
        "slot_count": draw_slot_count(jax.random.fold_in(arg_keys[7], 71), 0),
        "slot_gate": jnp.clip(0.05 + 0.95 * jax.random.uniform(arg_keys[6], (N_DP, EXPERTS, CAP), jnp.float32) ** level_of(arg_keys[6], (N_DP, EXPERTS, CAP), ((0, 16),), -0.2, 0.2), 0.05, 1.0),
    }


def reference(grad_values, grad_scales, hidden_act, down_weight, slot_token, slot_count, slot_gate):
    down_rows = down_weight.reshape(EXPERTS, FW, D).astype(jnp.float32)

    def per_group(total, which):
        values = lax.dynamic_slice_in_dim(grad_values, which * GROUP, GROUP, 0)
        scales = lax.dynamic_slice_in_dim(grad_scales, which * GROUP, GROUP, 0)
        slot_tok = slot_token[which]
        slot_live = jnp.arange(CAP, dtype=jnp.int32)[None, :] < slot_count[which][:, None]
        picked = values[slot_tok].astype(jnp.float32) * scales[slot_tok].astype(jnp.float32)[..., None]
        routed = jnp.where(slot_live[..., None], picked, 0.0).astype(jnp.bfloat16)
        project = jnp.einsum("esd,efd->esf", routed.astype(jnp.float32), down_rows)
        slot_gw = slot_gate[which]
        hidden = hidden_act[which].reshape(CAP, EXPERTS, FW).transpose(1, 0, 2).astype(jnp.float32)
        grad_hidden = (slot_gw[..., None] * project).astype(jnp.bfloat16)
        grad_hidden = grad_hidden.transpose(1, 0, 2).reshape(CAP, EXPERTS * FW)
        weighted = (slot_gw[..., None] * hidden).astype(jnp.bfloat16)
        weight_part = jnp.einsum("esf,esd->efd", weighted.astype(jnp.float32), routed.astype(jnp.float32))
        partial_sum = jnp.sum(hidden * project, axis=2)
        onehot = ((slot_tok[..., None] == jnp.arange(GROUP, dtype=jnp.int32)) & slot_live[..., None]).astype(jnp.float32)
        gate_part = jnp.einsum("es,esg->ge", partial_sum, onehot)
        return total + weight_part, (grad_hidden, gate_part)

    total, outputs = lax.scan(per_group, jnp.zeros((EXPERTS, FW, D), jnp.float32), jnp.arange(N_DP, dtype=jnp.int32))
    hidden_grad, gate_grad = outputs
    weight_grad = total.reshape(EXPERTS * FW, D).astype(jnp.bfloat16)
    return hidden_grad, weight_grad, gate_grad.reshape(TOKENS, EXPERTS)
```

```python
import jax
import jax.numpy as jnp
from jax import lax
from jax.sharding import PartitionSpec as P

BF, F32 = jnp.bfloat16, jnp.float32


def on_device(grad_values, grad_scales, hidden_act, down_weight, slot_token, slot_count, slot_gate):
    nz, nc, ny, nx = (lax.axis_size(a) for a in "zcyx")
    experts = slot_token.shape[1]
    owner = lax.axis_index("y") // (ny // experts)
    rows, width = grad_values.shape
    group = rows * ny * nx
    pick = lambda a: lax.dynamic_index_in_dim(a[0], owner, 0, keepdims=False)
    tok, num, gate = pick(slot_token), pick(slot_count), pick(slot_gate)
    slots = tok.shape[0]
    live = jnp.arange(slots, dtype=jnp.int32) < num
    tok = jnp.where(live, tok, group)
    hidden = hidden_act[0]
    units = hidden.shape[1]

    scaled = (grad_values.astype(F32) * grad_scales.astype(F32)[:, None]).astype(BF)
    everything = lax.all_gather(scaled, ("y", "x"), axis=0, tiled=True)

    parts = nc * nx
    cols = width // parts
    send = scaled.reshape(rows, parts, cols).transpose(1, 0, 2)
    mine = lax.all_to_all(send, ("c", "x"), 0, 0)
    mine = mine.reshape(nc, nx * rows, cols)
    mine = lax.all_gather(mine, "y", axis=1, tiled=True)
    weighted = (gate[:, None] * hidden.astype(F32)).astype(BF)
    tok_row = jnp.broadcast_to(tok.astype(BF)[None, :], (16, slots))
    pack = jnp.concatenate([weighted, tok_row], axis=0)
    packs = lax.all_gather(pack, ("c", "x"), axis=0, tiled=False)
    packs = packs.reshape(nc, nx, slots + 16, units)
    toks = packs[:, 0, slots, :].astype(jnp.int32)
    pick_all = (toks[:, :, None] == jnp.arange(group, dtype=jnp.int32)).astype(BF)
    routed = jnp.einsum("gst,gtd->gsd", pick_all, mine, preferred_element_type=F32).astype(BF)
    part = jnp.einsum("gxsj,gsd->xjd", packs[:, :, :slots], routed, preferred_element_type=F32)
    per = units // nz
    part = part.astype(BF).reshape(nx, nz, per, cols).transpose(1, 0, 2, 3)
    got = lax.all_to_all(part.reshape(nz * nx, per, cols), ("z", "x"), 0, 0)
    total = jnp.sum(got.reshape(nz, nx, per, cols).astype(F32), axis=0).astype(BF)
    half = total.transpose(1, 0, 2).reshape(per, nx * cols)
    half = lax.all_gather(half, "z", axis=0, tiled=True)
    other = lax.ppermute(half, "c", [(i, nc - 1 - i) for i in range(nc)])
    first = lax.axis_index("c") == 0
    weight_grad = jnp.concatenate(
        [jnp.where(first, half, other), jnp.where(first, other, half)], axis=1
    )

    everything, half = lax.optimization_barrier((everything, half))
    dims = (((1,), (1,)), ((), ()))
    by_token = lax.dot_general(everything, down_weight, dims, preferred_element_type=F32)
    onehot = (tok[:, None] == jnp.arange(group, dtype=jnp.int32)).astype(F32)
    project = jnp.dot(onehot, by_token, precision=lax.Precision.HIGHEST)
    hidden_grad = (gate[:, None] * project).astype(BF)[None]
    partial = jnp.sum(hidden.astype(F32) * project, axis=1)
    per_token = jnp.dot(partial, onehot, precision=lax.Precision.HIGHEST)
    spread = lax.all_to_all(per_token.reshape(ny * nx, rows), ("y", "x"), 0, 0)
    gate_grad = spread.reshape(experts, -1, rows).sum(axis=1).T
    return hidden_grad, weight_grad, gate_grad


def solution(mesh):
    fine = jax.sharding.Mesh(mesh.devices.reshape(8, 2, 8, 4), ("z", "c", "y", "x"))
    dp, expert = ("z", "c"), ("y", "x")
    return jax.shard_map(
        on_device,
        mesh=fine,
        in_specs=(
            P(dp + expert, None),
            P(dp + expert),
            P(dp, None, expert),
            P(expert, None),
            P(dp, None, None),
            P(dp, None),
            P(dp, None, None),
        ),
        out_specs=(P(dp, None, expert), P(expert, None), P(dp + expert, None)),
        check_vma=False,
    )
```

```python
import jax
import jax.numpy as jnp
from jax import lax
from jax.sharding import PartitionSpec as P

BF, F32 = jnp.bfloat16, jnp.float32
DP, EXPERT = ("z", "c"), ("e", "q", "x")


def on_device(grad_values, grad_scales, hidden_act, down_weight, slot_token, slot_count, slot_gate):
    nz, nc, ne, nq, nx = (lax.axis_size(a) for a in "zceqx")
    core, owner = lax.axis_index("c"), lax.axis_index("e")
    rows, width = grad_values.shape
    ny = ne * nq
    group = rows * ny * nx
    pick = lambda a: lax.dynamic_index_in_dim(a[0], owner, 0, keepdims=False)
    tok, num, gate = pick(slot_token), pick(slot_count), pick(slot_gate)
    slots = tok.shape[0]
    live = jnp.arange(slots, dtype=jnp.int32) < num
    tok = jnp.where(live, tok, group)
    hidden = hidden_act[0]
    units = hidden.shape[1]
    cols = width // (nc * nq)

    scaled = (grad_values.astype(F32) * grad_scales.astype(F32)[:, None]).astype(BF)
    send = scaled.reshape(rows, nc, 1, nq, cols).transpose(1, 2, 3, 0, 4)
    send = jnp.broadcast_to(send, (nc, ne, nq, rows, cols)).reshape(-1, rows, cols)
    mine = lax.all_to_all(send, ("c", "e", "q"), 0, 0)

    weighted = (gate[:, None] * hidden.astype(F32)).astype(BF)
    tok_row = jnp.broadcast_to(tok.astype(BF)[None, :], (16, slots))
    pack = jnp.concatenate([weighted, tok_row], axis=0)
    packs = jnp.broadcast_to(pack[None], (nc * nq,) + pack.shape)
    packs = lax.all_to_all(packs, ("c", "q"), 0, 0)

    own_cols = lax.dynamic_slice_in_dim(down_weight, core * (nq * cols), nq * cols, 1)
    own_cols = own_cols.reshape(units, nq, cols).transpose(1, 0, 2)
    own_cols, mine = lax.optimization_barrier((own_cols, mine))
    w_cols = lax.all_to_all(own_cols, "q", 0, 0)

    mine = mine.reshape(nc, ny * rows, cols)
    mine = lax.all_gather(mine, "x", axis=1, tiled=True)
    ids = jnp.arange(group, dtype=jnp.int32).reshape(ny, nx, rows)
    ids = ids.transpose(1, 0, 2).reshape(-1)

    packs = packs.reshape(nc, nq, slots + 16, units)
    toks = packs[:, 0, slots, :].astype(jnp.int32)
    pick_all = (toks[:, :, None] == ids).astype(BF)
    routed = jnp.einsum("gst,gtd->gsd", pick_all, mine, preferred_element_type=F32).astype(BF)
    part = jnp.einsum("gqsj,gsd->qjd", packs[:, :, :slots], routed, preferred_element_type=F32)
    per = units // nz
    part = part.astype(BF).reshape(nq, nz, per, cols).transpose(1, 0, 2, 3)
    got = lax.all_to_all(part, "z", 0, 0)

    proj = jnp.einsum("gsd,qjd->gqsj", routed, w_cols, preferred_element_type=F32).astype(BF)
    proj = lax.all_to_all(proj.reshape(nc * nq, slots, units), ("c", "q"), 0, 0)

    total = jnp.sum(got.astype(F32), axis=0).astype(BF)
    total = lax.all_to_all(total, "q", 0, 0)
    half = total.transpose(1, 0, 2).reshape(per, nq * cols)

    project = jnp.sum(proj.astype(F32), axis=0)
    hidden_grad = (gate[:, None] * project).astype(BF)[None]
    partial = jnp.sum(hidden.astype(F32) * project, axis=1)
    onehot = (tok[:, None] == jnp.arange(group, dtype=jnp.int32)).astype(F32)
    per_token = jnp.dot(partial, onehot, precision=lax.Precision.HIGHEST)
    spread = lax.all_to_all(per_token.reshape(ny * nx, rows), EXPERT, 0, 0)
    gate_grad = spread.reshape(ne, -1, rows).sum(axis=1).T

    half = lax.all_gather(half, "z", axis=0, tiled=True)
    cut = units // 2
    weight_grad = jnp.concatenate(
        [lax.all_gather(half[i : i + cut], "c", axis=1, tiled=True) for i in (0, cut)], axis=0
    )
    return hidden_grad, weight_grad, gate_grad


def solution(mesh):
    fine = jax.sharding.Mesh(mesh.devices.reshape(8, 2, 2, 4, 4), DP + EXPERT)
    return jax.shard_map(
        on_device,
        mesh=fine,
        in_specs=(
            P(DP + EXPERT, None),
            P(DP + EXPERT),
            P(DP, None, EXPERT),
            P(EXPERT, None),
            P(DP, None, None),
            P(DP, None),
            P(DP, None, None),
        ),
        out_specs=(P(DP, None, EXPERT), P(EXPERT, None), P(DP + EXPERT, None)),
        check_vma=False,
    )
```

```python
import jax
import jax.numpy as jnp
from jax import lax
from jax.sharding import PartitionSpec as P

BF, F32 = jnp.bfloat16, jnp.float32
DP, EXPERT = ("h", "l", "c"), ("e", "q", "x")
SIZES = (4, 2, 2, 2, 4, 4)
SPLIT = ("l", "c", "x")
LANES, TILES = 128, 4
EXTRA = 16


def tiles(a):
    *lead, rows, cols = a.shape
    a = jnp.pad(a, [(0, 0)] * (a.ndim - 1) + [(0, TILES * LANES - cols)])
    a = jnp.swapaxes(a.reshape(*lead, rows, TILES, LANES), -3, -2)
    return a.reshape(*lead, TILES * rows, LANES)


def untiled(a, cols):
    *lead, rows, _ = a.shape
    a = jnp.swapaxes(a.reshape(*lead, TILES, rows // TILES, LANES), -3, -2)
    return a.reshape(*lead, rows // TILES, TILES * LANES)[..., :cols]


def slices(a):
    rows, width = a.shape
    a = a.reshape(rows, 8, 2, width // 16)
    return tiles(a.transpose(2, 1, 0, 3).reshape(16, rows, width // 16))


def on_device(grad_values, grad_scales, hidden_act, down_weight, slot_token, slot_count, slot_gate):
    nh, nl, nc, ne, nq, nx = (lax.axis_size(a) for a in "hlceqx")
    low, core, owner = (lax.axis_index(a) for a in "lce")
    rows, width = grad_values.shape
    ny, quarters = ne * nq, nl * nc
    group = rows * ny * nx
    pick = lambda a: lax.dynamic_index_in_dim(a[0], owner, 0, keepdims=False)
    tok, num, gate = pick(slot_token), pick(slot_count), pick(slot_gate)
    slots = tok.shape[0]
    live = jnp.arange(slots, dtype=jnp.int32) < num
    tok = jnp.where(live, tok, group)
    hidden = hidden_act[0]
    units = hidden.shape[1]
    dests = quarters * nx

    scaled = (grad_values.astype(F32) * grad_scales.astype(F32)[:, None]).astype(BF)
    weighted = (gate[:, None] * hidden.astype(F32)).astype(BF)
    tok_row = jnp.broadcast_to(tok.astype(BF)[None, :], (EXTRA, slots))
    pack = jnp.concatenate([weighted, tok_row], axis=0)
    share = units // quarters
    w_rows = lax.dynamic_slice_in_dim(down_weight, (low * nc + core) * share, share, 0)
    send = jnp.concatenate(
        [
            slices(scaled),
            jnp.broadcast_to(pack[None], (dests,) + pack.shape),
            slices(w_rows),
        ],
        axis=1,
    )
    got = lax.all_to_all(send, SPLIT, 0, 0)
    a, b, cols = TILES * rows, TILES * rows + slots + EXTRA, width // dests
    mine = untiled(got[:, :a], cols).reshape(quarters, nx * rows, cols)
    mine = lax.all_gather(mine, ("e", "q"), axis=0)
    packs = got[:, a:b].reshape(quarters, nx, slots + EXTRA, units)
    w_cols = untiled(got[:, b:], cols).reshape(quarters, nx, share, cols)

    toks = packs[:, 0, slots, :].astype(jnp.int32)
    ids = jnp.arange(group, dtype=jnp.int32)
    pick_all = (toks[:, :, None] == ids).astype(BF)
    mine = mine.transpose(1, 0, 2, 3).reshape(quarters, group, cols)
    routed = jnp.einsum("gst,gtd->gsd", pick_all, mine, preferred_element_type=F32).astype(BF)
    part = jnp.einsum("gxsj,gsd->xjd", packs[:, :, :slots], routed, preferred_element_type=F32)
    part = part.astype(BF).reshape(nx, nh, units // nh, cols).transpose(1, 0, 2, 3)
    sums = lax.all_to_all(part, "h", 0, 0)
    w_cols = w_cols.transpose(1, 0, 2, 3).reshape(nx, units, cols)
    proj = jnp.einsum("gsd,xjd->gxsj", routed, w_cols, preferred_element_type=F32).astype(BF)

    sums = jnp.sum(sums.astype(F32), axis=0).astype(BF)
    per = units // nh // quarters
    sums = sums.reshape(nx, quarters, per, cols).transpose(1, 0, 2, 3)
    send = jnp.concatenate(
        [tiles(sums).reshape(dests, TILES * per, LANES), proj.reshape(dests, slots, units)], axis=1
    )
    got = lax.all_to_all(send, SPLIT, 0, 0)
    a = TILES * per
    block = untiled(got[:, :a], cols).reshape(nl, nc * nx, per, cols)
    block = block.transpose(2, 1, 0, 3).reshape(per, width)
    project = jnp.sum(got[:, a:].astype(F32), axis=0)
    hidden_grad = (gate[:, None] * project).astype(BF)[None]
    partial = jnp.sum(hidden.astype(F32) * project, axis=1)
    onehot = (tok[:, None] == ids).astype(F32)
    per_token = jnp.dot(partial, onehot, precision=lax.Precision.HIGHEST)
    spread = lax.all_to_all(per_token.reshape(ny * nx, rows), EXPERT, 0, 0)
    gate_grad = spread.reshape(ne, -1, rows).sum(axis=1).T

    block = lax.all_gather(block, ("h", "l"), axis=0)
    cut = nh * nl // 2
    halves = [lax.all_gather(block[i : i + cut], "c", axis=1, tiled=True) for i in (0, cut)]
    weight_grad = jnp.concatenate([a.reshape(-1, width) for a in halves], axis=0)
    return hidden_grad, weight_grad, gate_grad


def solution(mesh):
    fine = jax.sharding.Mesh(mesh.devices.reshape(SIZES), DP + EXPERT)
    return jax.shard_map(
        on_device,
        mesh=fine,
        in_specs=(
            P(DP + EXPERT, None),
            P(DP + EXPERT),
            P(DP, None, EXPERT),
            P(EXPERT, None),
            P(DP, None, None),
            P(DP, None),
            P(DP, None, None),
        ),
        out_specs=(P(DP, None, EXPERT), P(EXPERT, None), P(DP + EXPERT, None)),
        check_vma=False,
    )
```

```python
import jax
import jax.numpy as jnp
from jax import lax
from jax.sharding import PartitionSpec as P

BF, F32 = jnp.bfloat16, jnp.float32
DP, EXPERT = ("h", "l", "c"), ("e", "q", "x")
SIZES = (4, 2, 2, 2, 4, 4)
SPLIT = ("l", "c", "x")
LANES, TILES = 128, 4
EXTRA = 16


def tiles(a):
    *lead, rows, cols = a.shape
    a = jnp.pad(a, [(0, 0)] * (a.ndim - 1) + [(0, TILES * LANES - cols)])
    a = jnp.swapaxes(a.reshape(*lead, rows, TILES, LANES), -3, -2)
    return a.reshape(*lead, TILES * rows, LANES)


def untiled(a, cols):
    *lead, rows, _ = a.shape
    a = jnp.swapaxes(a.reshape(*lead, TILES, rows // TILES, LANES), -3, -2)
    return a.reshape(*lead, rows // TILES, TILES * LANES)[..., :cols]


def slices(a):
    rows, width = a.shape
    a = a.reshape(rows, 8, 2, width // 16)
    return tiles(a.transpose(2, 1, 0, 3).reshape(16, rows, width // 16))


def on_device(grad_values, grad_scales, hidden_act, down_weight, slot_token, slot_count, slot_gate):
    nh, nl, nc, ne, nq, nx = (lax.axis_size(a) for a in "hlceqx")
    low, core, owner = (lax.axis_index(a) for a in "lce")
    rows, width = grad_values.shape
    ny, quarters = ne * nq, nl * nc
    group = rows * ny * nx
    pick = lambda a: lax.dynamic_index_in_dim(a[0], owner, 0, keepdims=False)
    tok, num, gate = pick(slot_token), pick(slot_count), pick(slot_gate)
    slots = tok.shape[0]
    live = jnp.arange(slots, dtype=jnp.int32) < num
    tok = jnp.where(live, tok, group)
    hidden = hidden_act[0]
    units = hidden.shape[1]
    dests = quarters * nx

    scaled = (grad_values.astype(F32) * grad_scales.astype(F32)[:, None]).astype(BF)
    cols = width // dests
    mine = lax.all_to_all(slices(scaled), SPLIT, 0, 0)

    weighted = (gate[:, None] * hidden.astype(F32)).astype(BF)
    tok_row = jnp.broadcast_to(tok.astype(BF)[None, :], (EXTRA, slots))
    pack = jnp.concatenate([weighted, tok_row], axis=0)
    share = units // quarters
    w_rows = lax.dynamic_slice_in_dim(down_weight, (low * nc + core) * share, share, 0)
    send = jnp.concatenate(
        [jnp.broadcast_to(pack[None], (dests,) + pack.shape), slices(w_rows)], axis=1
    )
    send, mine = lax.optimization_barrier((send, mine))
    got = lax.all_to_all(send, SPLIT, 0, 0)
    mine = untiled(mine, cols).reshape(quarters, nx * rows, cols)
    mine = lax.all_gather(mine, ("e", "q"), axis=0)
    b = slots + EXTRA
    packs = got[:, :b].reshape(quarters, nx, slots + EXTRA, units)
    w_cols = untiled(got[:, b:], cols).reshape(quarters, nx, share, cols)

    toks = packs[:, 0, slots, :].astype(jnp.int32)
    ids = jnp.arange(group, dtype=jnp.int32)
    pick_all = (toks[:, :, None] == ids).astype(BF)
    mine = mine.transpose(1, 0, 2, 3).reshape(quarters, group, cols)
    routed = jnp.einsum("gst,gtd->gsd", pick_all, mine, preferred_element_type=F32).astype(BF)
    part = jnp.einsum("gxsj,gsd->xjd", packs[:, :, :slots], routed, preferred_element_type=F32)
    part = part.astype(BF).reshape(nx, nh, units // nh, cols).transpose(1, 0, 2, 3)
    sums = lax.all_to_all(part, "h", 0, 0)
    w_cols = w_cols.transpose(1, 0, 2, 3).reshape(nx, units, cols)
    proj = jnp.einsum("gsd,xjd->gxsj", routed, w_cols, preferred_element_type=F32).astype(BF)

    per = units // nh // quarters
    sums = jnp.sum(sums.astype(F32), axis=0).astype(BF)
    sums = sums.reshape(nx, quarters, per, cols).transpose(1, 0, 2, 3)
    send = jnp.concatenate(
        [tiles(sums).reshape(dests, TILES * per, LANES), proj.reshape(dests, slots, units)], axis=1
    )
    got = lax.all_to_all(send, SPLIT, 0, 0)
    a = TILES * per
    block = untiled(got[:, :a], cols).reshape(nl, nc * nx, per, cols)
    block = block.transpose(2, 1, 0, 3).reshape(per, width)
    proj = got[:, a:]
    project = jnp.sum(proj.astype(F32), axis=0)
    hidden_grad = (gate[:, None] * project).astype(BF)[None]
    partial = jnp.sum(hidden.astype(F32) * project, axis=1)
    onehot = (tok[:, None] == ids).astype(F32)
    per_token = jnp.dot(partial, onehot, precision=lax.Precision.HIGHEST)
    spread = lax.all_to_all(per_token.reshape(ny * nx, rows), EXPERT, 0, 0)
    gate_grad = spread.reshape(ne, -1, rows).sum(axis=1).T

    block = lax.all_gather(block, ("h", "l"), axis=0)
    cut = nh * nl // 2
    halves = [lax.all_gather(block[i : i + cut], "c", axis=1, tiled=True) for i in (0, cut)]
    weight_grad = jnp.concatenate([a.reshape(-1, width) for a in halves], axis=0)
    return hidden_grad, weight_grad, gate_grad


def solution(mesh):
    fine = jax.sharding.Mesh(mesh.devices.reshape(SIZES), DP + EXPERT)
    return jax.shard_map(
        on_device,
        mesh=fine,
        in_specs=(
            P(DP + EXPERT, None),
            P(DP + EXPERT),
            P(DP, None, EXPERT),
            P(EXPERT, None),
            P(DP, None, None),
            P(DP, None),
            P(DP, None, None),
        ),
        out_specs=(P(DP, None, EXPERT), P(EXPERT, None), P(DP + EXPERT, None)),
        check_vma=False,
    )
```

```python
import jax
import jax.numpy as jnp
from jax import lax
from jax.experimental import pallas as pl
from jax.experimental.pallas import tpu as pltpu
from jax.sharding import PartitionSpec as P

BF, F32, I32 = jnp.bfloat16, jnp.float32, jnp.int32
DP, EXPERT = ("h", "l", "c"), ("e", "q", "x")
H, L, C, E, Q, X = SIZES = (4, 2, 2, 2, 4, 4)
SPLIT = ("l", "c", "x")
QUARTERS, PARTS = L * C, L * C * X
LANES, TILES = 128, 4
WIDTH, SLOTS, UNITS, ROWS = 7168, 128, 128, 8
GROUP = E * Q * X * ROWS
COLS, WIDE = WIDTH // PARTS, TILES * LANES
PAIR = 2 * COLS
SHARE = UNITS // QUARTERS
CHUNK = UNITS // H
PER = CHUNK // QUARTERS
EXTRA = 16
PACK = SLOTS + EXTRA
BACK = TILES * PER


def lanes(shape):
    return lax.broadcasted_iota(I32, shape, len(shape) - 1)


def column(row):
    n = row.shape[1]
    across, down = lanes((n, n)), lax.broadcasted_iota(I32, (n, n), 0)
    return jnp.sum(jnp.where(across == down, row, jnp.zeros_like(row)), axis=1, keepdims=True)


def slice_of(a, n, l):
    start = n * PAIR
    if l == 0:
        a = a[:, start : start + WIDE]
    else:
        a = pltpu.roll(a[:, start + PAIR - WIDE : start + PAIR], COLS, 1)
    return jnp.where(lanes(a.shape) < COLS, a, 0.0)


def tokens_kernel(values_ref, scales_ref, out_ref):
    scaled = values_ref[...].astype(F32) * column(scales_ref[...].astype(F32))
    for l in range(L):
        for n in range(C * X):
            out_ref[l * C * X + n] = slice_of(scaled, n, l)[:, :COLS].astype(BF)


def own_slots(where_ref, tok_ref, count_ref):
    owner = where_ref[0]
    tok = jnp.where(owner == 0, tok_ref[0:1, :], tok_ref[1:2, :])
    return jnp.where(lanes((1, SLOTS)) < count_ref[0, owner], tok, GROUP)


def own_gate(where_ref, gate_ref):
    return column(jnp.where(where_ref[0] == 0, gate_ref[0:1, :], gate_ref[1:2, :]))


def pack_kernel(where_ref, count_ref, tok_ref, gate_ref, hidden_ref, w_ref, out_ref):
    weighted = (own_gate(where_ref, gate_ref) * hidden_ref[...].astype(F32)).astype(BF)
    tok = own_slots(where_ref, tok_ref, count_ref).astype(F32)
    tok = jnp.broadcast_to(tok, (EXTRA, SLOTS)).astype(BF)
    w = w_ref[...].astype(F32)
    for l in range(L):
        for n in range(C * X):
            at = l * C * X + n
            out_ref[at, 0:SLOTS, :] = weighted
            out_ref[at, SLOTS:PACK, :] = tok
            part = slice_of(w, n, l).astype(BF)
            for t in range(TILES):
                low = PACK + t * SHARE
                out_ref[at, low : low + SHARE, :] = part[:, t * LANES : (t + 1) * LANES]


def weight_kernel(mine_ref, pack_ref, part_ref, routed_ref):
    routed_ref[:, COLS:] = jnp.zeros((QUARTERS * SLOTS, WIDE - COLS), BF)
    ids = lax.broadcasted_iota(I32, (GROUP, SLOTS), 0)
    first = (((0,), (0,)), ((), ()))
    for g in range(QUARTERS):
        tok = pack_ref[g * X, SLOTS:PACK, :].astype(F32)[0:1, :].astype(I32)
        picks = jnp.where(ids == tok, 1.0, 0.0).astype(BF)
        rows = mine_ref[:, g].reshape(GROUP, COLS)
        routed = lax.dot_general(picks, rows, first, preferred_element_type=F32)
        routed_ref[g * SLOTS : (g + 1) * SLOTS, :COLS] = routed.astype(BF)
    routed = routed_ref[:, :COLS]
    for x in range(X):
        weighted = jnp.concatenate([pack_ref[g * X + x, :SLOTS, :] for g in range(QUARTERS)], axis=0)
        part = lax.dot_general(weighted, routed, first, preferred_element_type=F32).astype(BF)
        for h in range(H):
            part_ref[h, x] = part[h * CHUNK : (h + 1) * CHUNK]


def project_kernel(routed_ref, pack_ref, out_ref):
    routed = routed_ref[...]
    for x in range(X):
        w = [
            jnp.concatenate(
                [pack_ref[q * X + x, PACK + t * SHARE : PACK + (t + 1) * SHARE, :] for q in range(QUARTERS)],
                axis=0,
            )
            for t in range(TILES)
        ]
        w = jnp.concatenate(w, axis=1)
        proj = lax.dot_general(routed, w, (((1,), (1,)), ((), ())), preferred_element_type=F32)
        for g in range(QUARTERS):
            out_ref[g * X + x] = proj[g * SLOTS : (g + 1) * SLOTS].astype(BF)


def back_kernel(sums_ref, proj_ref, out_ref):
    for x in range(X):
        total = sums_ref[0, x].astype(F32)
        for h in range(1, H):
            total = total + sums_ref[h, x].astype(F32)
        total = jnp.concatenate([total, jnp.zeros((CHUNK, WIDE - COLS), F32)], axis=1)
        for g in range(QUARTERS):
            rows = total[g * PER : (g + 1) * PER]
            rows = [rows[:, t * LANES : (t + 1) * LANES] for t in range(TILES)]
            out_ref[g * X + x, 0:BACK, :] = jnp.concatenate(rows, axis=0).astype(BF)
            out_ref[g * X + x, BACK:, :] = proj_ref[g * X + x]


def finish_kernel(
    where_ref, count_ref, tok_ref, gate_ref, hidden_ref, got_ref, grad_ref, spread_ref, block_ref
):
    project = got_ref[0, BACK:, :].astype(F32)
    for n in range(1, PARTS):
        project = project + got_ref[n, BACK:, :].astype(F32)
    grad_ref[...] = (own_gate(where_ref, gate_ref) * project).astype(BF)
    partial = jnp.sum(hidden_ref[...].astype(F32) * project, axis=1, keepdims=True)
    tok = column(own_slots(where_ref, tok_ref, count_ref))
    device = jnp.where(lanes((SLOTS, E * Q * X)) == tok // ROWS, 1.0, 0.0)
    row = jnp.where(lanes((SLOTS, ROWS)) == tok % ROWS, partial, 0.0)
    spread_ref[...] = lax.dot_general(
        device, row, (((0,), (0,)), ((), ())), precision=lax.Precision.HIGHEST, preferred_element_type=F32
    )
    low = lanes((PER, LANES)) < COLS % LANES
    for n in range(C * X):
        a, b = (got_ref[l * C * X + n, 0:BACK, :].astype(F32) for l in range(L))
        a, b = ([p[t * PER : (t + 1) * PER] for t in range(TILES)] for p in (a, b))
        b = [pltpu.roll(p, COLS % LANES, 1) for p in b]
        tiles = a[:-1] + [jnp.where(low, p, r) for p, r in zip([a[-1]] + b[:-1], b)]
        block_ref[:, n * PAIR : (n + 1) * PAIR] = jnp.concatenate(tiles, axis=1).astype(BF)


VM, SM = pl.BlockSpec(memory_space=pltpu.VMEM), pl.BlockSpec(memory_space=pltpu.SMEM)


def call(kernel, outs, *args, scalars=0, flops=0):
    outs = [jax.ShapeDtypeStruct(s, d) for s, d in outs]
    nbytes = sum(a.size * a.dtype.itemsize for a in list(args) + outs)
    return pl.pallas_call(
        kernel,
        out_shape=outs,
        in_specs=[SM] * scalars + [VM] * (len(args) - scalars),
        out_specs=[VM] * len(outs),
        cost_estimate=pl.CostEstimate(flops=flops, bytes_accessed=nbytes, transcendentals=0),
        compiler_params=pltpu.CompilerParams(vmem_limit_bytes=32 * 1024 * 1024),
    )(*args)


def on_device(grad_values, grad_scales, hidden_act, down_weight, slot_token, slot_count, slot_gate):
    low, core, owner = (lax.axis_index(a) for a in "lce")
    hidden, tok, gate = hidden_act[0], slot_token[0], slot_gate[0]
    where = owner[None].astype(I32)

    (send,) = call(
        tokens_kernel, [((PARTS, ROWS, COLS), BF)], grad_values, grad_scales.reshape(1, ROWS)
    )
    mine = lax.all_to_all(send, SPLIT, 0, 0)

    w_rows = lax.dynamic_slice_in_dim(down_weight, (low * C + core) * SHARE, SHARE, 0)
    (pack,) = call(
        pack_kernel,
        [((PARTS, PACK + TILES * SHARE, LANES), BF)],
        where, slot_count, tok, gate, hidden, w_rows,
        scalars=2,
    )
    pack, mine = lax.optimization_barrier((pack, mine))
    pack = lax.all_to_all(pack, SPLIT, 0, 0)
    mine = lax.all_gather(mine.reshape(QUARTERS, X * ROWS, COLS), ("e", "q"), axis=0)

    part, routed = call(
        weight_kernel,
        [((H, X, CHUNK, COLS), BF), ((QUARTERS * SLOTS, WIDE), BF)],
        mine, pack,
        flops=2 * QUARTERS * SLOTS * COLS * (GROUP + X * UNITS),
    )
    sums = lax.all_to_all(part, "h", 0, 0)
    (proj,) = call(
        project_kernel,
        [((PARTS, SLOTS, UNITS), BF)],
        routed, pack,
        flops=2 * QUARTERS * SLOTS * WIDE * X * UNITS,
    )

    (send,) = call(back_kernel, [((PARTS, BACK + SLOTS, LANES), BF)], sums, proj)
    got = lax.all_to_all(send, SPLIT, 0, 0)
    hidden_grad, spread, block = call(
        finish_kernel,
        [((SLOTS, UNITS), BF), ((E * Q * X, ROWS), F32), ((PER, WIDTH), BF)],
        where, slot_count, tok, gate, hidden, got,
        scalars=2,
    )
    spread = lax.all_to_all(spread, EXPERT, 0, 0)
    gate_grad = spread.reshape(E, Q * X, ROWS).sum(axis=1).T

    block = lax.all_gather(block, ("h", "l"), axis=0)
    cut = H * L // 2
    halves = [lax.all_gather(block[i : i + cut], "c", axis=1, tiled=True) for i in (0, cut)]
    weight_grad = jnp.concatenate([a.reshape(-1, WIDTH) for a in halves], axis=0)
    return hidden_grad[None], weight_grad, gate_grad


def solution(mesh):
    fine = jax.sharding.Mesh(mesh.devices.reshape(SIZES), DP + EXPERT)
    return jax.shard_map(
        on_device,
        mesh=fine,
        in_specs=(
            P(DP + EXPERT, None),
            P(DP + EXPERT),
            P(DP, None, EXPERT),
            P(EXPERT, None),
            P(DP, None, None),
            P(DP, None),
            P(DP, None, None),
        ),
        out_specs=(P(DP, None, EXPERT), P(EXPERT, None), P(DP + EXPERT, None)),
        check_vma=False,
    )
```

```python
import jax
import jax.numpy as jnp
from jax import lax
from jax.experimental import pallas as pl
from jax.experimental.pallas import tpu as pltpu
from jax.sharding import PartitionSpec as P

BF, F32, I32 = jnp.bfloat16, jnp.float32, jnp.int32
DP, EXPERT = ("h", "l", "c"), ("e", "m", "n", "x")
H, L, C, E, M, N, X = SIZES = (4, 2, 2, 2, 2, 2, 4)
SPLIT = ("l", "c", "x")
QUARTERS, PARTS = L * C, L * C * X
LANES, TILES = 128, 4
WIDTH, SLOTS, UNITS, ROWS = 7168, 128, 128, 8
GROUP = E * M * N * X * ROWS
COLS, WIDE = WIDTH // PARTS, TILES * LANES
PAIR = 2 * COLS
SHARE = UNITS // QUARTERS
CHUNK = UNITS // H
PER = CHUNK // C
EXTRA = 16
PACK = SLOTS + EXTRA
BACK = TILES * PER


def lanes(shape):
    return lax.broadcasted_iota(I32, shape, len(shape) - 1)


def column(row):
    n = row.shape[1]
    across, down = lanes((n, n)), lax.broadcasted_iota(I32, (n, n), 0)
    return jnp.sum(jnp.where(across == down, row, jnp.zeros_like(row)), axis=1, keepdims=True)


def slice_of(a, n, l):
    start = n * PAIR
    if l == 0:
        a = a[:, start : start + WIDE]
    else:
        a = pltpu.roll(a[:, start + PAIR - WIDE : start + PAIR], COLS, 1)
    return jnp.where(lanes(a.shape) < COLS, a, 0.0)


def tokens_kernel(values_ref, scales_ref, out_ref):
    scaled = values_ref[...].astype(F32) * column(scales_ref[...].astype(F32))
    for l in range(L):
        for n in range(C * X):
            part = slice_of(scaled, n, l)[:, :COLS].astype(BF)
            for i in range(N):
                out_ref[((l * C + n // X) * N + i) * X + n % X] = part


def own_slots(where_ref, tok_ref, count_ref):
    owner = where_ref[0]
    tok = jnp.where(owner == 0, tok_ref[0:1, :], tok_ref[1:2, :])
    return jnp.where(lanes((1, SLOTS)) < count_ref[0, owner], tok, GROUP)


def own_gate(where_ref, gate_ref):
    return column(jnp.where(where_ref[0] == 0, gate_ref[0:1, :], gate_ref[1:2, :]))


def pack_kernel(where_ref, count_ref, tok_ref, gate_ref, hidden_ref, w_ref, out_ref):
    weighted = (own_gate(where_ref, gate_ref) * hidden_ref[...].astype(F32)).astype(BF)
    tok = own_slots(where_ref, tok_ref, count_ref).astype(F32)
    tok = jnp.broadcast_to(tok, (EXTRA, SLOTS)).astype(BF)
    w = w_ref[...].astype(F32)
    for l in range(L):
        for n in range(C * X):
            at = l * C * X + n
            out_ref[at, 0:SLOTS, :] = weighted
            out_ref[at, SLOTS:PACK, :] = tok
            part = slice_of(w, n, l).astype(BF)
            for t in range(TILES):
                low = PACK + t * SHARE
                out_ref[at, low : low + SHARE, :] = part[:, t * LANES : (t + 1) * LANES]


def weight_kernel(mine_ref, pack_ref, part_ref, routed_ref):
    routed_ref[:, COLS:] = jnp.zeros((QUARTERS * SLOTS, WIDE - COLS), BF)
    ids = lax.broadcasted_iota(I32, (GROUP, SLOTS), 0)
    first = (((0,), (0,)), ((), ()))
    for g in range(QUARTERS):
        tok = pack_ref[g * X, SLOTS:PACK, :].astype(F32)[0:1, :].astype(I32)
        picks = jnp.where(ids == tok, 1.0, 0.0).astype(BF)
        rows = mine_ref[:, g].reshape(GROUP, COLS)
        routed = lax.dot_general(picks, rows, first, preferred_element_type=F32)
        routed_ref[g * SLOTS : (g + 1) * SLOTS, :COLS] = routed.astype(BF)
    routed = routed_ref[:, :COLS]
    for x in range(X):
        weighted = jnp.concatenate([pack_ref[g * X + x, :SLOTS, :] for g in range(QUARTERS)], axis=0)
        part = lax.dot_general(weighted, routed, first, preferred_element_type=F32).astype(BF)
        for h in range(H):
            part_ref[h, x] = part[h * CHUNK : (h + 1) * CHUNK]


def project_kernel(routed_ref, pack_ref, out_ref):
    routed = routed_ref[...]
    for x in range(X):
        w = [
            jnp.concatenate(
                [pack_ref[q * X + x, PACK + t * SHARE : PACK + (t + 1) * SHARE, :] for q in range(QUARTERS)],
                axis=0,
            )
            for t in range(TILES)
        ]
        w = jnp.concatenate(w, axis=1)
        proj = lax.dot_general(routed, w, (((1,), (1,)), ((), ())), preferred_element_type=F32)
        for g in range(QUARTERS):
            out_ref[g * X + x] = proj[g * SLOTS : (g + 1) * SLOTS].astype(BF)


def back_kernel(sums_ref, proj_ref, out_ref):
    for x in range(X):
        total = sums_ref[0, x].astype(F32)
        for h in range(1, H):
            total = total + sums_ref[h, x].astype(F32)
        total = jnp.concatenate([total, jnp.zeros((CHUNK, WIDE - COLS), F32)], axis=1)
        for g in range(QUARTERS):
            c = g % C
            rows = total[c * PER : (c + 1) * PER]
            rows = [rows[:, t * LANES : (t + 1) * LANES] for t in range(TILES)]
            out_ref[g * X + x, 0:BACK, :] = jnp.concatenate(rows, axis=0).astype(BF)
            out_ref[g * X + x, BACK:, :] = proj_ref[g * X + x]


def finish_kernel(
    where_ref, count_ref, tok_ref, gate_ref, hidden_ref, got_ref, grad_ref, spread_ref, block_ref
):
    project = got_ref[0, BACK:, :].astype(F32)
    for n in range(1, PARTS):
        project = project + got_ref[n, BACK:, :].astype(F32)
    grad_ref[...] = (own_gate(where_ref, gate_ref) * project).astype(BF)
    partial = jnp.sum(hidden_ref[...].astype(F32) * project, axis=1, keepdims=True)
    tok = column(own_slots(where_ref, tok_ref, count_ref))
    device = jnp.where(lanes((SLOTS, E * M * N * X)) == tok // ROWS, 1.0, 0.0)
    row = jnp.where(lanes((SLOTS, ROWS)) == tok % ROWS, partial, 0.0)
    spread_ref[...] = lax.dot_general(
        device, row, (((0,), (0,)), ((), ())), precision=lax.Precision.HIGHEST, preferred_element_type=F32
    )
    low = lanes((PER, LANES)) < COLS % LANES
    for n in range(C * X):
        a, b = (got_ref[l * C * X + n, 0:BACK, :].astype(F32) for l in range(L))
        a, b = ([p[t * PER : (t + 1) * PER] for t in range(TILES)] for p in (a, b))
        b = [pltpu.roll(p, COLS % LANES, 1) for p in b]
        tiles = a[:-1] + [jnp.where(low, p, r) for p, r in zip([a[-1]] + b[:-1], b)]
        block_ref[:, n * PAIR : (n + 1) * PAIR] = jnp.concatenate(tiles, axis=1).astype(BF)


VM, SM = pl.BlockSpec(memory_space=pltpu.VMEM), pl.BlockSpec(memory_space=pltpu.SMEM)


def call(kernel, outs, *args, scalars=0, flops=0):
    outs = [jax.ShapeDtypeStruct(s, d) for s, d in outs]
    nbytes = sum(a.size * a.dtype.itemsize for a in list(args) + outs)
    return pl.pallas_call(
        kernel,
        out_shape=outs,
        in_specs=[SM] * scalars + [VM] * (len(args) - scalars),
        out_specs=[VM] * len(outs),
        cost_estimate=pl.CostEstimate(flops=flops, bytes_accessed=nbytes, transcendentals=0),
        compiler_params=pltpu.CompilerParams(vmem_limit_bytes=32 * 1024 * 1024),
    )(*args)


def on_device(grad_values, grad_scales, hidden_act, down_weight, slot_token, slot_count, slot_gate):
    low, core, owner = (lax.axis_index(a) for a in "lce")
    hidden, tok, gate = hidden_act[0], slot_token[0], slot_gate[0]
    where = owner[None].astype(I32)

    (send,) = call(
        tokens_kernel, [((N * PARTS, ROWS, COLS), BF)], grad_values, grad_scales.reshape(1, ROWS)
    )
    mine = lax.all_to_all(send, ("l", "c", "n", "x"), 0, 0)

    w_rows = lax.dynamic_slice_in_dim(down_weight, (low * C + core) * SHARE, SHARE, 0)
    (pack,) = call(
        pack_kernel,
        [((PARTS, PACK + TILES * SHARE, LANES), BF)],
        where, slot_count, tok, gate, hidden, w_rows,
        scalars=2,
    )
    pack, mine = lax.optimization_barrier((pack, mine))
    pack = lax.all_to_all(pack, SPLIT, 0, 0)
    mine = lax.all_gather(mine.reshape(QUARTERS, N * X * ROWS, COLS), ("e", "m"), axis=0)

    part, routed = call(
        weight_kernel,
        [((H, X, CHUNK, COLS), BF), ((QUARTERS * SLOTS, WIDE), BF)],
        mine, pack,
        flops=2 * QUARTERS * SLOTS * COLS * (GROUP + X * UNITS),
    )
    sums = lax.all_to_all(part, "h", 0, 0)
    (proj,) = call(
        project_kernel,
        [((PARTS, SLOTS, UNITS), BF)],
        routed, pack,
        flops=2 * QUARTERS * SLOTS * WIDE * X * UNITS,
    )

    (send,) = call(back_kernel, [((PARTS, BACK + SLOTS, LANES), BF)], sums, proj)
    got = lax.all_to_all(send, SPLIT, 0, 0)
    hidden_grad, spread, block = call(
        finish_kernel,
        [((SLOTS, UNITS), BF), ((E * M * N * X, ROWS), F32), ((PER, WIDTH), BF)],
        where, slot_count, tok, gate, hidden, got,
        scalars=2,
    )
    spread = lax.all_to_all(spread, EXPERT, 0, 0)
    gate_grad = spread.reshape(E, M * N * X, ROWS).sum(axis=1).T

    block = lax.all_gather(block, "h", axis=0)
    cut = H // 2
    halves = [lax.all_gather(block[i : i + cut], "c", axis=1, tiled=True) for i in (0, cut)]
    weight_grad = jnp.concatenate([a.reshape(-1, WIDTH) for a in halves], axis=0)
    return hidden_grad[None], weight_grad, gate_grad


def solution(mesh):
    fine = jax.sharding.Mesh(mesh.devices.reshape(SIZES), DP + EXPERT)
    return jax.shard_map(
        on_device,
        mesh=fine,
        in_specs=(
            P(DP + EXPERT, None),
            P(DP + EXPERT),
            P(DP, None, EXPERT),
            P(EXPERT, None),
            P(DP, None, None),
            P(DP, None),
            P(DP, None, None),
        ),
        out_specs=(P(DP, None, EXPERT), P(EXPERT, None), P(DP + EXPERT, None)),
        check_vma=False,
    )
```

```python
import jax
import jax.numpy as jnp
from jax import lax
from jax.experimental import pallas as pl
from jax.experimental.pallas import tpu as pltpu
from jax.sharding import PartitionSpec as P

BF, F32, I32 = jnp.bfloat16, jnp.float32, jnp.int32
DP, EXPERT = ("h", "l", "c"), ("e", "m", "n", "x")
H, L, C, E, M, N, X = SIZES = (4, 2, 2, 2, 2, 2, 4)
SPLIT = ("l", "c", "x")
QUARTERS, PARTS = L * C, L * C * X
LANES, TILES = 128, 4
WIDTH, SLOTS, UNITS, ROWS = 7168, 128, 128, 8
GROUP = E * M * N * X * ROWS
COLS, WIDE = WIDTH // PARTS, TILES * LANES
PAIR = 2 * COLS
SHARE = UNITS // QUARTERS
CHUNK = UNITS // H
PER = CHUNK // C
EXTRA = 16
PACK = SLOTS + EXTRA
BACK = TILES * PER
OWNED = E * M * N * ROWS


def lanes(shape):
    return lax.broadcasted_iota(I32, shape, len(shape) - 1)


def column(row):
    n = row.shape[1]
    across, down = lanes((n, n)), lax.broadcasted_iota(I32, (n, n), 0)
    return jnp.sum(jnp.where(across == down, row, jnp.zeros_like(row)), axis=1, keepdims=True)


def slice_of(a, n, l):
    start = n * PAIR
    if l == 0:
        a = a[:, start : start + WIDE]
    else:
        a = pltpu.roll(a[:, start + PAIR - WIDE : start + PAIR], COLS, 1)
    return jnp.where(lanes(a.shape) < COLS, a, 0.0)


def tokens_kernel(values_ref, scales_ref, out_ref):
    scaled = values_ref[...].astype(F32) * column(scales_ref[...].astype(F32))
    for l in range(L):
        for n in range(C * X):
            part = slice_of(scaled, n, l)[:, :COLS].astype(BF)
            for i in range(N):
                out_ref[((l * C + n // X) * N + i) * X + n % X] = part


def own_slots(where_ref, tok_ref, count_ref):
    owner = where_ref[0]
    tok = jnp.where(owner == 0, tok_ref[0:1, :], tok_ref[1:2, :])
    return jnp.where(lanes((1, SLOTS)) < count_ref[0, owner], tok, GROUP)


def own_gate(where_ref, gate_ref):
    return column(jnp.where(where_ref[0] == 0, gate_ref[0:1, :], gate_ref[1:2, :]))


def split3(a):
    high = a.astype(BF)
    rest = a - high.astype(F32)
    mid = rest.astype(BF)
    return high.astype(F32), mid.astype(F32), rest - mid.astype(F32)


def stack_rows(rows):
    shape = (EXTRA, rows[0].shape[1])
    at, out = lax.broadcasted_iota(I32, shape, 0), jnp.zeros(shape, F32)
    for i, row in enumerate(rows):
        out = jnp.where(at == i, row, out)
    return out.astype(BF)


def pack_kernel(where_ref, count_ref, tok_ref, gate_ref, hidden_ref, w_ref, out_ref):
    gate = jnp.where(where_ref[0] == 0, gate_ref[0:1, :], gate_ref[1:2, :])
    tok = own_slots(where_ref, tok_ref, count_ref).astype(F32)
    extra = stack_rows((tok,) + split3(gate))
    w = w_ref[...].astype(F32)
    for l in range(L):
        for n in range(C * X):
            at = l * C * X + n
            out_ref[at, 0:SLOTS, :] = hidden_ref[...]
            out_ref[at, SLOTS:PACK, :] = extra
            part = slice_of(w, n, l).astype(BF)
            for t in range(TILES):
                low = PACK + t * SHARE
                out_ref[at, low : low + SHARE, :] = part[:, t * LANES : (t + 1) * LANES]


def weight_kernel(mine_ref, pack_ref, part_ref, routed_ref):
    routed_ref[:, COLS:] = jnp.zeros((QUARTERS * SLOTS, WIDE - COLS), BF)
    ids = lax.broadcasted_iota(I32, (GROUP, SLOTS), 0)
    first = (((0,), (0,)), ((), ()))
    gates = []
    for g in range(QUARTERS):
        extra = pack_ref[g * X, SLOTS:PACK, :].astype(F32)
        gates.append(column(extra[1:2] + extra[2:3] + extra[3:4]))
        picks = jnp.where(ids == extra[0:1].astype(I32), 1.0, 0.0).astype(BF)
        rows = mine_ref[:, g].reshape(GROUP, COLS)
        rows = lax.dot_general(picks, rows, first, preferred_element_type=F32)
        routed_ref[g * SLOTS : (g + 1) * SLOTS, :COLS] = rows.astype(BF)
    rows = routed_ref[:, :COLS]
    for x in range(X):
        weighted = [
            (gates[g] * pack_ref[g * X + x, :SLOTS, :].astype(F32)).astype(BF) for g in range(QUARTERS)
        ]
        weighted = jnp.concatenate(weighted, axis=0)
        part = lax.dot_general(weighted, rows, first, preferred_element_type=F32).astype(BF)
        for h in range(H):
            part_ref[h, x] = part[h * CHUNK : (h + 1) * CHUNK]


def back_kernel(sums_ref, routed_ref, pack_ref, out_ref):
    for x in range(X):
        total = sums_ref[0, x].astype(F32)
        for h in range(1, H):
            total = total + sums_ref[h, x].astype(F32)
        total = jnp.concatenate([total, jnp.zeros((CHUNK, WIDE - COLS), F32)], axis=1).astype(BF)
        for g in range(QUARTERS):
            rows = total[g % C * PER : (g % C + 1) * PER]
            for t in range(TILES):
                out_ref[g * X + x, t * PER : (t + 1) * PER, :] = rows[:, t * LANES : (t + 1) * LANES]
    routed = routed_ref[...]
    gates = [jnp.zeros((SLOTS, 1), F32)] * QUARTERS
    for x in range(X):
        w = [
            jnp.concatenate(
                [pack_ref[q * X + x, PACK + t * SHARE : PACK + (t + 1) * SHARE, :] for q in range(QUARTERS)],
                axis=0,
            )
            for t in range(TILES)
        ]
        w = jnp.concatenate(w, axis=1)
        proj = lax.dot_general(routed, w, (((1,), (1,)), ((), ())), preferred_element_type=F32)
        for g in range(QUARTERS):
            rows = proj[g * SLOTS : (g + 1) * SLOTS]
            out_ref[g * X + x, BACK : BACK + SLOTS, :] = rows.astype(BF)
            hidden = pack_ref[g * X + x, :SLOTS, :].astype(F32)
            gates[g] = gates[g] + jnp.sum(hidden * rows, axis=1, keepdims=True)
    at = lanes((SLOTS, LANES))
    for g in range(QUARTERS):
        tok = column(pack_ref[g * X, SLOTS:PACK, :].astype(F32)[0:1]).astype(I32)
        device, spot = tok // ROWS, tok % ROWS
        spot = jnp.where(tok < GROUP, device // X * ROWS + spot, LANES)
        for x in range(X):
            here = (at == spot) & (device % X == x)
            row = jnp.sum(jnp.where(here, gates[g], 0.0), axis=0, keepdims=True)
            high, mid, low = split3(row)
            out_ref[g * X + x, BACK + SLOTS :, :] = stack_rows((high + pltpu.roll(mid, OWNED, 1), low))


def finish_kernel(where_ref, gate_ref, got_ref, grad_ref, spread_ref, block_ref):
    project = got_ref[0, BACK : BACK + SLOTS, :].astype(F32)
    gates = got_ref[0, BACK + SLOTS :, :].astype(F32)
    for n in range(1, PARTS):
        project = project + got_ref[n, BACK : BACK + SLOTS, :].astype(F32)
        gates = gates + got_ref[n, BACK + SLOTS :, :].astype(F32)
    grad_ref[...] = (own_gate(where_ref, gate_ref) * project).astype(BF)
    row = gates[0:1] + (pltpu.roll(gates[0:1], OWNED, 1) + gates[1:2])
    shape = (E * M * N, LANES)
    row = jnp.where(lanes(shape) // ROWS == lax.broadcasted_iota(I32, shape, 0), row, 0.0)
    shape = (LANES, ROWS)
    fold = jnp.where(lax.broadcasted_iota(I32, shape, 0) % ROWS == lanes(shape), 1.0, 0.0)
    spread_ref[...] = jnp.dot(
        row, fold, precision=lax.Precision.HIGHEST, preferred_element_type=F32
    )
    low = lanes((PER, LANES)) < COLS % LANES
    for n in range(C * X):
        a, b = (got_ref[l * C * X + n, 0:BACK, :].astype(F32) for l in range(L))
        a, b = ([p[t * PER : (t + 1) * PER] for t in range(TILES)] for p in (a, b))
        b = [pltpu.roll(p, COLS % LANES, 1) for p in b]
        tiles = a[:-1] + [jnp.where(low, p, r) for p, r in zip([a[-1]] + b[:-1], b)]
        block_ref[:, n * PAIR : (n + 1) * PAIR] = jnp.concatenate(tiles, axis=1).astype(BF)


VM, SM = pl.BlockSpec(memory_space=pltpu.VMEM), pl.BlockSpec(memory_space=pltpu.SMEM)


def call(kernel, places, outs, *args, flops=0):
    outs = [jax.ShapeDtypeStruct(s, d) for s, d in outs]
    nbytes = sum(a.size * a.dtype.itemsize for a in list(args) + outs)
    return pl.pallas_call(
        kernel,
        out_shape=outs,
        in_specs=places,
        out_specs=[VM] * len(outs),
        cost_estimate=pl.CostEstimate(flops=flops, bytes_accessed=nbytes, transcendentals=0),
        compiler_params=pltpu.CompilerParams(vmem_limit_bytes=32 * 1024 * 1024),
    )(*args)


def on_device(grad_values, grad_scales, hidden_act, down_weight, slot_token, slot_count, slot_gate):
    low, core, owner = (lax.axis_index(a) for a in "lce")
    hidden, tok, gate = hidden_act[0], slot_token[0], slot_gate[0]
    where = owner[None].astype(I32)

    (send,) = call(
        tokens_kernel,
        [VM, VM],
        [((N * PARTS, ROWS, COLS), BF)],
        grad_values, grad_scales.reshape(1, ROWS),
    )
    mine = lax.all_to_all(send, ("l", "c", "n", "x"), 0, 0)

    w_rows = lax.dynamic_slice_in_dim(down_weight, (low * C + core) * SHARE, SHARE, 0)
    (pack,) = call(
        pack_kernel,
        [SM, SM, VM, VM, VM, VM],
        [((PARTS, PACK + TILES * SHARE, LANES), BF)],
        where, slot_count, tok, gate, hidden, w_rows,
    )
    pack, mine = lax.optimization_barrier((pack, mine))
    pack = lax.all_to_all(pack, SPLIT, 0, 0)
    mine = lax.all_gather(mine.reshape(QUARTERS, N * X * ROWS, COLS), ("e", "m"), axis=0)

    part, routed = call(
        weight_kernel,
        [VM, VM],
        [((H, X, CHUNK, COLS), BF), ((QUARTERS * SLOTS, WIDE), BF)],
        mine, pack,
        flops=2 * QUARTERS * SLOTS * COLS * (GROUP + X * UNITS),
    )
    sums = lax.all_to_all(part, "h", 0, 0)

    (send,) = call(
        back_kernel,
        [VM, VM, VM],
        [((PARTS, BACK + PACK, LANES), BF)],
        sums, routed, pack,
        flops=2 * QUARTERS * SLOTS * WIDE * X * UNITS,
    )
    got = lax.all_to_all(send, SPLIT, 0, 0)
    hidden_grad, spread, block = call(
        finish_kernel,
        [SM, VM, VM],
        [((SLOTS, UNITS), BF), ((E * M * N, ROWS), F32), ((PER, WIDTH), BF)],
        where, gate, got,
    )
    spread = lax.all_to_all(spread, ("e", "m", "n"), 0, 0, tiled=True)
    gate_grad = spread.reshape(E, M * N, ROWS).sum(axis=1).T

    block = lax.all_gather(block, "h", axis=0)
    cut = H // 2
    halves = [lax.all_gather(block[i : i + cut], "c", axis=1, tiled=True) for i in (0, cut)]
    weight_grad = jnp.concatenate([a.reshape(-1, WIDTH) for a in halves], axis=0)
    return hidden_grad[None], weight_grad, gate_grad


def solution(mesh):
    fine = jax.sharding.Mesh(mesh.devices.reshape(SIZES), DP + EXPERT)
    return jax.shard_map(
        on_device,
        mesh=fine,
        in_specs=(
            P(DP + EXPERT, None),
            P(DP + EXPERT),
            P(DP, None, EXPERT),
            P(EXPERT, None),
            P(DP, None, None),
            P(DP, None),
            P(DP, None, None),
        ),
        out_specs=(P(DP, None, EXPERT), P(EXPERT, None), P(DP + EXPERT, None)),
        check_vma=False,
    )
```

```python
import jax
import jax.numpy as jnp
from jax import lax
from jax.experimental import pallas as pl
from jax.experimental.pallas import tpu as pltpu
from jax.sharding import PartitionSpec as P

BF, F32, I32 = jnp.bfloat16, jnp.float32, jnp.int32
DP, EXPERT = ("h", "l", "c"), ("e", "m", "n", "x")
H, L, C, E, M, N, X = SIZES = (4, 2, 2, 2, 2, 2, 4)
SPLIT = ("l", "c", "x")
QUARTERS, PARTS = L * C, L * C * X
LANES, TILES = 128, 4
WIDTH, SLOTS, UNITS, ROWS = 7168, 128, 128, 8
GROUP = E * M * N * X * ROWS
COLS, WIDE = WIDTH // PARTS, TILES * LANES
PAIR = 2 * COLS
SHARE = UNITS // QUARTERS
CHUNK = UNITS // H
EXTRA = 16
PACK = SLOTS + EXTRA
WHOLE, HALF = (TILES - 1) * CHUNK, CHUNK // 2
BACK = WHOLE + HALF
TAIL = COLS % LANES
OWNED = E * M * N * ROWS


def lanes(shape):
    return lax.broadcasted_iota(I32, shape, len(shape) - 1)


def column(row):
    n = row.shape[1]
    across, down = lanes((n, n)), lax.broadcasted_iota(I32, (n, n), 0)
    return jnp.sum(jnp.where(across == down, row, jnp.zeros_like(row)), axis=1, keepdims=True)


def slice_of(a, n, l):
    start = n * PAIR
    if l == 0:
        a = a[:, start : start + WIDE]
    else:
        a = pltpu.roll(a[:, start + PAIR - WIDE : start + PAIR], COLS, 1)
    return jnp.where(lanes(a.shape) < COLS, a, 0.0)


def tokens_kernel(values_ref, scales_ref, out_ref):
    scaled = values_ref[...].astype(F32) * column(scales_ref[...].astype(F32))
    for l in range(L):
        for n in range(C * X):
            part = slice_of(scaled, n, l)[:, :COLS].astype(BF)
            for i in range(N):
                out_ref[((l * C + n // X) * N + i) * X + n % X] = part


def own_slots(where_ref, tok_ref, count_ref):
    owner = where_ref[0]
    tok = jnp.where(owner == 0, tok_ref[0:1, :], tok_ref[1:2, :])
    return jnp.where(lanes((1, SLOTS)) < count_ref[0, owner], tok, GROUP)


def own_gate(where_ref, gate_ref):
    return column(jnp.where(where_ref[0] == 0, gate_ref[0:1, :], gate_ref[1:2, :]))


def split3(a):
    high = a.astype(BF)
    rest = a - high.astype(F32)
    mid = rest.astype(BF)
    return high.astype(F32), mid.astype(F32), rest - mid.astype(F32)


def stack_rows(rows):
    shape = (EXTRA, rows[0].shape[1])
    at, out = lax.broadcasted_iota(I32, shape, 0), jnp.zeros(shape, F32)
    for i, row in enumerate(rows):
        out = jnp.where(at == i, row, out)
    return out.astype(BF)


def pack_kernel(where_ref, count_ref, tok_ref, gate_ref, hidden_ref, w_ref, out_ref):
    gate = jnp.where(where_ref[0] == 0, gate_ref[0:1, :], gate_ref[1:2, :])
    tok = own_slots(where_ref, tok_ref, count_ref).astype(F32)
    extra = stack_rows((tok,) + split3(gate))
    w = w_ref[...].astype(F32)
    for l in range(L):
        for n in range(C * X):
            at = l * C * X + n
            out_ref[at, 0:SLOTS, :] = hidden_ref[...]
            out_ref[at, SLOTS:PACK, :] = extra
            part = slice_of(w, n, l).astype(BF)
            for t in range(TILES):
                low = PACK + t * SHARE
                out_ref[at, low : low + SHARE, :] = part[:, t * LANES : (t + 1) * LANES]


def weight_kernel(core_ref, mine_ref, pack_ref, part_ref, keep_ref, send_ref, routed_ref):
    routed_ref[:, COLS:] = jnp.zeros((QUARTERS * SLOTS, WIDE - COLS), BF)
    ids = lax.broadcasted_iota(I32, (GROUP, SLOTS), 0)
    first = (((0,), (0,)), ((), ()))
    gates = []
    for g in range(QUARTERS):
        extra = pack_ref[g * X, SLOTS:PACK, :].astype(F32)
        gates.append(column(extra[1:2] + extra[2:3] + extra[3:4]))
        picks = jnp.where(ids == extra[0:1].astype(I32), 1.0, 0.0).astype(BF)
        rows = mine_ref[:, g].reshape(GROUP, COLS)
        rows = lax.dot_general(picks, rows, first, preferred_element_type=F32)
        routed_ref[g * SLOTS : (g + 1) * SLOTS, :COLS] = rows.astype(BF)
    routed = routed_ref[...]

    for x in range(X):
        weighted = [
            (gates[g] * pack_ref[g * X + x, :SLOTS, :].astype(F32)).astype(BF) for g in range(QUARTERS)
        ]
        weighted = jnp.concatenate(weighted, axis=0)
        part = lax.dot_general(weighted, routed, first, preferred_element_type=F32)
        for h in range(H):
            rows = part[h * CHUNK : (h + 1) * CHUNK]
            for t in range(TILES - 1):
                part_ref[h, x, t * CHUNK : (t + 1) * CHUNK, :] = rows[:, t * LANES : (t + 1) * LANES].astype(BF)
            rows = rows[:, WIDE - LANES :]
            part_ref[h, x, WHOLE:, :] = (rows[:HALF] + pltpu.roll(rows[HALF:], TAIL, 1)).astype(BF)

    core = core_ref[0]
    groups = [l * C + c for c in (core, 1 - core) for l in range(L)]
    outs = [(ref, l) for ref in (keep_ref, send_ref) for l in range(L)]
    routed = jnp.concatenate(
        [routed_ref[pl.ds(pl.multiple_of(g * SLOTS, SLOTS), SLOTS), :] for g in groups], axis=0
    )
    sums = [jnp.zeros((SLOTS, 1), F32)] * QUARTERS
    for x in range(X):
        w = [
            jnp.concatenate(
                [pack_ref[q * X + x, PACK + t * SHARE : PACK + (t + 1) * SHARE, :] for q in range(QUARTERS)],
                axis=0,
            )
            for t in range(TILES)
        ]
        w = jnp.concatenate(w, axis=1)
        proj = lax.dot_general(routed, w, (((1,), (1,)), ((), ())), preferred_element_type=F32)
        for i, (ref, l) in enumerate(outs):
            rows = proj[i * SLOTS : (i + 1) * SLOTS]
            ref[l * X + x, 0:SLOTS, :] = rows.astype(BF)
            hidden = pack_ref[groups[i] * X + x, :SLOTS, :].astype(F32)
            sums[i] = sums[i] + jnp.sum(hidden * rows, axis=1, keepdims=True)
    at = lanes((SLOTS, LANES))
    for i, (ref, l) in enumerate(outs):
        tok = column(pack_ref[groups[i] * X, SLOTS:PACK, :].astype(F32)[0:1]).astype(I32)
        device, spot = tok // ROWS, tok % ROWS
        spot = jnp.where(tok < GROUP, device // X * ROWS + spot, LANES)
        for x in range(X):
            here = (at == spot) & (device % X == x)
            row = jnp.sum(jnp.where(here, sums[i], 0.0), axis=0, keepdims=True)
            ref[l * X + x, SLOTS:PACK, :] = terms(row)


def terms(row):
    high, mid, low = split3(row)
    return stack_rows((high + pltpu.roll(mid, OWNED, 1), low))


def row_of(tile):
    row = tile[0:1] + (pltpu.roll(tile[0:1], OWNED, 1) + tile[1:2])
    return jnp.where(lanes(row.shape) < OWNED, row, 0.0)


def back_kernel(sums_ref, keep_ref, other_ref, out_ref):
    for x in range(X):
        total = sums_ref[0, x].astype(F32)
        for h in range(1, H):
            total = total + sums_ref[h, x].astype(F32)
        for l in range(L):
            out_ref[l * X + x, 0:BACK, :] = total.astype(BF)
    for n in range(L * X):
        both = keep_ref[n].astype(F32) + other_ref[n].astype(F32)
        out_ref[n, BACK : BACK + SLOTS, :] = both[:SLOTS].astype(BF)
        out_ref[n, BACK + SLOTS :, :] = terms(row_of(both[SLOTS:]))


def finish_kernel(where_ref, gate_ref, got_ref, grad_ref, spread_ref, block_ref):
    both = got_ref[0, BACK:, :].astype(F32)
    for n in range(1, L * X):
        both = both + got_ref[n, BACK:, :].astype(F32)
    grad_ref[...] = (own_gate(where_ref, gate_ref) * both[:SLOTS]).astype(BF)
    shape = (E * M * N, LANES)
    row = jnp.where(lanes(shape) // ROWS == lax.broadcasted_iota(I32, shape, 0), row_of(both[SLOTS:]), 0.0)
    shape = (LANES, ROWS)
    fold = jnp.where(lax.broadcasted_iota(I32, shape, 0) % ROWS == lanes(shape), 1.0, 0.0)
    spread_ref[...] = jnp.dot(
        row, fold, precision=lax.Precision.HIGHEST, preferred_element_type=F32
    )
    low = lanes((CHUNK, LANES)) < TAIL
    for x in range(X):
        a, b = (got_ref[l * X + x, 0:BACK, :].astype(F32) for l in range(L))
        a, b = (
            [p[t * CHUNK : (t + 1) * CHUNK] for t in range(TILES - 1)]
            + [jnp.concatenate([p[WHOLE:], pltpu.roll(p[WHOLE:], TAIL, 1)], axis=0)]
            for p in (a, b)
        )
        b = [pltpu.roll(p, TAIL, 1) for p in b]
        tiles = a[:-1] + [jnp.where(low, p, r) for p, r in zip([a[-1]] + b[:-1], b)]
        block_ref[:, x * PAIR : (x + 1) * PAIR] = jnp.concatenate(tiles, axis=1).astype(BF)


VM, SM = pl.BlockSpec(memory_space=pltpu.VMEM), pl.BlockSpec(memory_space=pltpu.SMEM)


def call(kernel, places, outs, *args, scratch=(), flops=0):
    outs = [jax.ShapeDtypeStruct(s, d) for s, d in outs]
    nbytes = sum(a.size * a.dtype.itemsize for a in list(args) + outs)
    return pl.pallas_call(
        kernel,
        out_shape=outs,
        in_specs=places,
        out_specs=[VM] * len(outs),
        scratch_shapes=scratch,
        cost_estimate=pl.CostEstimate(flops=flops, bytes_accessed=nbytes, transcendentals=0),
        compiler_params=pltpu.CompilerParams(vmem_limit_bytes=32 * 1024 * 1024),
    )(*args)


def on_device(grad_values, grad_scales, hidden_act, down_weight, slot_token, slot_count, slot_gate):
    low, core, owner = (lax.axis_index(a) for a in "lce")
    hidden, tok, gate = hidden_act[0], slot_token[0], slot_gate[0]
    where = owner[None].astype(I32)

    (send,) = call(
        tokens_kernel,
        [VM, VM],
        [((N * PARTS, ROWS, COLS), BF)],
        grad_values, grad_scales.reshape(1, ROWS),
    )
    mine = lax.all_to_all(send, ("l", "c", "n", "x"), 0, 0)

    w_rows = lax.dynamic_slice_in_dim(down_weight, (low * C + core) * SHARE, SHARE, 0)
    (pack,) = call(
        pack_kernel,
        [SM, SM, VM, VM, VM, VM],
        [((PARTS, PACK + TILES * SHARE, LANES), BF)],
        where, slot_count, tok, gate, hidden, w_rows,
    )
    pack, mine = lax.optimization_barrier((pack, mine))
    pack = lax.all_to_all(pack, SPLIT, 0, 0)
    mine = lax.all_gather(mine.reshape(QUARTERS, N * X * ROWS, COLS), ("e", "m"), axis=0)

    part, keep, other = call(
        weight_kernel,
        [SM, VM, VM],
        [((H, X, BACK, LANES), BF), ((L * X, PACK, LANES), BF), ((L * X, PACK, LANES), BF)],
        core[None].astype(I32), mine, pack,
        scratch=[pltpu.VMEM((QUARTERS * SLOTS, WIDE), BF)],
        flops=2 * QUARTERS * SLOTS * (COLS * GROUP + 2 * WIDE * X * UNITS),
    )
    other = lax.ppermute(other, "c", [(i, C - 1 - i) for i in range(C)])
    sums = lax.all_to_all(part, "h", 0, 0)

    (send,) = call(
        back_kernel,
        [VM, VM, VM],
        [((L * X, BACK + PACK, LANES), BF)],
        sums, keep, other,
    )
    got = lax.all_to_all(send, ("l", "x"), 0, 0)
    hidden_grad, spread, block = call(
        finish_kernel,
        [SM, VM, VM],
        [((SLOTS, UNITS), BF), ((E * M * N, ROWS), F32), ((CHUNK, X * PAIR), BF)],
        where, gate, got,
    )
    spread = lax.all_to_all(spread, ("e", "m", "n"), 0, 0, tiled=True)
    gate_grad = spread.reshape(E, M * N, ROWS).sum(axis=1).T

    block = lax.all_gather(block, "h", axis=0, tiled=True)
    cut = UNITS // 2
    halves = [lax.all_gather(block[i : i + cut], "c", axis=1, tiled=True) for i in (0, cut)]
    return hidden_grad[None], jnp.concatenate(halves, axis=0), gate_grad


def solution(mesh):
    fine = jax.sharding.Mesh(mesh.devices.reshape(SIZES), DP + EXPERT)
    return jax.shard_map(
        on_device,
        mesh=fine,
        in_specs=(
            P(DP + EXPERT, None),
            P(DP + EXPERT),
            P(DP, None, EXPERT),
            P(EXPERT, None),
            P(DP, None, None),
            P(DP, None),
            P(DP, None, None),
        ),
        out_specs=(P(DP, None, EXPERT), P(EXPERT, None), P(DP + EXPERT, None)),
        check_vma=False,
    )
```

```python
import jax
import jax.numpy as jnp
from jax import lax
from jax.experimental import pallas as pl
from jax.experimental.pallas import tpu as pltpu
from jax.sharding import PartitionSpec as P

BF, F32, I32 = jnp.bfloat16, jnp.float32, jnp.int32
DP, EXPERT = ("h", "l", "c"), ("e", "m", "n", "x")
H, L, C, E, M, N, X = SIZES = (4, 2, 2, 2, 2, 2, 4)
SPLIT = ("l", "c", "x")
QUARTERS, PARTS = L * C, L * C * X
LANES, TILES = 128, 4
WIDTH, SLOTS, UNITS, ROWS = 7168, 128, 128, 8
GROUP = E * M * N * X * ROWS
COLS, WIDE = WIDTH // PARTS, TILES * LANES
PAIR = 2 * COLS
SHARE = UNITS // QUARTERS
CHUNK = UNITS // H
EXTRA = 16
PACK = SLOTS + EXTRA
FULL, TAIL = TILES - 1, COLS % LANES
TOKS = N * X * ROWS
BACK = FULL * CHUNK + CHUNK // 2
W_PART = FULL * SHARE + SHARE // 2
DENSE = FULL * TOKS + TOKS // 2
OWNED = E * M * N * ROWS


def lanes(shape):
    return lax.broadcasted_iota(I32, shape, len(shape) - 1)


def column(row):
    n = row.shape[1]
    across, down = lanes((n, n)), lax.broadcasted_iota(I32, (n, n), 0)
    return jnp.sum(jnp.where(across == down, row, jnp.zeros_like(row)), axis=1, keepdims=True)


def slice_of(a, n, l):
    start = n * PAIR
    if l == 0:
        a = a[:, start : start + WIDE]
    else:
        a = pltpu.roll(a[:, start + PAIR - WIDE : start + PAIR], COLS, 1)
    return jnp.where(lanes(a.shape) < COLS, a, 0.0)


def dense(a):
    half = a.shape[0] // 2
    last = a[:, FULL * LANES :]
    last = last[:half] + pltpu.roll(last[half:], TAIL, 1)
    return jnp.concatenate([a[:, t * LANES : (t + 1) * LANES] for t in range(FULL)] + [last], axis=0)


def last_tile(a):
    return jnp.concatenate([a, pltpu.roll(a, TAIL, 1)], axis=0)


def tokens_kernel(values_all, scales_all, out_ref, values_ref, scales_ref, sem):
    loads = [
        pltpu.make_async_copy(src, dst, sem.at[i])
        for i, (src, dst) in enumerate(((values_all, values_ref), (scales_all, scales_ref)))
    ]
    for load in loads:
        load.start()
    for load in loads:
        load.wait()
    scaled = values_ref[...].astype(F32) * column(scales_ref[...].astype(F32))
    for l in range(L):
        for n in range(C * X):
            part = slice_of(scaled, n, l).astype(BF)
            for i in range(N):
                out_ref[((l * C + n // X) * N + i) * X + n % X] = part


def own_slots(where_ref, tok_ref, count_ref):
    owner = where_ref[0]
    tok = jnp.where(owner == 0, tok_ref[0:1, :], tok_ref[1:2, :])
    return jnp.where(lanes((1, SLOTS)) < count_ref[0, owner], tok, GROUP)


def own_gate(where_ref, gate_ref):
    return column(jnp.where(where_ref[0] == 0, gate_ref[0:1, :], gate_ref[1:2, :]))


def split3(a):
    high = a.astype(BF)
    rest = a - high.astype(F32)
    mid = rest.astype(BF)
    return high.astype(F32), mid.astype(F32), rest - mid.astype(F32)


def stack_rows(rows):
    shape = (EXTRA, rows[0].shape[1])
    at, out = lax.broadcasted_iota(I32, shape, 0), jnp.zeros(shape, F32)
    for i, row in enumerate(rows):
        out = jnp.where(at == i, row, out)
    return out.astype(BF)


def pack_kernel(where_ref, count_ref, tok_ref, gate_ref, hidden_ref, w_ref, out_ref):
    gate = jnp.where(where_ref[0] == 0, gate_ref[0:1, :], gate_ref[1:2, :])
    tok = own_slots(where_ref, tok_ref, count_ref).astype(F32)
    extra = stack_rows((tok,) + split3(gate))
    w = w_ref[...].astype(F32)
    for l in range(L):
        for n in range(C * X):
            at = l * C * X + n
            out_ref[at, 0:SLOTS, :] = hidden_ref[...]
            out_ref[at, SLOTS:PACK, :] = extra
            out_ref[at, PACK:, :] = dense(slice_of(w, n, l)).astype(BF)


def dense_kernel(rows_ref, out_ref):
    for g in range(QUARTERS):
        out_ref[g] = dense(rows_ref[g].astype(F32)).astype(BF)


def weight_kernel(core_ref, mine_ref, pack_ref, part_ref, keep_ref, send_ref, routed_ref):
    ids = lax.broadcasted_iota(I32, (GROUP, SLOTS), 0)
    first = (((0,), (0,)), ((), ()))
    gates = []
    for g in range(QUARTERS):
        extra = pack_ref[g * X, SLOTS:PACK, :].astype(F32)
        gates.append(column(extra[1:2] + extra[2:3] + extra[3:4]))
        picks = jnp.where(ids == extra[0:1].astype(I32), 1.0, 0.0).astype(BF)
        rows = [mine_ref[:, g, t * TOKS : (t + 1) * TOKS, :].reshape(GROUP, LANES) for t in range(FULL)]
        rows += [
            jnp.concatenate(
                [last_tile(mine_ref[i, g, FULL * TOKS :, :].astype(F32)).astype(BF) for i in range(E * M)],
                axis=0,
            )
        ]
        rows = jnp.concatenate(rows, axis=1)
        rows = lax.dot_general(picks, rows, first, preferred_element_type=F32)
        rows = jnp.where(lanes(rows.shape) < COLS, rows, 0.0)
        routed_ref[g * SLOTS : (g + 1) * SLOTS, :] = rows.astype(BF)
    routed = routed_ref[...]

    for x in range(X):
        weighted = [
            (gates[g] * pack_ref[g * X + x, :SLOTS, :].astype(F32)).astype(BF) for g in range(QUARTERS)
        ]
        weighted = jnp.concatenate(weighted, axis=0)
        part = lax.dot_general(weighted, routed, first, preferred_element_type=F32)
        for h in range(H):
            part_ref[h, x] = dense(part[h * CHUNK : (h + 1) * CHUNK]).astype(BF)

    core = core_ref[0]
    groups = [l * C + c for c in (core, 1 - core) for l in range(L)]
    outs = [(ref, l) for ref in (keep_ref, send_ref) for l in range(L)]
    routed = jnp.concatenate(
        [routed_ref[pl.ds(pl.multiple_of(g * SLOTS, SLOTS), SLOTS), :] for g in groups], axis=0
    )
    sums = [jnp.zeros((SLOTS, 1), F32)] * QUARTERS
    for x in range(X):
        w = []
        for q in range(QUARTERS):
            rows = pack_ref[q * X + x, PACK:, :]
            rows = [rows[t * SHARE : (t + 1) * SHARE] for t in range(FULL)] + [
                last_tile(rows[FULL * SHARE :].astype(F32)).astype(BF)
            ]
            w.append(jnp.concatenate(rows, axis=1))
        w = jnp.concatenate(w, axis=0)
        proj = lax.dot_general(routed, w, (((1,), (1,)), ((), ())), preferred_element_type=F32)
        for i, (ref, l) in enumerate(outs):
            rows = proj[i * SLOTS : (i + 1) * SLOTS]
            ref[l * X + x, 0:SLOTS, :] = rows.astype(BF)
            hidden = pack_ref[groups[i] * X + x, :SLOTS, :].astype(F32)
            sums[i] = sums[i] + jnp.sum(hidden * rows, axis=1, keepdims=True)
    at = lanes((SLOTS, LANES))
    for i, (ref, l) in enumerate(outs):
        tok = column(pack_ref[groups[i] * X, SLOTS:PACK, :].astype(F32)[0:1]).astype(I32)
        device, spot = tok // ROWS, tok % ROWS
        spot = jnp.where(tok < GROUP, device // X * ROWS + spot, LANES)
        for x in range(X):
            here = (at == spot) & (device % X == x)
            row = jnp.sum(jnp.where(here, sums[i], 0.0), axis=0, keepdims=True)
            ref[l * X + x, SLOTS:PACK, :] = terms(row)


def terms(row):
    high, mid, low = split3(row)
    return stack_rows((high + pltpu.roll(mid, OWNED, 1), low))


def row_of(tile):
    row = tile[0:1] + (pltpu.roll(tile[0:1], OWNED, 1) + tile[1:2])
    return jnp.where(lanes(row.shape) < OWNED, row, 0.0)


def back_kernel(sums_ref, keep_ref, other_ref, out_ref):
    for x in range(X):
        total = sums_ref[0, x].astype(F32)
        for h in range(1, H):
            total = total + sums_ref[h, x].astype(F32)
        for l in range(L):
            out_ref[l * X + x, 0:BACK, :] = total.astype(BF)
    for n in range(L * X):
        both = keep_ref[n].astype(F32) + other_ref[n].astype(F32)
        out_ref[n, BACK : BACK + SLOTS, :] = both[:SLOTS].astype(BF)
        out_ref[n, BACK + SLOTS :, :] = terms(row_of(both[SLOTS:]))


def finish_kernel(where_ref, gate_ref, got_ref, grad_ref, spread_ref, block_ref):
    both = got_ref[0, BACK:, :].astype(F32)
    for n in range(1, L * X):
        both = both + got_ref[n, BACK:, :].astype(F32)
    grad_ref[...] = (own_gate(where_ref, gate_ref) * both[:SLOTS]).astype(BF)
    shape = (E * M * N, LANES)
    row = jnp.where(lanes(shape) // ROWS == lax.broadcasted_iota(I32, shape, 0), row_of(both[SLOTS:]), 0.0)
    shape = (LANES, ROWS)
    fold = jnp.where(lax.broadcasted_iota(I32, shape, 0) % ROWS == lanes(shape), 1.0, 0.0)
    spread_ref[...] = jnp.dot(
        row, fold, precision=lax.Precision.HIGHEST, preferred_element_type=F32
    )
    low = lanes((CHUNK, LANES)) < TAIL
    for x in range(X):
        a, b = (got_ref[l * X + x, 0:BACK, :].astype(F32) for l in range(L))
        a, b = (
            [p[t * CHUNK : (t + 1) * CHUNK] for t in range(FULL)] + [last_tile(p[FULL * CHUNK :])]
            for p in (a, b)
        )
        b = [pltpu.roll(p, TAIL, 1) for p in b]
        tiles = a[:-1] + [jnp.where(low, p, r) for p, r in zip([a[-1]] + b[:-1], b)]
        block_ref[:, x * PAIR : (x + 1) * PAIR] = jnp.concatenate(tiles, axis=1).astype(BF)


VM, SM, HBM = (pl.BlockSpec(memory_space=m) for m in (pltpu.VMEM, pltpu.SMEM, pl.ANY))


def call(kernel, places, outs, *args, scratch=(), flops=0, vmem=32):
    outs = [jax.ShapeDtypeStruct(s, d) for s, d in outs]
    nbytes = sum(a.size * a.dtype.itemsize for a in list(args) + outs)
    return pl.pallas_call(
        kernel,
        out_shape=outs,
        in_specs=places,
        out_specs=[VM] * len(outs),
        scratch_shapes=scratch,
        cost_estimate=pl.CostEstimate(flops=flops, bytes_accessed=nbytes, transcendentals=0),
        compiler_params=pltpu.CompilerParams(vmem_limit_bytes=vmem * 1024 * 1024),
    )(*args)


def on_device(grad_values, grad_scales, hidden_act, down_weight, slot_token, slot_count, slot_gate):
    low, core, owner = (lax.axis_index(a) for a in "lce")
    hidden, tok, gate = hidden_act[0], slot_token[0], slot_gate[0]
    where = owner[None].astype(I32)

    (send,) = call(
        tokens_kernel,
        [HBM, HBM],
        [((N * PARTS, ROWS, WIDE), BF)],
        grad_values, grad_scales.reshape(1, ROWS),
        scratch=[
            pltpu.VMEM((ROWS, WIDTH), BF), pltpu.VMEM((1, ROWS), BF), pltpu.SemaphoreType.DMA((2,))
        ],
        vmem=60,
    )
    mine = lax.all_to_all(send, ("l", "c", "n", "x"), 0, 0)

    w_rows = lax.dynamic_slice_in_dim(down_weight, (low * C + core) * SHARE, SHARE, 0)
    (pack,) = call(
        pack_kernel,
        [SM, SM, VM, VM, VM, VM],
        [((PARTS, PACK + W_PART, LANES), BF)],
        where, slot_count, tok, gate, hidden, w_rows,
    )
    pack, mine = lax.optimization_barrier((pack, mine))
    pack = lax.all_to_all(pack, SPLIT, 0, 0)
    (mine,) = call(
        dense_kernel, [VM], [((QUARTERS, DENSE, LANES), BF)], mine.reshape(QUARTERS, TOKS, WIDE)
    )
    mine = lax.all_gather(mine, ("e", "m"), axis=0)

    part, keep, other = call(
        weight_kernel,
        [SM, VM, VM],
        [((H, X, BACK, LANES), BF), ((L * X, PACK, LANES), BF), ((L * X, PACK, LANES), BF)],
        core[None].astype(I32), mine, pack,
        scratch=[pltpu.VMEM((QUARTERS * SLOTS, WIDE), BF)],
        flops=2 * QUARTERS * SLOTS * (COLS * GROUP + 2 * WIDE * X * UNITS),
    )
    other = lax.ppermute(other, "c", [(i, C - 1 - i) for i in range(C)])
    sums = lax.all_to_all(part, "h", 0, 0)

    (send,) = call(
        back_kernel,
        [VM, VM, VM],
        [((L * X, BACK + PACK, LANES), BF)],
        sums, keep, other,
    )
    got = lax.all_to_all(send, ("l", "x"), 0, 0)
    hidden_grad, spread, block = call(
        finish_kernel,
        [SM, VM, VM],
        [((SLOTS, UNITS), BF), ((E * M * N, ROWS), F32), ((CHUNK, X * PAIR), BF)],
        where, gate, got,
    )
    spread = lax.all_to_all(spread, ("e", "m", "n"), 0, 0, tiled=True)
    gate_grad = spread.reshape(E, M * N, ROWS).sum(axis=1).T

    block = lax.all_gather(block, "h", axis=0, tiled=True)
    cut = UNITS // 2
    halves = [lax.all_gather(block[i : i + cut], "c", axis=1, tiled=True) for i in (0, cut)]
    return hidden_grad[None], jnp.concatenate(halves, axis=0), gate_grad


def solution(mesh):
    fine = jax.sharding.Mesh(mesh.devices.reshape(SIZES), DP + EXPERT)
    return jax.shard_map(
        on_device,
        mesh=fine,
        in_specs=(
            P(DP + EXPERT, None),
            P(DP + EXPERT),
            P(DP, None, EXPERT),
            P(EXPERT, None),
            P(DP, None, None),
            P(DP, None),
            P(DP, None, None),
        ),
        out_specs=(P(DP, None, EXPERT), P(EXPERT, None), P(DP + EXPERT, None)),
        check_vma=False,
    )
```

```python
import jax
import jax.numpy as jnp
from jax import lax
from jax.experimental import pallas as pl
from jax.experimental.pallas import tpu as pltpu
from jax.sharding import PartitionSpec as P

BF, F32, I32 = jnp.bfloat16, jnp.float32, jnp.int32
DP, EXPERT = ("h", "l", "c"), ("e", "m", "n", "x")
H, L, C, E, M, N, X = SIZES = (4, 2, 2, 2, 2, 2, 4)
SPLIT = ("l", "c", "x")
QUARTERS, PARTS = L * C, L * C * X
LANES, TILES = 128, 4
WIDTH, SLOTS, UNITS, ROWS = 7168, 128, 128, 8
GROUP = E * M * N * X * ROWS
COLS, WIDE = WIDTH // PARTS, TILES * LANES
PAIR = 2 * COLS
SHARE = UNITS // QUARTERS
CHUNK = UNITS // H
EXTRA = 16
PACK = SLOTS + EXTRA
FULL, TAIL = TILES - 1, COLS % LANES
TOKS = N * X * ROWS
BACK = FULL * CHUNK + CHUNK // 2
W_PART = FULL * SHARE + SHARE // 2
DENSE = FULL * TOKS + TOKS // 2
OWNED = E * M * N * ROWS


def lanes(shape):
    return lax.broadcasted_iota(I32, shape, len(shape) - 1)


def column(row):
    n = row.shape[1]
    across, down = lanes((n, n)), lax.broadcasted_iota(I32, (n, n), 0)
    return jnp.sum(jnp.where(across == down, row, jnp.zeros_like(row)), axis=1, keepdims=True)


def slice_of(a, n, l):
    start = n * PAIR
    if l == 0:
        a = a[:, start : start + WIDE]
    else:
        a = pltpu.roll(a[:, start + PAIR - WIDE : start + PAIR], COLS, 1)
    return jnp.where(lanes(a.shape) < COLS, a, 0.0)


def dense(a):
    half = a.shape[0] // 2
    last = a[:, FULL * LANES :]
    last = last[:half] + pltpu.roll(last[half:], TAIL, 1)
    return jnp.concatenate([a[:, t * LANES : (t + 1) * LANES] for t in range(FULL)] + [last], axis=0)


def last_tile(a):
    return jnp.concatenate([a, pltpu.roll(a, TAIL, 1)], axis=0)


def tokens_kernel(values_all, scales_all, out_ref, values_ref, scales_ref, sem):
    loads = [
        pltpu.make_async_copy(src, dst, sem.at[i])
        for i, (src, dst) in enumerate(((values_all, values_ref), (scales_all, scales_ref)))
    ]
    for load in loads:
        load.start()
    for load in loads:
        load.wait()
    scaled = values_ref[...].astype(F32) * column(scales_ref[...].astype(F32))
    for l in range(L):
        for n in range(C * X):
            part = slice_of(scaled, n, l).astype(BF)
            for i in range(N):
                out_ref[((l * C + n // X) * N + i) * X + n % X] = part


def own_slots(where_ref, tok_ref, count_ref):
    owner = where_ref[0]
    tok = jnp.where(owner == 0, tok_ref[0:1, :], tok_ref[1:2, :])
    return jnp.where(lanes((1, SLOTS)) < count_ref[0, owner], tok, GROUP)


def own_gate(where_ref, gate_ref):
    return column(jnp.where(where_ref[0] == 0, gate_ref[0:1, :], gate_ref[1:2, :]))


def split3(a):
    high = a.astype(BF)
    rest = a - high.astype(F32)
    mid = rest.astype(BF)
    return high.astype(F32), mid.astype(F32), rest - mid.astype(F32)


def stack_rows(rows):
    shape = (EXTRA, rows[0].shape[1])
    at, out = lax.broadcasted_iota(I32, shape, 0), jnp.zeros(shape, F32)
    for i, row in enumerate(rows):
        out = jnp.where(at == i, row, out)
    return out.astype(BF)


def pack_kernel(where_ref, count_ref, tok_ref, gate_ref, hidden_ref, w_ref, out_ref):
    gate = jnp.where(where_ref[0] == 0, gate_ref[0:1, :], gate_ref[1:2, :])
    tok = own_slots(where_ref, tok_ref, count_ref).astype(F32)
    extra = stack_rows((tok,) + split3(gate))
    w = w_ref[...].astype(F32)
    for l in range(L):
        for n in range(C * X):
            at = l * C * X + n
            out_ref[at, 0:SLOTS, :] = hidden_ref[...]
            out_ref[at, SLOTS:PACK, :] = extra
            out_ref[at, PACK:, :] = dense(slice_of(w, n, l)).astype(BF)


def dense_kernel(rows_ref, out_ref):
    for g in range(QUARTERS):
        out_ref[g] = dense(rows_ref[g].astype(F32)).astype(BF)


def weight_kernel(core_ref, mine_ref, pack_ref, part_ref, keep_ref, send_ref, routed_ref):
    ids = lax.broadcasted_iota(I32, (GROUP, SLOTS), 0)
    first = (((0,), (0,)), ((), ()))
    gates = []
    for g in range(QUARTERS):
        extra = pack_ref[g * X, SLOTS:PACK, :].astype(F32)
        gates.append(column(extra[1:2] + extra[2:3] + extra[3:4]))
        picks = jnp.where(ids == extra[0:1].astype(I32), 1.0, 0.0).astype(BF)
        rows = [mine_ref[:, g, t * TOKS : (t + 1) * TOKS, :].reshape(GROUP, LANES) for t in range(FULL)]
        rows += [
            jnp.concatenate(
                [last_tile(mine_ref[i, g, FULL * TOKS :, :].astype(F32)).astype(BF) for i in range(E * M)],
                axis=0,
            )
        ]
        rows = jnp.concatenate(rows, axis=1)
        rows = lax.dot_general(picks, rows, first, preferred_element_type=F32)
        rows = jnp.where(lanes(rows.shape) < COLS, rows, 0.0)
        routed_ref[g * SLOTS : (g + 1) * SLOTS, :] = rows.astype(BF)
    routed = routed_ref[...]

    for x in range(X):
        weighted = [
            (gates[g] * pack_ref[g * X + x, :SLOTS, :].astype(F32)).astype(BF) for g in range(QUARTERS)
        ]
        weighted = jnp.concatenate(weighted, axis=0)
        part = lax.dot_general(weighted, routed, first, preferred_element_type=F32)
        for h in range(H):
            part_ref[h, x] = dense(part[h * CHUNK : (h + 1) * CHUNK]).astype(BF)

    core = core_ref[0]
    groups = [l * C + c for c in (core, 1 - core) for l in range(L)]
    outs = [(ref, l) for ref in (keep_ref, send_ref) for l in range(L)]
    routed = jnp.concatenate(
        [routed_ref[pl.ds(pl.multiple_of(g * SLOTS, SLOTS), SLOTS), :] for g in groups], axis=0
    )
    sums = [jnp.zeros((SLOTS, 1), F32)] * QUARTERS
    for x in range(X):
        w = []
        for q in range(QUARTERS):
            rows = pack_ref[q * X + x, PACK:, :]
            rows = [rows[t * SHARE : (t + 1) * SHARE] for t in range(FULL)] + [
                last_tile(rows[FULL * SHARE :].astype(F32)).astype(BF)
            ]
            w.append(jnp.concatenate(rows, axis=1))
        w = jnp.concatenate(w, axis=0)
        proj = lax.dot_general(routed, w, (((1,), (1,)), ((), ())), preferred_element_type=F32)
        for i, (ref, l) in enumerate(outs):
            rows = proj[i * SLOTS : (i + 1) * SLOTS]
            ref[l * X + x, 0:SLOTS, :] = rows.astype(BF)
            hidden = pack_ref[groups[i] * X + x, :SLOTS, :].astype(F32)
            sums[i] = sums[i] + jnp.sum(hidden * rows, axis=1, keepdims=True)
    at = lanes((SLOTS, LANES))
    for i, (ref, l) in enumerate(outs):
        tok = column(pack_ref[groups[i] * X, SLOTS:PACK, :].astype(F32)[0:1]).astype(I32)
        device, spot = tok // ROWS, tok % ROWS
        spot = jnp.where(tok < GROUP, device // X * ROWS + spot, LANES)
        for x in range(X):
            here = (at == spot) & (device % X == x)
            row = jnp.sum(jnp.where(here, sums[i], 0.0), axis=0, keepdims=True)
            ref[l * X + x, SLOTS:PACK, :] = terms(row)


def terms(row):
    high, mid, low = split3(row)
    return stack_rows((high + pltpu.roll(mid, OWNED, 1), low))


def row_of(tile):
    row = tile[0:1] + (pltpu.roll(tile[0:1], OWNED, 1) + tile[1:2])
    return jnp.where(lanes(row.shape) < OWNED, row, 0.0)


def back_kernel(sums_ref, keep_ref, other_ref, out_ref):
    for x in range(X):
        total = sums_ref[0, x].astype(F32)
        for h in range(1, H):
            total = total + sums_ref[h, x].astype(F32)
        for l in range(L):
            out_ref[l * X + x, 0:BACK, :] = total.astype(BF)
    for n in range(L * X):
        both = keep_ref[n].astype(F32) + other_ref[n].astype(F32)
        out_ref[n, BACK : BACK + SLOTS, :] = both[:SLOTS].astype(BF)
        out_ref[n, BACK + SLOTS :, :] = terms(row_of(both[SLOTS:]))


def finish_kernel(where_ref, gate_ref, got_ref, grad_ref, spread_ref, block_ref):
    both = got_ref[0, BACK:, :].astype(F32)
    for n in range(1, L * X):
        both = both + got_ref[n, BACK:, :].astype(F32)
    grad_ref[...] = (own_gate(where_ref, gate_ref) * both[:SLOTS]).astype(BF)
    shape = (E * M * N, LANES)
    row = jnp.where(lanes(shape) // ROWS == lax.broadcasted_iota(I32, shape, 0), row_of(both[SLOTS:]), 0.0)
    shape = (LANES, ROWS)
    fold = jnp.where(lax.broadcasted_iota(I32, shape, 0) % ROWS == lanes(shape), 1.0, 0.0)
    spread_ref[...] = jnp.dot(
        row, fold, precision=lax.Precision.HIGHEST, preferred_element_type=F32
    )
    low = lanes((CHUNK, LANES)) < TAIL
    for x in range(X):
        a, b = (got_ref[l * X + x, 0:BACK, :].astype(F32) for l in range(L))
        a, b = (
            [p[t * CHUNK : (t + 1) * CHUNK] for t in range(FULL)] + [last_tile(p[FULL * CHUNK :])]
            for p in (a, b)
        )
        b = [pltpu.roll(p, TAIL, 1) for p in b]
        tiles = a[:-1] + [jnp.where(low, p, r) for p, r in zip([a[-1]] + b[:-1], b)]
        block_ref[:, x * PAIR : (x + 1) * PAIR] = jnp.concatenate(tiles, axis=1).astype(BF)


def put_columns(half_ref, out_ref, core, sem):
    width = X * PAIR
    copy = pltpu.make_async_copy(
        half_ref, out_ref.at[:, pl.ds(pl.multiple_of(core * width, LANES), width)], sem
    )
    copy.start()
    return copy


def own_half_kernel(core_ref, half_ref, out_ref, sem):
    put_columns(half_ref, out_ref, core_ref[0], sem).wait()


def other_half_kernel(core_ref, half_ref, spread_ref, out_in_ref, out_ref, gate_ref, sem):
    copy = put_columns(half_ref, out_ref, 1 - core_ref[0], sem)
    for e in range(E):
        gate_ref[e : e + 1, :] = jnp.sum(spread_ref[e * M * N : (e + 1) * M * N, :], axis=0, keepdims=True)
    copy.wait()


VM, SM, HBM = (pl.BlockSpec(memory_space=m) for m in (pltpu.VMEM, pltpu.SMEM, pl.ANY))


def call(kernel, places, outs, *args, scratch=(), flops=0, vmem=32, out_places=None, aliases={}):
    outs = [jax.ShapeDtypeStruct(s, d) for s, d in outs]
    nbytes = sum(a.size * a.dtype.itemsize for a in list(args) + outs)
    return pl.pallas_call(
        kernel,
        out_shape=outs,
        in_specs=places,
        out_specs=out_places or [VM] * len(outs),
        input_output_aliases=aliases,
        scratch_shapes=scratch,
        cost_estimate=pl.CostEstimate(flops=flops, bytes_accessed=nbytes, transcendentals=0),
        compiler_params=pltpu.CompilerParams(vmem_limit_bytes=vmem * 1024 * 1024),
    )(*args)


def on_device(grad_values, grad_scales, hidden_act, down_weight, slot_token, slot_count, slot_gate):
    low, core, owner = (lax.axis_index(a) for a in "lce")
    hidden, tok, gate = hidden_act[0], slot_token[0], slot_gate[0]
    where = owner[None].astype(I32)

    (send,) = call(
        tokens_kernel,
        [HBM, HBM],
        [((N * PARTS, ROWS, WIDE), BF)],
        grad_values, grad_scales.reshape(1, ROWS),
        scratch=[
            pltpu.VMEM((ROWS, WIDTH), BF), pltpu.VMEM((1, ROWS), BF), pltpu.SemaphoreType.DMA((2,))
        ],
        vmem=60,
    )
    mine = lax.all_to_all(send, ("l", "c", "n", "x"), 0, 0)

    w_rows = lax.dynamic_slice_in_dim(down_weight, (low * C + core) * SHARE, SHARE, 0)
    (pack,) = call(
        pack_kernel,
        [SM, SM, VM, VM, VM, VM],
        [((PARTS, PACK + W_PART, LANES), BF)],
        where, slot_count, tok, gate, hidden, w_rows,
    )
    pack, mine = lax.optimization_barrier((pack, mine))
    pack = lax.all_to_all(pack, SPLIT, 0, 0)
    (mine,) = call(
        dense_kernel, [VM], [((QUARTERS, DENSE, LANES), BF)], mine.reshape(QUARTERS, TOKS, WIDE)
    )
    mine = lax.all_gather(mine, ("e", "m"), axis=0)

    part, keep, other = call(
        weight_kernel,
        [SM, VM, VM],
        [((H, X, BACK, LANES), BF), ((L * X, PACK, LANES), BF), ((L * X, PACK, LANES), BF)],
        core[None].astype(I32), mine, pack,
        scratch=[pltpu.VMEM((QUARTERS * SLOTS, WIDE), BF)],
        flops=2 * QUARTERS * SLOTS * (COLS * GROUP + 2 * WIDE * X * UNITS),
    )
    other = lax.ppermute(other, "c", [(i, C - 1 - i) for i in range(C)])
    sums = lax.all_to_all(part, "h", 0, 0)

    (send,) = call(
        back_kernel,
        [VM, VM, VM],
        [((L * X, BACK + PACK, LANES), BF)],
        sums, keep, other,
    )
    got = lax.all_to_all(send, ("l", "x"), 0, 0)
    hidden_grad, spread, block = call(
        finish_kernel,
        [SM, VM, VM],
        [((SLOTS, UNITS), BF), ((E * M * N, ROWS), F32), ((CHUNK, X * PAIR), BF)],
        where, gate, got,
    )
    spread = lax.all_to_all(spread, ("e", "m", "n"), 0, 0, tiled=True)

    block = lax.all_gather(block, "h", axis=0, tiled=True)
    block, spread = lax.optimization_barrier((block, spread))
    other = lax.ppermute(block, "c", [(i, C - 1 - i) for i in range(C)])
    where = core[None].astype(I32)
    sem = [pltpu.SemaphoreType.DMA(())]
    (whole,) = call(
        own_half_kernel, [SM, VM], [((UNITS, WIDTH), BF)], where, block, scratch=sem, out_places=[HBM]
    )
    weight_grad, gate_grad = call(
        other_half_kernel,
        [SM, HBM, VM, HBM],
        [((UNITS, WIDTH), BF), ((E, ROWS), F32)],
        where, other, spread, whole,
        scratch=sem,
        out_places=[HBM, VM],
        aliases={3: 0},
    )
    return hidden_grad[None], weight_grad, gate_grad.T


def solution(mesh):
    fine = jax.sharding.Mesh(mesh.devices.reshape(SIZES), DP + EXPERT)
    return jax.shard_map(
        on_device,
        mesh=fine,
        in_specs=(
            P(DP + EXPERT, None),
            P(DP + EXPERT),
            P(DP, None, EXPERT),
            P(EXPERT, None),
            P(DP, None, None),
            P(DP, None),
            P(DP, None, None),
        ),
        out_specs=(P(DP, None, EXPERT), P(EXPERT, None), P(DP + EXPERT, None)),
        check_vma=False,
    )
```

```python
import jax
import jax.numpy as jnp
from jax import lax
from jax.experimental import pallas as pl
from jax.experimental.pallas import tpu as pltpu
from jax.sharding import PartitionSpec as P

BF, F32, I32 = jnp.bfloat16, jnp.float32, jnp.int32
DP, EXPERT = ("h", "l", "c"), ("e", "m", "n", "x")
H, L, C, E, M, N, X = SIZES = (4, 2, 2, 2, 2, 2, 4)
SPLIT = ("l", "c", "x")
QUARTERS, PARTS = L * C, L * C * X
LANES, TILES = 128, 4
WIDTH, SLOTS, UNITS, ROWS = 7168, 128, 128, 8
GROUP = E * M * N * X * ROWS
COLS, WIDE = WIDTH // PARTS, TILES * LANES
PAIR = 2 * COLS
SHARE = UNITS // QUARTERS
CHUNK = UNITS // H
EXTRA = 16
PACK = SLOTS + EXTRA
FULL, TAIL = TILES - 1, COLS % LANES
TOKS = N * X * ROWS
BACK = FULL * CHUNK + CHUNK // 2
W_PART = FULL * SHARE + SHARE // 2
DENSE = FULL * TOKS + TOKS // 2
OWNED = E * M * N * ROWS


def lanes(shape):
    return lax.broadcasted_iota(I32, shape, len(shape) - 1)


def column(row):
    n = row.shape[1]
    across, down = lanes((n, n)), lax.broadcasted_iota(I32, (n, n), 0)
    return jnp.sum(jnp.where(across == down, row, jnp.zeros_like(row)), axis=1, keepdims=True)


def slice_of(a, n, l):
    start = n * PAIR
    if l == 0:
        a = a[:, start : start + WIDE]
    else:
        a = pltpu.roll(a[:, start + PAIR - WIDE : start + PAIR], COLS, 1)
    return jnp.where(lanes(a.shape) < COLS, a, 0.0)


def dense(a):
    half = a.shape[0] // 2
    last = a[:, FULL * LANES :]
    last = last[:half] + pltpu.roll(last[half:], TAIL, 1)
    return jnp.concatenate([a[:, t * LANES : (t + 1) * LANES] for t in range(FULL)] + [last], axis=0)


def last_tile(a):
    return jnp.concatenate([a, pltpu.roll(a, TAIL, 1)], axis=0)


def tokens_kernel(values_ref, scales_ref, out_ref):
    scaled = values_ref[...].astype(F32) * column(scales_ref[...].astype(F32))
    for l in range(L):
        for n in range(C * X):
            part = slice_of(scaled, n, l).astype(BF)
            for i in range(N):
                out_ref[((l * C + n // X) * N + i) * X + n % X] = part


def own_slots(where_ref, tok_ref, count_ref):
    owner = where_ref[0]
    tok = jnp.where(owner == 0, tok_ref[0:1, :], tok_ref[1:2, :])
    return jnp.where(lanes((1, SLOTS)) < count_ref[0, owner], tok, GROUP)


def own_gate(where_ref, gate_ref):
    return column(jnp.where(where_ref[0] == 0, gate_ref[0:1, :], gate_ref[1:2, :]))


def split3(a):
    high = a.astype(BF)
    rest = a - high.astype(F32)
    mid = rest.astype(BF)
    return high.astype(F32), mid.astype(F32), rest - mid.astype(F32)


def stack_rows(rows):
    shape = (EXTRA, rows[0].shape[1])
    at, out = lax.broadcasted_iota(I32, shape, 0), jnp.zeros(shape, F32)
    for i, row in enumerate(rows):
        out = jnp.where(at == i, row, out)
    return out.astype(BF)


def pack_kernel(where_ref, count_ref, tok_ref, gate_ref, hidden_ref, w_ref, out_ref):
    gate = jnp.where(where_ref[0] == 0, gate_ref[0:1, :], gate_ref[1:2, :])
    tok = own_slots(where_ref, tok_ref, count_ref).astype(F32)
    extra = stack_rows((tok,) + split3(gate))
    w = w_ref[...].astype(F32)
    for l in range(L):
        for n in range(C * X):
            at = l * C * X + n
            out_ref[at, 0:SLOTS, :] = hidden_ref[...]
            out_ref[at, SLOTS:PACK, :] = extra
            out_ref[at, PACK:, :] = dense(slice_of(w, n, l)).astype(BF)


def dense_kernel(rows_ref, out_ref):
    for g in range(QUARTERS):
        out_ref[g] = dense(rows_ref[g].astype(F32)).astype(BF)


def weight_kernel(core_ref, mine_ref, pack_ref, part_ref, keep_ref, send_ref, routed_ref):
    ids = lax.broadcasted_iota(I32, (GROUP, SLOTS), 0)
    first = (((0,), (0,)), ((), ()))
    gates = []
    for g in range(QUARTERS):
        extra = pack_ref[g * X, SLOTS:PACK, :].astype(F32)
        gates.append(column(extra[1:2] + extra[2:3] + extra[3:4]))
        picks = jnp.where(ids == extra[0:1].astype(I32), 1.0, 0.0).astype(BF)
        rows = [mine_ref[:, g, t * TOKS : (t + 1) * TOKS, :].reshape(GROUP, LANES) for t in range(FULL)]
        rows += [
            jnp.concatenate(
                [last_tile(mine_ref[i, g, FULL * TOKS :, :].astype(F32)).astype(BF) for i in range(E * M)],
                axis=0,
            )
        ]
        rows = jnp.concatenate(rows, axis=1)
        rows = lax.dot_general(picks, rows, first, preferred_element_type=F32)
        rows = jnp.where(lanes(rows.shape) < COLS, rows, 0.0)
        routed_ref[g * SLOTS : (g + 1) * SLOTS, :] = rows.astype(BF)
    routed = routed_ref[...]

    for x in range(X):
        weighted = [
            (gates[g] * pack_ref[g * X + x, :SLOTS, :].astype(F32)).astype(BF) for g in range(QUARTERS)
        ]
        weighted = jnp.concatenate(weighted, axis=0)
        part = lax.dot_general(weighted, routed, first, preferred_element_type=F32)
        for h in range(H):
            part_ref[h, x] = dense(part[h * CHUNK : (h + 1) * CHUNK]).astype(BF)

    core = core_ref[0]
    groups = [l * C + c for c in (core, 1 - core) for l in range(L)]
    outs = [(ref, l) for ref in (keep_ref, send_ref) for l in range(L)]
    routed = jnp.concatenate(
        [routed_ref[pl.ds(pl.multiple_of(g * SLOTS, SLOTS), SLOTS), :] for g in groups], axis=0
    )
    sums = [jnp.zeros((SLOTS, 1), F32)] * QUARTERS
    for x in range(X):
        w = []
        for q in range(QUARTERS):
            rows = pack_ref[q * X + x, PACK:, :]
            rows = [rows[t * SHARE : (t + 1) * SHARE] for t in range(FULL)] + [
                last_tile(rows[FULL * SHARE :].astype(F32)).astype(BF)
            ]
            w.append(jnp.concatenate(rows, axis=1))
        w = jnp.concatenate(w, axis=0)
        proj = lax.dot_general(routed, w, (((1,), (1,)), ((), ())), preferred_element_type=F32)
        for i, (ref, l) in enumerate(outs):
            rows = proj[i * SLOTS : (i + 1) * SLOTS]
            ref[l * X + x, 0:SLOTS, :] = rows.astype(BF)
            hidden = pack_ref[groups[i] * X + x, :SLOTS, :].astype(F32)
            sums[i] = sums[i] + jnp.sum(hidden * rows, axis=1, keepdims=True)
    at = lanes((SLOTS, LANES))
    for i, (ref, l) in enumerate(outs):
        tok = column(pack_ref[groups[i] * X, SLOTS:PACK, :].astype(F32)[0:1]).astype(I32)
        device, spot = tok // ROWS, tok % ROWS
        spot = jnp.where(tok < GROUP, device // X * ROWS + spot, LANES)
        for x in range(X):
            here = (at == spot) & (device % X == x)
            row = jnp.sum(jnp.where(here, sums[i], 0.0), axis=0, keepdims=True)
            ref[l * X + x, SLOTS:PACK, :] = terms(row)


def terms(row):
    high, mid, low = split3(row)
    return stack_rows((high + pltpu.roll(mid, OWNED, 1), low))


def row_of(tile):
    row = tile[0:1] + (pltpu.roll(tile[0:1], OWNED, 1) + tile[1:2])
    return jnp.where(lanes(row.shape) < OWNED, row, 0.0)


def back_kernel(sums_ref, keep_ref, other_ref, out_ref):
    for x in range(X):
        total = sums_ref[0, x].astype(F32)
        for h in range(1, H):
            total = total + sums_ref[h, x].astype(F32)
        for l in range(L):
            out_ref[l * X + x, 0:BACK, :] = total.astype(BF)
    for n in range(L * X):
        both = keep_ref[n].astype(F32) + other_ref[n].astype(F32)
        out_ref[n, BACK : BACK + SLOTS, :] = both[:SLOTS].astype(BF)
        out_ref[n, BACK + SLOTS :, :] = terms(row_of(both[SLOTS:]))


def finish_kernel(where_ref, gate_ref, got_ref, grad_ref, spread_ref, block_ref):
    both = got_ref[0, BACK:, :].astype(F32)
    for n in range(1, L * X):
        both = both + got_ref[n, BACK:, :].astype(F32)
    grad_ref[...] = (own_gate(where_ref, gate_ref) * both[:SLOTS]).astype(BF)
    shape = (E * M * N, LANES)
    row = jnp.where(lanes(shape) // ROWS == lax.broadcasted_iota(I32, shape, 0), row_of(both[SLOTS:]), 0.0)
    shape = (LANES, ROWS)
    fold = jnp.where(lax.broadcasted_iota(I32, shape, 0) % ROWS == lanes(shape), 1.0, 0.0)
    spread_ref[...] = jnp.dot(
        row, fold, precision=lax.Precision.HIGHEST, preferred_element_type=F32
    )
    low = lanes((CHUNK, LANES)) < TAIL
    for x in range(X):
        a, b = (got_ref[l * X + x, 0:BACK, :].astype(F32) for l in range(L))
        a, b = (
            [p[t * CHUNK : (t + 1) * CHUNK] for t in range(FULL)] + [last_tile(p[FULL * CHUNK :])]
            for p in (a, b)
        )
        b = [pltpu.roll(p, TAIL, 1) for p in b]
        tiles = a[:-1] + [jnp.where(low, p, r) for p, r in zip([a[-1]] + b[:-1], b)]
        block_ref[:, x * PAIR : (x + 1) * PAIR] = jnp.concatenate(tiles, axis=1).astype(BF)


def put_columns(half_ref, out_ref, core, sem):
    width = X * PAIR
    copy = pltpu.make_async_copy(
        half_ref, out_ref.at[:, pl.ds(pl.multiple_of(core * width, LANES), width)], sem
    )
    copy.start()
    return copy


def own_half_kernel(core_ref, half_ref, out_ref, sem):
    put_columns(half_ref, out_ref, core_ref[0], sem).wait()


def other_half_kernel(core_ref, half_ref, spread_ref, out_in_ref, out_ref, gate_ref, sem):
    copy = put_columns(half_ref, out_ref, 1 - core_ref[0], sem)
    for e in range(E):
        gate_ref[e : e + 1, :] = jnp.sum(spread_ref[e * M * N : (e + 1) * M * N, :], axis=0, keepdims=True)
    copy.wait()


VM, SM, HBM = (pl.BlockSpec(memory_space=m) for m in (pltpu.VMEM, pltpu.SMEM, pl.ANY))


def call(kernel, places, outs, *args, scratch=(), flops=0, vmem=32, out_places=None, aliases={}):
    outs = [jax.ShapeDtypeStruct(s, d) for s, d in outs]
    nbytes = sum(a.size * a.dtype.itemsize for a in list(args) + outs)
    return pl.pallas_call(
        kernel,
        out_shape=outs,
        in_specs=places,
        out_specs=out_places or [VM] * len(outs),
        input_output_aliases=aliases,
        scratch_shapes=scratch,
        cost_estimate=pl.CostEstimate(flops=flops, bytes_accessed=nbytes, transcendentals=0),
        compiler_params=pltpu.CompilerParams(vmem_limit_bytes=vmem * 1024 * 1024),
    )(*args)


def on_device(grad_values, grad_scales, hidden_act, down_weight, slot_token, slot_count, slot_gate):
    low, core, owner = (lax.axis_index(a) for a in "lce")
    hidden, tok, gate = hidden_act[0], slot_token[0], slot_gate[0]
    where = owner[None].astype(I32)

    (send,) = call(
        tokens_kernel,
        [VM, VM],
        [((N * PARTS, ROWS, WIDE), BF)],
        grad_values, grad_scales.reshape(1, ROWS),
        vmem=60,
    )
    mine = lax.all_to_all(send, ("l", "c", "n", "x"), 0, 0)

    w_rows = lax.dynamic_slice_in_dim(down_weight, (low * C + core) * SHARE, SHARE, 0)
    (pack,) = call(
        pack_kernel,
        [SM, SM, VM, VM, VM, VM],
        [((PARTS, PACK + W_PART, LANES), BF)],
        where, slot_count, tok, gate, hidden, w_rows,
    )
    pack, mine = lax.optimization_barrier((pack, mine))
    pack = lax.all_to_all(pack, SPLIT, 0, 0)
    (mine,) = call(
        dense_kernel, [VM], [((QUARTERS, DENSE, LANES), BF)], mine.reshape(QUARTERS, TOKS, WIDE)
    )
    mine = lax.all_gather(mine, ("e", "m"), axis=0)

    part, keep, other = call(
        weight_kernel,
        [SM, VM, VM],
        [((H, X, BACK, LANES), BF), ((L * X, PACK, LANES), BF), ((L * X, PACK, LANES), BF)],
        core[None].astype(I32), mine, pack,
        scratch=[pltpu.VMEM((QUARTERS * SLOTS, WIDE), BF)],
        flops=2 * QUARTERS * SLOTS * (COLS * GROUP + 2 * WIDE * X * UNITS),
    )
    other = lax.ppermute(other, "c", [(i, C - 1 - i) for i in range(C)])
    sums = lax.all_to_all(part, "h", 0, 0)

    (send,) = call(
        back_kernel,
        [VM, VM, VM],
        [((L * X, BACK + PACK, LANES), BF)],
        sums, keep, other,
    )
    got = lax.all_to_all(send, ("l", "x"), 0, 0)
    hidden_grad, spread, block = call(
        finish_kernel,
        [SM, VM, VM],
        [((SLOTS, UNITS), BF), ((E * M * N, ROWS), F32), ((CHUNK, X * PAIR), BF)],
        where, gate, got,
    )
    spread = lax.all_to_all(spread, ("e", "m", "n"), 0, 0, tiled=True)

    block = lax.all_gather(block, "h", axis=0, tiled=True)
    block, spread = lax.optimization_barrier((block, spread))
    other = lax.ppermute(block, "c", [(i, C - 1 - i) for i in range(C)])
    where = core[None].astype(I32)
    sem = [pltpu.SemaphoreType.DMA(())]
    (whole,) = call(
        own_half_kernel, [SM, VM], [((UNITS, WIDTH), BF)], where, block, scratch=sem, out_places=[HBM]
    )
    weight_grad, gate_grad = call(
        other_half_kernel,
        [SM, HBM, VM, HBM],
        [((UNITS, WIDTH), BF), ((E, ROWS), F32)],
        where, other, spread, whole,
        scratch=sem,
        out_places=[HBM, VM],
        aliases={3: 0},
    )
    return hidden_grad[None], weight_grad, gate_grad.T


def solution(mesh):
    fine = jax.sharding.Mesh(mesh.devices.reshape(SIZES), DP + EXPERT)
    return jax.shard_map(
        on_device,
        mesh=fine,
        in_specs=(
            P(DP + EXPERT, None),
            P(DP + EXPERT),
            P(DP, None, EXPERT),
            P(EXPERT, None),
            P(DP, None, None),
            P(DP, None),
            P(DP, None, None),
        ),
        out_specs=(P(DP, None, EXPERT), P(EXPERT, None), P(DP + EXPERT, None)),
        check_vma=False,
    )
```

```python
import jax
import jax.numpy as jnp
from jax import lax
from jax.experimental import pallas as pl
from jax.experimental.pallas import tpu as pltpu
from jax.sharding import PartitionSpec as P

BF, F32, I32 = jnp.bfloat16, jnp.float32, jnp.int32
DP, EXPERT = ("h", "l", "c"), ("e", "m", "n", "x")
H, L, C, E, M, N, X = SIZES = (4, 2, 2, 2, 2, 2, 4)
QUARTERS, PARTS = L * C, L * C * X
LANES, TILES = 128, 4
WIDTH, SLOTS, UNITS, ROWS = 7168, 128, 128, 8
GROUP = E * M * N * X * ROWS
COLS, WIDE = WIDTH // PARTS, TILES * LANES
PAIR = 2 * COLS
SHARE = UNITS // L
CHUNK = UNITS // H
EXTRA = 16
PACK = SLOTS + EXTRA
FULL, TAIL = TILES - 1, COLS % LANES
TOKS = N * X * ROWS
BACK = FULL * CHUNK + CHUNK // 2
W_PART = FULL * SHARE + SHARE // 2
DENSE = FULL * TOKS + TOKS // 2
OWNED = E * M * N * ROWS


def lanes(shape):
    return lax.broadcasted_iota(I32, shape, len(shape) - 1)


def column(row):
    n = row.shape[1]
    across, down = lanes((n, n)), lax.broadcasted_iota(I32, (n, n), 0)
    return jnp.sum(jnp.where(across == down, row, jnp.zeros_like(row)), axis=1, keepdims=True)


def slice_of(a, n, l):
    start = n * PAIR
    if l == 0:
        a = a[:, start : start + WIDE]
    else:
        a = pltpu.roll(a[:, start + PAIR - WIDE : start + PAIR], COLS, 1)
    return jnp.where(lanes(a.shape) < COLS, a, 0.0)


def dense(a):
    half = a.shape[0] // 2
    last = a[:, FULL * LANES :]
    last = last[:half] + pltpu.roll(last[half:], TAIL, 1)
    return jnp.concatenate([a[:, t * LANES : (t + 1) * LANES] for t in range(FULL)] + [last], axis=0)


def last_tile(a):
    return jnp.concatenate([a, pltpu.roll(a, TAIL, 1)], axis=0)


def tokens_kernel(values_ref, scales_ref, out_ref):
    scaled = values_ref[...].astype(F32) * column(scales_ref[...].astype(F32))
    for l in range(L):
        for n in range(C * X):
            part = slice_of(scaled, n, l).astype(BF)
            for i in range(N):
                out_ref[((l * C + n // X) * N + i) * X + n % X] = part


def own_slots(where_ref, tok_ref, count_ref):
    owner = where_ref[0]
    tok = jnp.where(owner == 0, tok_ref[0:1, :], tok_ref[1:2, :])
    return jnp.where(lanes((1, SLOTS)) < count_ref[0, owner], tok, GROUP)


def own_gate(where_ref, gate_ref):
    return column(jnp.where(where_ref[0] == 0, gate_ref[0:1, :], gate_ref[1:2, :]))


def split3(a):
    high = a.astype(BF)
    rest = a - high.astype(F32)
    mid = rest.astype(BF)
    return high.astype(F32), mid.astype(F32), rest - mid.astype(F32)


def stack_rows(rows):
    shape = (EXTRA, rows[0].shape[1])
    at, out = lax.broadcasted_iota(I32, shape, 0), jnp.zeros(shape, F32)
    for i, row in enumerate(rows):
        out = jnp.where(at == i, row, out)
    return out.astype(BF)


def pack_kernel(where_ref, count_ref, tok_ref, gate_ref, hidden_ref, out_ref):
    gate = jnp.where(where_ref[0] == 0, gate_ref[0:1, :], gate_ref[1:2, :])
    tok = own_slots(where_ref, tok_ref, count_ref).astype(F32)
    out_ref[0:SLOTS, :] = hidden_ref[...]
    out_ref[SLOTS:PACK, :] = stack_rows((tok,) + split3(gate))


def send_kernel(packs_ref, w_ref, out_ref):
    w = w_ref[...].astype(F32)
    for l in range(L):
        for x in range(X):
            out_ref[l * X + x, 0 : C * PACK, :] = packs_ref[...]
            out_ref[l * X + x, C * PACK :, :] = dense(slice_of(w, x, l)).astype(BF)


def dense_kernel(rows_ref, out_ref):
    for g in range(QUARTERS):
        out_ref[g] = dense(rows_ref[g].astype(F32)).astype(BF)


def weight_kernel(core_ref, mine_ref, pack_ref, part_ref, keep_ref, send_ref, routed_ref):
    ids = lax.broadcasted_iota(I32, (GROUP, SLOTS), 0)
    first = (((0,), (0,)), ((), ()))
    gates = []
    for g in range(QUARTERS):
        extra = pack_ref[g // C * X, g % C * PACK + SLOTS : (g % C + 1) * PACK, :].astype(F32)
        gates.append(column(extra[1:2] + extra[2:3] + extra[3:4]))
        picks = jnp.where(ids == extra[0:1].astype(I32), 1.0, 0.0).astype(BF)
        rows = [mine_ref[:, g, t * TOKS : (t + 1) * TOKS, :].reshape(GROUP, LANES) for t in range(FULL)]
        rows += [
            jnp.concatenate(
                [last_tile(mine_ref[i, g, FULL * TOKS :, :].astype(F32)).astype(BF) for i in range(E * M)],
                axis=0,
            )
        ]
        rows = jnp.concatenate(rows, axis=1)
        rows = lax.dot_general(picks, rows, first, preferred_element_type=F32)
        rows = jnp.where(lanes(rows.shape) < COLS, rows, 0.0)
        routed_ref[g * SLOTS : (g + 1) * SLOTS, :] = rows.astype(BF)
    routed = routed_ref[...]

    for x in range(X):
        weighted = [
            (gates[g] * pack_ref[g // C * X + x, pl.ds(g % C * PACK, SLOTS), :].astype(F32)).astype(BF)
            for g in range(QUARTERS)
        ]
        weighted = jnp.concatenate(weighted, axis=0)
        part = lax.dot_general(weighted, routed, first, preferred_element_type=F32)
        for h in range(H):
            part_ref[h, x] = dense(part[h * CHUNK : (h + 1) * CHUNK]).astype(BF)

    core = core_ref[0]
    groups = [(l, c) for c in (core, 1 - core) for l in range(L)]
    outs = [(ref, l) for ref in (keep_ref, send_ref) for l in range(L)]
    routed = jnp.concatenate(
        [routed_ref[pl.ds(pl.multiple_of((l * C + c) * SLOTS, SLOTS), SLOTS), :] for l, c in groups], axis=0
    )
    sums = [jnp.zeros((SLOTS, 1), F32)] * QUARTERS
    for x in range(X):
        w = []
        for l in range(L):
            rows = pack_ref[l * X + x, C * PACK :, :]
            rows = [rows[t * SHARE : (t + 1) * SHARE] for t in range(FULL)] + [
                last_tile(rows[FULL * SHARE :].astype(F32)).astype(BF)
            ]
            w.append(jnp.concatenate(rows, axis=1))
        w = jnp.concatenate(w, axis=0)
        proj = lax.dot_general(routed, w, (((1,), (1,)), ((), ())), preferred_element_type=F32)
        for i, (ref, l) in enumerate(outs):
            rows = proj[i * SLOTS : (i + 1) * SLOTS]
            ref[l * X + x, 0:SLOTS, :] = rows.astype(BF)
            at = pl.multiple_of(groups[i][1] * PACK, EXTRA)
            hidden = pack_ref[l * X + x, pl.ds(at, SLOTS), :].astype(F32)
            sums[i] = sums[i] + jnp.sum(hidden * rows, axis=1, keepdims=True)
    at = lanes((SLOTS, LANES))
    for i, (ref, l) in enumerate(outs):
        row = pl.multiple_of(groups[i][1] * PACK + SLOTS, EXTRA)
        tok = column(pack_ref[l * X, pl.ds(row, EXTRA), :].astype(F32)[0:1]).astype(I32)
        device, spot = tok // ROWS, tok % ROWS
        spot = jnp.where(tok < GROUP, device // X * ROWS + spot, LANES)
        for x in range(X):
            here = (at == spot) & (device % X == x)
            row = jnp.sum(jnp.where(here, sums[i], 0.0), axis=0, keepdims=True)
            ref[l * X + x, SLOTS:PACK, :] = terms(row)


def terms(row):
    high, mid, low = split3(row)
    return stack_rows((high + pltpu.roll(mid, OWNED, 1), low))


def row_of(tile):
    row = tile[0:1] + (pltpu.roll(tile[0:1], OWNED, 1) + tile[1:2])
    return jnp.where(lanes(row.shape) < OWNED, row, 0.0)


def back_kernel(sums_ref, keep_ref, other_ref, out_ref):
    for x in range(X):
        total = sums_ref[0, x].astype(F32)
        for h in range(1, H):
            total = total + sums_ref[h, x].astype(F32)
        for l in range(L):
            out_ref[l * X + x, 0:BACK, :] = total.astype(BF)
    for n in range(L * X):
        both = keep_ref[n].astype(F32) + other_ref[n].astype(F32)
        out_ref[n, BACK : BACK + SLOTS, :] = both[:SLOTS].astype(BF)
        out_ref[n, BACK + SLOTS :, :] = terms(row_of(both[SLOTS:]))


def finish_kernel(where_ref, gate_ref, got_ref, grad_ref, spread_ref, block_ref):
    both = got_ref[0, BACK:, :].astype(F32)
    for n in range(1, L * X):
        both = both + got_ref[n, BACK:, :].astype(F32)
    grad_ref[...] = (own_gate(where_ref, gate_ref) * both[:SLOTS]).astype(BF)
    shape = (E * M * N, LANES)
    row = jnp.where(lanes(shape) // ROWS == lax.broadcasted_iota(I32, shape, 0), row_of(both[SLOTS:]), 0.0)
    shape = (LANES, ROWS)
    fold = jnp.where(lax.broadcasted_iota(I32, shape, 0) % ROWS == lanes(shape), 1.0, 0.0)
    spread_ref[...] = jnp.dot(
        row, fold, precision=lax.Precision.HIGHEST, preferred_element_type=F32
    )
    low = lanes((CHUNK, LANES)) < TAIL
    for x in range(X):
        a, b = (got_ref[l * X + x, 0:BACK, :].astype(F32) for l in range(L))
        a, b = (
            [p[t * CHUNK : (t + 1) * CHUNK] for t in range(FULL)] + [last_tile(p[FULL * CHUNK :])]
            for p in (a, b)
        )
        b = [pltpu.roll(p, TAIL, 1) for p in b]
        tiles = a[:-1] + [jnp.where(low, p, r) for p, r in zip([a[-1]] + b[:-1], b)]
        block_ref[:, x * PAIR : (x + 1) * PAIR] = jnp.concatenate(tiles, axis=1).astype(BF)


def put_columns(half_ref, out_ref, core, sem):
    width = X * PAIR
    copy = pltpu.make_async_copy(
        half_ref, out_ref.at[:, pl.ds(pl.multiple_of(core * width, LANES), width)], sem
    )
    copy.start()
    return copy


def own_half_kernel(core_ref, half_ref, out_ref, sem):
    put_columns(half_ref, out_ref, core_ref[0], sem).wait()


def other_half_kernel(core_ref, half_ref, spread_ref, out_in_ref, out_ref, gate_ref, sem):
    copy = put_columns(half_ref, out_ref, 1 - core_ref[0], sem)
    for e in range(E):
        gate_ref[e : e + 1, :] = jnp.sum(spread_ref[e * M * N : (e + 1) * M * N, :], axis=0, keepdims=True)
    copy.wait()


VM, SM, HBM = (pl.BlockSpec(memory_space=m) for m in (pltpu.VMEM, pltpu.SMEM, pl.ANY))


def call(kernel, places, outs, *args, scratch=(), flops=0, vmem=32, out_places=None, aliases={}):
    outs = [jax.ShapeDtypeStruct(s, d) for s, d in outs]
    nbytes = sum(a.size * a.dtype.itemsize for a in list(args) + outs)
    return pl.pallas_call(
        kernel,
        out_shape=outs,
        in_specs=places,
        out_specs=out_places or [VM] * len(outs),
        input_output_aliases=aliases,
        scratch_shapes=scratch,
        cost_estimate=pl.CostEstimate(flops=flops, bytes_accessed=nbytes, transcendentals=0),
        compiler_params=pltpu.CompilerParams(vmem_limit_bytes=vmem * 1024 * 1024),
    )(*args)


def on_device(grad_values, grad_scales, hidden_act, down_weight, slot_token, slot_count, slot_gate):
    low, core, owner = (lax.axis_index(a) for a in "lce")
    hidden, tok, gate = hidden_act[0], slot_token[0], slot_gate[0]
    where = owner[None].astype(I32)

    (send,) = call(
        tokens_kernel,
        [VM, VM],
        [((N * PARTS, ROWS, WIDE), BF)],
        grad_values, grad_scales.reshape(1, ROWS),
        vmem=60,
    )
    mine = lax.all_to_all(send, ("l", "c", "n", "x"), 0, 0)

    (pack,) = call(
        pack_kernel,
        [SM, SM, VM, VM, VM],
        [((PACK, LANES), BF)],
        where, slot_count, tok, gate, hidden,
    )
    packs = lax.all_gather(pack, "c", axis=0, tiled=True)
    width = X * PAIR
    w_part = lax.dynamic_slice(down_weight, (low * SHARE, core * width), (SHARE, width))
    (pack,) = call(send_kernel, [VM, VM], [((L * X, C * PACK + W_PART, LANES), BF)], packs, w_part)
    pack, mine = lax.optimization_barrier((pack, mine))
    pack = lax.all_to_all(pack, ("l", "x"), 0, 0)
    (mine,) = call(
        dense_kernel, [VM], [((QUARTERS, DENSE, LANES), BF)], mine.reshape(QUARTERS, TOKS, WIDE)
    )
    mine = lax.all_gather(mine, ("e", "m"), axis=0)

    part, keep, other = call(
        weight_kernel,
        [SM, VM, VM],
        [((H, X, BACK, LANES), BF), ((L * X, PACK, LANES), BF), ((L * X, PACK, LANES), BF)],
        core[None].astype(I32), mine, pack,
        scratch=[pltpu.VMEM((QUARTERS * SLOTS, WIDE), BF)],
        flops=2 * QUARTERS * SLOTS * (COLS * GROUP + 2 * WIDE * X * UNITS),
    )
    other = lax.ppermute(other, "c", [(i, C - 1 - i) for i in range(C)])
    sums = lax.all_to_all(part, "h", 0, 0)

    (send,) = call(
        back_kernel,
        [VM, VM, VM],
        [((L * X, BACK + PACK, LANES), BF)],
        sums, keep, other,
    )
    got = lax.all_to_all(send, ("l", "x"), 0, 0)
    hidden_grad, spread, block = call(
        finish_kernel,
        [SM, VM, VM],
        [((SLOTS, UNITS), BF), ((E * M * N, ROWS), F32), ((CHUNK, X * PAIR), BF)],
        where, gate, got,
    )
    spread = lax.all_to_all(spread, ("e", "m", "n"), 0, 0, tiled=True)

    block = lax.all_gather(block, "h", axis=0, tiled=True)
    block, spread = lax.optimization_barrier((block, spread))
    other = lax.ppermute(block, "c", [(i, C - 1 - i) for i in range(C)])
    where = core[None].astype(I32)
    sem = [pltpu.SemaphoreType.DMA(())]
    (whole,) = call(
        own_half_kernel, [SM, VM], [((UNITS, WIDTH), BF)], where, block, scratch=sem, out_places=[HBM]
    )
    weight_grad, gate_grad = call(
        other_half_kernel,
        [SM, HBM, VM, HBM],
        [((UNITS, WIDTH), BF), ((E, ROWS), F32)],
        where, other, spread, whole,
        scratch=sem,
        out_places=[HBM, VM],
        aliases={3: 0},
    )
    return hidden_grad[None], weight_grad, gate_grad.T


def solution(mesh):
    fine = jax.sharding.Mesh(mesh.devices.reshape(SIZES), DP + EXPERT)
    return jax.shard_map(
        on_device,
        mesh=fine,
        in_specs=(
            P(DP + EXPERT, None),
            P(DP + EXPERT),
            P(DP, None, EXPERT),
            P(EXPERT, None),
            P(DP, None, None),
            P(DP, None),
            P(DP, None, None),
        ),
        out_specs=(P(DP, None, EXPERT), P(EXPERT, None), P(DP + EXPERT, None)),
        check_vma=False,
    )
```

```python
import jax
import jax.numpy as jnp
from jax import lax
from jax.experimental import pallas as pl
from jax.experimental.pallas import tpu as pltpu
from jax.sharding import PartitionSpec as P

BF, F32, I32 = jnp.bfloat16, jnp.float32, jnp.int32
DP, EXPERT = ("h", "l", "c"), ("e", "m", "n", "x")
H, L, C, E, M, N, X = SIZES = (4, 2, 2, 2, 2, 2, 4)
QUARTERS, PARTS = L * C, L * C * X
LANES, TILES = 128, 4
WIDTH, SLOTS, UNITS, ROWS = 7168, 128, 128, 8
GROUP = E * M * N * X * ROWS
COLS, WIDE = WIDTH // PARTS, TILES * LANES
PAIR = 2 * COLS
SHARE = UNITS // L
CHUNK = UNITS // H
EXTRA = 16
PACK = SLOTS + EXTRA
FULL, TAIL = TILES - 1, COLS % LANES
TOKS = N * X * ROWS
BACK = FULL * CHUNK + CHUNK // 2
W_PART = FULL * SHARE + SHARE // 2
DENSE = FULL * TOKS + TOKS // 2
FLAT = ROWS * WIDTH // LANES
OWNED = E * M * N * ROWS


def lanes(shape):
    return lax.broadcasted_iota(I32, shape, len(shape) - 1)


def column(row):
    n = row.shape[1]
    across, down = lanes((n, n)), lax.broadcasted_iota(I32, (n, n), 0)
    return jnp.sum(jnp.where(across == down, row, jnp.zeros_like(row)), axis=1, keepdims=True)


def slice_of(a, n, l):
    start = n * PAIR
    if l == 0:
        a = a[:, start : start + WIDE]
    else:
        a = pltpu.roll(a[:, start + PAIR - WIDE : start + PAIR], COLS, 1)
    return jnp.where(lanes(a.shape) < COLS, a, 0.0)


def dense(a):
    half = a.shape[0] // 2
    last = a[:, FULL * LANES :]
    last = last[:half] + pltpu.roll(last[half:], TAIL, 1)
    return jnp.concatenate([a[:, t * LANES : (t + 1) * LANES] for t in range(FULL)] + [last], axis=0)


def last_tile(a):
    return jnp.concatenate([a, pltpu.roll(a, TAIL, 1)], axis=0)


def own_slots(where_ref, tok_ref, count_ref):
    owner = where_ref[0]
    tok = jnp.where(owner == 0, tok_ref[0:1, :], tok_ref[1:2, :])
    return jnp.where(lanes((1, SLOTS)) < count_ref[0, owner], tok, GROUP)


def own_gate(where_ref, gate_ref):
    return column(jnp.where(where_ref[0] == 0, gate_ref[0:1, :], gate_ref[1:2, :]))


def split3(a):
    high = a.astype(BF)
    rest = a - high.astype(F32)
    mid = rest.astype(BF)
    return high.astype(F32), mid.astype(F32), rest - mid.astype(F32)


def stack_rows(rows):
    shape = (EXTRA, rows[0].shape[1])
    at, out = lax.broadcasted_iota(I32, shape, 0), jnp.zeros(shape, F32)
    for i, row in enumerate(rows):
        out = jnp.where(at == i, row, out)
    return out.astype(BF)


def first_kernel(where_ref, count_ref, tok_ref, gate_ref, hidden_ref, values_ref, scales_ref, out_ref):
    scaled = values_ref[...].astype(F32) * column(scales_ref[...].astype(F32))
    for t in range(0, WIDTH // LANES, 2):
        two = [scaled[:, i * LANES : (i + 1) * LANES] for i in (t, t + 1)]
        out_ref[t * ROWS : (t + 2) * ROWS, :] = jnp.concatenate(two, axis=0).astype(BF)
    gate = jnp.where(where_ref[0] == 0, gate_ref[0:1, :], gate_ref[1:2, :])
    tok = own_slots(where_ref, tok_ref, count_ref).astype(F32)
    out_ref[FLAT : FLAT + SLOTS, :] = hidden_ref[...]
    out_ref[FLAT + SLOTS :, :] = stack_rows((tok,) + split3(gate))


def tokens_kernel(core_ref, both_ref, out_ref):
    half = FLAT // C
    rows = []
    for c in range(C):
        a = both_ref[c, pl.ds(pl.multiple_of(core_ref[0] * half, EXTRA), half), :].astype(F32)
        rows.append(jnp.concatenate([a[i : i + ROWS] for i in range(0, half, ROWS)], axis=1))
    rows = jnp.concatenate(rows, axis=0)
    for l in range(L):
        for x in range(X):
            part = slice_of(rows, x, l).astype(BF)
            for i in range(N):
                out_ref[(l * N + i) * X + x] = part


def send_kernel(both_ref, w_ref, out_ref):
    w = w_ref[...].astype(F32)
    for l in range(L):
        for x in range(X):
            for c in range(C):
                out_ref[l * X + x, c * PACK : (c + 1) * PACK, :] = both_ref[c, FLAT:, :]
            out_ref[l * X + x, C * PACK :, :] = dense(slice_of(w, x, l)).astype(BF)


def dense_kernel(rows_ref, out_ref):
    for l in range(L):
        rows = [rows_ref[l * N * X + i].astype(F32) for i in range(N * X)]
        for c in range(C):
            part = jnp.concatenate([a[c * ROWS : (c + 1) * ROWS] for a in rows], axis=0)
            out_ref[l * C + c] = dense(part).astype(BF)


def weight_kernel(core_ref, mine_ref, pack_ref, part_ref, keep_ref, send_ref, routed_ref):
    ids = lax.broadcasted_iota(I32, (GROUP, SLOTS), 0)
    first = (((0,), (0,)), ((), ()))
    gates = []
    for g in range(QUARTERS):
        extra = pack_ref[g // C * X, g % C * PACK + SLOTS : (g % C + 1) * PACK, :].astype(F32)
        gates.append(column(extra[1:2] + extra[2:3] + extra[3:4]))
        picks = jnp.where(ids == extra[0:1].astype(I32), 1.0, 0.0).astype(BF)
        rows = [mine_ref[:, g, t * TOKS : (t + 1) * TOKS, :].reshape(GROUP, LANES) for t in range(FULL)]
        rows += [
            jnp.concatenate(
                [last_tile(mine_ref[i, g, FULL * TOKS :, :].astype(F32)).astype(BF) for i in range(E * M)],
                axis=0,
            )
        ]
        rows = jnp.concatenate(rows, axis=1)
        rows = lax.dot_general(picks, rows, first, preferred_element_type=F32)
        rows = jnp.where(lanes(rows.shape) < COLS, rows, 0.0)
        routed_ref[g * SLOTS : (g + 1) * SLOTS, :] = rows.astype(BF)
    routed = routed_ref[...]

    for x in range(X):
        weighted = [
            (gates[g] * pack_ref[g // C * X + x, pl.ds(g % C * PACK, SLOTS), :].astype(F32)).astype(BF)
            for g in range(QUARTERS)
        ]
        weighted = jnp.concatenate(weighted, axis=0)
        part = lax.dot_general(weighted, routed, first, preferred_element_type=F32)
        for h in range(H):
            part_ref[h, x] = dense(part[h * CHUNK : (h + 1) * CHUNK]).astype(BF)

    core = core_ref[0]
    groups = [(l, c) for c in (core, 1 - core) for l in range(L)]
    outs = [(ref, l) for ref in (keep_ref, send_ref) for l in range(L)]
    routed = jnp.concatenate(
        [routed_ref[pl.ds(pl.multiple_of((l * C + c) * SLOTS, SLOTS), SLOTS), :] for l, c in groups], axis=0
    )
    sums = [jnp.zeros((SLOTS, 1), F32)] * QUARTERS
    for x in range(X):
        w = []
        for l in range(L):
            rows = pack_ref[l * X + x, C * PACK :, :]
            rows = [rows[t * SHARE : (t + 1) * SHARE] for t in range(FULL)] + [
                last_tile(rows[FULL * SHARE :].astype(F32)).astype(BF)
            ]
            w.append(jnp.concatenate(rows, axis=1))
        w = jnp.concatenate(w, axis=0)
        proj = lax.dot_general(routed, w, (((1,), (1,)), ((), ())), preferred_element_type=F32)
        for i, (ref, l) in enumerate(outs):
            rows = proj[i * SLOTS : (i + 1) * SLOTS]
            ref[l * X + x, 0:SLOTS, :] = rows.astype(BF)
            at = pl.multiple_of(groups[i][1] * PACK, EXTRA)
            hidden = pack_ref[l * X + x, pl.ds(at, SLOTS), :].astype(F32)
            sums[i] = sums[i] + jnp.sum(hidden * rows, axis=1, keepdims=True)
    at = lanes((SLOTS, LANES))
    for i, (ref, l) in enumerate(outs):
        row = pl.multiple_of(groups[i][1] * PACK + SLOTS, EXTRA)
        tok = column(pack_ref[l * X, pl.ds(row, EXTRA), :].astype(F32)[0:1]).astype(I32)
        device, spot = tok // ROWS, tok % ROWS
        spot = jnp.where(tok < GROUP, device // X * ROWS + spot, LANES)
        for x in range(X):
            here = (at == spot) & (device % X == x)
            row = jnp.sum(jnp.where(here, sums[i], 0.0), axis=0, keepdims=True)
            ref[l * X + x, SLOTS:PACK, :] = terms(row)


def terms(row):
    high, mid, low = split3(row)
    return stack_rows((high + pltpu.roll(mid, OWNED, 1), low))


def row_of(tile):
    row = tile[0:1] + (pltpu.roll(tile[0:1], OWNED, 1) + tile[1:2])
    return jnp.where(lanes(row.shape) < OWNED, row, 0.0)


def back_kernel(sums_ref, keep_ref, other_ref, out_ref):
    for x in range(X):
        total = sums_ref[0, x].astype(F32)
        for h in range(1, H):
            total = total + sums_ref[h, x].astype(F32)
        for l in range(L):
            out_ref[l * X + x, 0:BACK, :] = total.astype(BF)
    for n in range(L * X):
        both = keep_ref[n].astype(F32) + other_ref[n].astype(F32)
        out_ref[n, BACK : BACK + SLOTS, :] = both[:SLOTS].astype(BF)
        out_ref[n, BACK + SLOTS :, :] = terms(row_of(both[SLOTS:]))


def finish_kernel(where_ref, gate_ref, got_ref, grad_ref, spread_ref, block_ref):
    both = got_ref[0, BACK:, :].astype(F32)
    for n in range(1, L * X):
        both = both + got_ref[n, BACK:, :].astype(F32)
    grad_ref[...] = (own_gate(where_ref, gate_ref) * both[:SLOTS]).astype(BF)
    shape = (E * M * N, LANES)
    row = jnp.where(lanes(shape) // ROWS == lax.broadcasted_iota(I32, shape, 0), row_of(both[SLOTS:]), 0.0)
    shape = (LANES, ROWS)
    fold = jnp.where(lax.broadcasted_iota(I32, shape, 0) % ROWS == lanes(shape), 1.0, 0.0)
    spread_ref[...] = jnp.dot(
        row, fold, precision=lax.Precision.HIGHEST, preferred_element_type=F32
    )
    low = lanes((CHUNK, LANES)) < TAIL
    for x in range(X):
        a, b = (got_ref[l * X + x, 0:BACK, :].astype(F32) for l in range(L))
        a, b = (
            [p[t * CHUNK : (t + 1) * CHUNK] for t in range(FULL)] + [last_tile(p[FULL * CHUNK :])]
            for p in (a, b)
        )
        b = [pltpu.roll(p, TAIL, 1) for p in b]
        tiles = a[:-1] + [jnp.where(low, p, r) for p, r in zip([a[-1]] + b[:-1], b)]
        block_ref[:, x * PAIR : (x + 1) * PAIR] = jnp.concatenate(tiles, axis=1).astype(BF)


def put_columns(half_ref, out_ref, core, sem):
    width = X * PAIR
    copy = pltpu.make_async_copy(
        half_ref, out_ref.at[:, pl.ds(pl.multiple_of(core * width, LANES), width)], sem
    )
    copy.start()
    return copy


def own_half_kernel(core_ref, half_ref, out_ref, sem):
    put_columns(half_ref, out_ref, core_ref[0], sem).wait()


def other_half_kernel(core_ref, half_ref, spread_ref, out_in_ref, out_ref, gate_ref, sem):
    copy = put_columns(half_ref, out_ref, 1 - core_ref[0], sem)
    for e in range(E):
        gate_ref[e : e + 1, :] = jnp.sum(spread_ref[e * M * N : (e + 1) * M * N, :], axis=0, keepdims=True)
    copy.wait()


VM, SM, HBM = (pl.BlockSpec(memory_space=m) for m in (pltpu.VMEM, pltpu.SMEM, pl.ANY))


def call(kernel, places, outs, *args, scratch=(), flops=0, vmem=32, out_places=None, aliases={}):
    outs = [jax.ShapeDtypeStruct(s, d) for s, d in outs]
    nbytes = sum(a.size * a.dtype.itemsize for a in list(args) + outs)
    return pl.pallas_call(
        kernel,
        out_shape=outs,
        in_specs=places,
        out_specs=out_places or [VM] * len(outs),
        input_output_aliases=aliases,
        scratch_shapes=scratch,
        cost_estimate=pl.CostEstimate(flops=flops, bytes_accessed=nbytes, transcendentals=0),
        compiler_params=pltpu.CompilerParams(vmem_limit_bytes=vmem * 1024 * 1024),
    )(*args)


def on_device(grad_values, grad_scales, hidden_act, down_weight, slot_token, slot_count, slot_gate):
    low, core, owner = (lax.axis_index(a) for a in "lce")
    hidden, tok, gate = hidden_act[0], slot_token[0], slot_gate[0]
    where = owner[None].astype(I32)

    (both,) = call(
        first_kernel,
        [SM, SM, VM, VM, VM, VM, VM],
        [((FLAT + PACK, LANES), BF)],
        where, slot_count, tok, gate, hidden, grad_values, grad_scales.reshape(1, ROWS),
        vmem=60,
    )
    both = lax.all_gather(both, "c", axis=0)

    (send,) = call(
        tokens_kernel,
        [SM, VM],
        [((L * N * X, C * ROWS, WIDE), BF)],
        core[None].astype(I32), both,
    )
    mine = lax.all_to_all(send, ("l", "n", "x"), 0, 0)

    width = X * PAIR
    w_part = lax.dynamic_slice(down_weight, (low * SHARE, core * width), (SHARE, width))
    (pack,) = call(send_kernel, [VM, VM], [((L * X, C * PACK + W_PART, LANES), BF)], both, w_part)
    pack, mine = lax.optimization_barrier((pack, mine))
    pack = lax.all_to_all(pack, ("l", "x"), 0, 0)
    (mine,) = call(
        dense_kernel, [VM], [((QUARTERS, DENSE, LANES), BF)], mine
    )
    mine = lax.all_gather(mine, ("e", "m"), axis=0)

    part, keep, other = call(
        weight_kernel,
        [SM, VM, VM],
        [((H, X, BACK, LANES), BF), ((L * X, PACK, LANES), BF), ((L * X, PACK, LANES), BF)],
        core[None].astype(I32), mine, pack,
        scratch=[pltpu.VMEM((QUARTERS * SLOTS, WIDE), BF)],
        flops=2 * QUARTERS * SLOTS * (COLS * GROUP + 2 * WIDE * X * UNITS),
    )
    other = lax.ppermute(other, "c", [(i, C - 1 - i) for i in range(C)])
    sums = lax.all_to_all(part, "h", 0, 0)

    (send,) = call(
        back_kernel,
        [VM, VM, VM],
        [((L * X, BACK + PACK, LANES), BF)],
        sums, keep, other,
    )
    got = lax.all_to_all(send, ("l", "x"), 0, 0)
    hidden_grad, spread, block = call(
        finish_kernel,
        [SM, VM, VM],
        [((SLOTS, UNITS), BF), ((E * M * N, ROWS), F32), ((CHUNK, X * PAIR), BF)],
        where, gate, got,
    )
    spread = lax.all_to_all(spread, ("e", "m", "n"), 0, 0, tiled=True)

    block = lax.all_gather(block, "h", axis=0, tiled=True)
    block, spread = lax.optimization_barrier((block, spread))
    other = lax.ppermute(block, "c", [(i, C - 1 - i) for i in range(C)])
    where = core[None].astype(I32)
    sem = [pltpu.SemaphoreType.DMA(())]
    (whole,) = call(
        own_half_kernel, [SM, VM], [((UNITS, WIDTH), BF)], where, block, scratch=sem, out_places=[HBM]
    )
    weight_grad, gate_grad = call(
        other_half_kernel,
        [SM, HBM, VM, HBM],
        [((UNITS, WIDTH), BF), ((E, ROWS), F32)],
        where, other, spread, whole,
        scratch=sem,
        out_places=[HBM, VM],
        aliases={3: 0},
    )
    return hidden_grad[None], weight_grad, gate_grad.T


def solution(mesh):
    fine = jax.sharding.Mesh(mesh.devices.reshape(SIZES), DP + EXPERT)
    return jax.shard_map(
        on_device,
        mesh=fine,
        in_specs=(
            P(DP + EXPERT, None),
            P(DP + EXPERT),
            P(DP, None, EXPERT),
            P(EXPERT, None),
            P(DP, None, None),
            P(DP, None),
            P(DP, None, None),
        ),
        out_specs=(P(DP, None, EXPERT), P(EXPERT, None), P(DP + EXPERT, None)),
        check_vma=False,
    )
```

```python
import jax
import jax.numpy as jnp
from jax import lax
from jax.experimental import pallas as pl
from jax.experimental.pallas import tpu as pltpu
from jax.sharding import PartitionSpec as P

BF, F32, I32 = jnp.bfloat16, jnp.float32, jnp.int32
DP, EXPERT = ("h", "l", "c"), ("e", "m", "n", "x")
H, L, C, E, M, N, X = SIZES = (4, 2, 2, 2, 2, 2, 4)
QUARTERS, PARTS = L * C, L * C * X
LANES, TILES = 128, 4
WIDTH, SLOTS, UNITS, ROWS = 7168, 128, 128, 8
GROUP = E * M * N * X * ROWS
COLS, WIDE = WIDTH // PARTS, TILES * LANES
PAIR = 2 * COLS
SHARE = UNITS // L
CHUNK = UNITS // H
EXTRA = 16
PACK = SLOTS + EXTRA
FULL, TAIL = TILES - 1, COLS % LANES
TOKS = N * X * ROWS
BACK = FULL * CHUNK + CHUNK // 2
W_PART = FULL * SHARE + SHARE // 2
DENSE = FULL * TOKS + TOKS // 2
OWNED = E * M * N * ROWS


def lanes(shape):
    return lax.broadcasted_iota(I32, shape, len(shape) - 1)


def column(row):
    n = row.shape[1]
    across, down = lanes((n, n)), lax.broadcasted_iota(I32, (n, n), 0)
    return jnp.sum(jnp.where(across == down, row, jnp.zeros_like(row)), axis=1, keepdims=True)


def slice_of(a, n, l):
    start = n * PAIR
    if l == 0:
        a = a[:, start : start + WIDE]
    else:
        a = pltpu.roll(a[:, start + PAIR - WIDE : start + PAIR], COLS, 1)
    return jnp.where(lanes(a.shape) < COLS, a, 0.0)


def dense(a):
    half = a.shape[0] // 2
    last = a[:, FULL * LANES :]
    last = last[:half] + pltpu.roll(last[half:], TAIL, 1)
    return jnp.concatenate([a[:, t * LANES : (t + 1) * LANES] for t in range(FULL)] + [last], axis=0)


def last_tile(a):
    return jnp.concatenate([a, pltpu.roll(a, TAIL, 1)], axis=0)


def tokens_kernel(values_ref, scales_ref, out_ref):
    scaled = values_ref[...].astype(F32) * column(scales_ref[...].astype(F32))
    for l in range(L):
        for n in range(C * X):
            part = slice_of(scaled, n, l).astype(BF)
            for i in range(N):
                out_ref[((l * C + n // X) * N + i) * X + n % X] = part


def own_slots(where_ref, tok_ref, count_ref):
    owner = where_ref[0]
    tok = jnp.where(owner == 0, tok_ref[0:1, :], tok_ref[1:2, :])
    return jnp.where(lanes((1, SLOTS)) < count_ref[0, owner], tok, GROUP)


def own_gate(where_ref, gate_ref):
    return column(jnp.where(where_ref[0] == 0, gate_ref[0:1, :], gate_ref[1:2, :]))


def split3(a):
    high = a.astype(BF)
    rest = a - high.astype(F32)
    mid = rest.astype(BF)
    return high.astype(F32), mid.astype(F32), rest - mid.astype(F32)


def stack_rows(rows):
    shape = (EXTRA, rows[0].shape[1])
    at, out = lax.broadcasted_iota(I32, shape, 0), jnp.zeros(shape, F32)
    for i, row in enumerate(rows):
        out = jnp.where(at == i, row, out)
    return out.astype(BF)


def pack_kernel(where_ref, count_ref, tok_ref, gate_ref, hidden_ref, out_ref):
    gate = jnp.where(where_ref[0] == 0, gate_ref[0:1, :], gate_ref[1:2, :])
    tok = own_slots(where_ref, tok_ref, count_ref).astype(F32)
    out_ref[0:SLOTS, :] = hidden_ref[...]
    out_ref[SLOTS:PACK, :] = stack_rows((tok,) + split3(gate))


def send_kernel(packs_ref, w_ref, out_ref):
    w = w_ref[...].astype(F32)
    for l in range(L):
        for x in range(X):
            out_ref[l * X + x, 0 : C * PACK, :] = packs_ref[...]
            out_ref[l * X + x, C * PACK :, :] = dense(slice_of(w, x, l)).astype(BF)


def dense_kernel(rows_ref, out_ref):
    for g in range(QUARTERS):
        out_ref[g] = dense(rows_ref[g].astype(F32)).astype(BF)


def weight_kernel(mine_ref, pack_ref, part_ref, routed_ref):
    ids = lax.broadcasted_iota(I32, (GROUP, SLOTS), 0)
    first = (((0,), (0,)), ((), ()))
    gates = []
    for g in range(QUARTERS):
        extra = pack_ref[g // C * X, g % C * PACK + SLOTS : (g % C + 1) * PACK, :].astype(F32)
        gates.append(column(extra[1:2] + extra[2:3] + extra[3:4]))
        picks = jnp.where(ids == extra[0:1].astype(I32), 1.0, 0.0).astype(BF)
        rows = [mine_ref[:, g, t * TOKS : (t + 1) * TOKS, :].reshape(GROUP, LANES) for t in range(FULL)]
        rows += [
            jnp.concatenate(
                [last_tile(mine_ref[i, g, FULL * TOKS :, :].astype(F32)).astype(BF) for i in range(E * M)],
                axis=0,
            )
        ]
        rows = jnp.concatenate(rows, axis=1)
        rows = lax.dot_general(picks, rows, first, preferred_element_type=F32)
        rows = jnp.where(lanes(rows.shape) < COLS, rows, 0.0)
        routed_ref[g * SLOTS : (g + 1) * SLOTS, :] = rows.astype(BF)
    routed = routed_ref[...]

    for x in range(X):
        weighted = [
            (gates[g] * pack_ref[g // C * X + x, pl.ds(g % C * PACK, SLOTS), :].astype(F32)).astype(BF)
            for g in range(QUARTERS)
        ]
        weighted = jnp.concatenate(weighted, axis=0)
        part = lax.dot_general(weighted, routed, first, preferred_element_type=F32)
        for h in range(H):
            part_ref[h, x] = dense(part[h * CHUNK : (h + 1) * CHUNK]).astype(BF)


def project_kernel(core_ref, routed_ref, pack_ref, keep_ref, send_ref):
    core = core_ref[0]
    groups = [(l, c) for c in (core, 1 - core) for l in range(L)]
    outs = [(ref, l) for ref in (keep_ref, send_ref) for l in range(L)]
    routed = jnp.concatenate(
        [routed_ref[pl.ds(pl.multiple_of((l * C + c) * SLOTS, SLOTS), SLOTS), :] for l, c in groups], axis=0
    )
    sums = [jnp.zeros((SLOTS, 1), F32)] * QUARTERS
    for x in range(X):
        w = []
        for l in range(L):
            rows = pack_ref[l * X + x, C * PACK :, :]
            rows = [rows[t * SHARE : (t + 1) * SHARE] for t in range(FULL)] + [
                last_tile(rows[FULL * SHARE :].astype(F32)).astype(BF)
            ]
            w.append(jnp.concatenate(rows, axis=1))
        w = jnp.concatenate(w, axis=0)
        proj = lax.dot_general(routed, w, (((1,), (1,)), ((), ())), preferred_element_type=F32)
        for i, (ref, l) in enumerate(outs):
            rows = proj[i * SLOTS : (i + 1) * SLOTS]
            ref[l * X + x, 0:SLOTS, :] = rows.astype(BF)
            at = pl.multiple_of(groups[i][1] * PACK, EXTRA)
            hidden = pack_ref[l * X + x, pl.ds(at, SLOTS), :].astype(F32)
            sums[i] = sums[i] + jnp.sum(hidden * rows, axis=1, keepdims=True)
    at = lanes((SLOTS, LANES))
    for i, (ref, l) in enumerate(outs):
        row = pl.multiple_of(groups[i][1] * PACK + SLOTS, EXTRA)
        tok = column(pack_ref[l * X, pl.ds(row, EXTRA), :].astype(F32)[0:1]).astype(I32)
        device, spot = tok // ROWS, tok % ROWS
        spot = jnp.where(tok < GROUP, device // X * ROWS + spot, LANES)
        for x in range(X):
            here = (at == spot) & (device % X == x)
            row = jnp.sum(jnp.where(here, sums[i], 0.0), axis=0, keepdims=True)
            ref[l * X + x, SLOTS:PACK, :] = terms(row)


def terms(row):
    high, mid, low = split3(row)
    return stack_rows((high + pltpu.roll(mid, OWNED, 1), low))


def row_of(tile):
    row = tile[0:1] + (pltpu.roll(tile[0:1], OWNED, 1) + tile[1:2])
    return jnp.where(lanes(row.shape) < OWNED, row, 0.0)


def back_kernel(sums_ref, keep_ref, other_ref, out_ref):
    for x in range(X):
        total = sums_ref[0, x].astype(F32)
        for h in range(1, H):
            total = total + sums_ref[h, x].astype(F32)
        for l in range(L):
            out_ref[l * X + x, 0:BACK, :] = total.astype(BF)
    for n in range(L * X):
        both = keep_ref[n].astype(F32) + other_ref[n].astype(F32)
        out_ref[n, BACK : BACK + SLOTS, :] = both[:SLOTS].astype(BF)
        out_ref[n, BACK + SLOTS :, :] = terms(row_of(both[SLOTS:]))


def finish_kernel(where_ref, gate_ref, got_ref, grad_ref, spread_ref, block_ref):
    both = got_ref[0, BACK:, :].astype(F32)
    for n in range(1, L * X):
        both = both + got_ref[n, BACK:, :].astype(F32)
    grad_ref[...] = (own_gate(where_ref, gate_ref) * both[:SLOTS]).astype(BF)
    shape = (E * M * N, LANES)
    row = jnp.where(lanes(shape) // ROWS == lax.broadcasted_iota(I32, shape, 0), row_of(both[SLOTS:]), 0.0)
    shape = (LANES, ROWS)
    fold = jnp.where(lax.broadcasted_iota(I32, shape, 0) % ROWS == lanes(shape), 1.0, 0.0)
    spread_ref[...] = jnp.dot(
        row, fold, precision=lax.Precision.HIGHEST, preferred_element_type=F32
    )
    low = lanes((CHUNK, LANES)) < TAIL
    for x in range(X):
        a, b = (got_ref[l * X + x, 0:BACK, :].astype(F32) for l in range(L))
        a, b = (
            [p[t * CHUNK : (t + 1) * CHUNK] for t in range(FULL)] + [last_tile(p[FULL * CHUNK :])]
            for p in (a, b)
        )
        b = [pltpu.roll(p, TAIL, 1) for p in b]
        tiles = a[:-1] + [jnp.where(low, p, r) for p, r in zip([a[-1]] + b[:-1], b)]
        block_ref[:, x * PAIR : (x + 1) * PAIR] = jnp.concatenate(tiles, axis=1).astype(BF)


def put_columns(half_ref, out_ref, core, sem):
    width = X * PAIR
    copy = pltpu.make_async_copy(
        half_ref, out_ref.at[:, pl.ds(pl.multiple_of(core * width, LANES), width)], sem
    )
    copy.start()
    return copy


def own_half_kernel(core_ref, half_ref, out_ref, sem):
    put_columns(half_ref, out_ref, core_ref[0], sem).wait()


def other_half_kernel(core_ref, half_ref, spread_ref, out_in_ref, out_ref, gate_ref, sem):
    copy = put_columns(half_ref, out_ref, 1 - core_ref[0], sem)
    for e in range(E):
        gate_ref[e : e + 1, :] = jnp.sum(spread_ref[e * M * N : (e + 1) * M * N, :], axis=0, keepdims=True)
    copy.wait()


VM, SM, HBM = (pl.BlockSpec(memory_space=m) for m in (pltpu.VMEM, pltpu.SMEM, pl.ANY))


def call(kernel, places, outs, *args, scratch=(), flops=0, vmem=32, out_places=None, aliases={}):
    outs = [jax.ShapeDtypeStruct(s, d) for s, d in outs]
    nbytes = sum(a.size * a.dtype.itemsize for a in list(args) + outs)
    return pl.pallas_call(
        kernel,
        out_shape=outs,
        in_specs=places,
        out_specs=out_places or [VM] * len(outs),
        input_output_aliases=aliases,
        scratch_shapes=scratch,
        cost_estimate=pl.CostEstimate(flops=flops, bytes_accessed=nbytes, transcendentals=0),
        compiler_params=pltpu.CompilerParams(vmem_limit_bytes=vmem * 1024 * 1024),
    )(*args)


def on_device(grad_values, grad_scales, hidden_act, down_weight, slot_token, slot_count, slot_gate):
    low, core, owner = (lax.axis_index(a) for a in "lce")
    hidden, tok, gate = hidden_act[0], slot_token[0], slot_gate[0]
    where = owner[None].astype(I32)

    (send,) = call(
        tokens_kernel,
        [VM, VM],
        [((N * PARTS, ROWS, WIDE), BF)],
        grad_values, grad_scales.reshape(1, ROWS),
        vmem=60,
    )
    mine = lax.all_to_all(send, ("l", "c", "n", "x"), 0, 0)

    (pack,) = call(
        pack_kernel,
        [SM, SM, VM, VM, VM],
        [((PACK, LANES), BF)],
        where, slot_count, tok, gate, hidden,
    )
    packs = lax.all_gather(pack, "c", axis=0, tiled=True)
    width = X * PAIR
    w_part = lax.dynamic_slice(down_weight, (low * SHARE, core * width), (SHARE, width))
    (pack,) = call(send_kernel, [VM, VM], [((L * X, C * PACK + W_PART, LANES), BF)], packs, w_part)
    pack, mine = lax.optimization_barrier((pack, mine))
    pack = lax.all_to_all(pack, ("l", "x"), 0, 0)
    (mine,) = call(
        dense_kernel, [VM], [((QUARTERS, DENSE, LANES), BF)], mine.reshape(QUARTERS, TOKS, WIDE)
    )
    mine = lax.all_gather(mine, ("e", "m"), axis=0)

    part, routed = call(
        weight_kernel,
        [VM, VM],
        [((H, X, BACK, LANES), BF), ((QUARTERS * SLOTS, WIDE), BF)],
        mine, pack,
        flops=2 * QUARTERS * SLOTS * WIDE * (GROUP + X * UNITS),
    )
    keep, other = call(
        project_kernel,
        [SM, VM, VM],
        [((L * X, PACK, LANES), BF), ((L * X, PACK, LANES), BF)],
        core[None].astype(I32), routed, pack,
        flops=2 * QUARTERS * SLOTS * WIDE * X * UNITS,
    )
    other = lax.ppermute(other, "c", [(i, C - 1 - i) for i in range(C)])
    sums = lax.all_to_all(part, "h", 0, 0)

    (send,) = call(
        back_kernel,
        [VM, VM, VM],
        [((L * X, BACK + PACK, LANES), BF)],
        sums, keep, other,
    )
    got = lax.all_to_all(send, ("l", "x"), 0, 0)
    hidden_grad, spread, block = call(
        finish_kernel,
        [SM, VM, VM],
        [((SLOTS, UNITS), BF), ((E * M * N, ROWS), F32), ((CHUNK, X * PAIR), BF)],
        where, gate, got,
    )
    spread = lax.all_to_all(spread, ("e", "m", "n"), 0, 0, tiled=True)

    block = lax.all_gather(block, "h", axis=0, tiled=True)
    block, spread = lax.optimization_barrier((block, spread))
    other = lax.ppermute(block, "c", [(i, C - 1 - i) for i in range(C)])
    where = core[None].astype(I32)
    sem = [pltpu.SemaphoreType.DMA(())]
    (whole,) = call(
        own_half_kernel, [SM, VM], [((UNITS, WIDTH), BF)], where, block, scratch=sem, out_places=[HBM]
    )
    weight_grad, gate_grad = call(
        other_half_kernel,
        [SM, HBM, VM, HBM],
        [((UNITS, WIDTH), BF), ((E, ROWS), F32)],
        where, other, spread, whole,
        scratch=sem,
        out_places=[HBM, VM],
        aliases={3: 0},
    )
    return hidden_grad[None], weight_grad, gate_grad.T


def solution(mesh):
    fine = jax.sharding.Mesh(mesh.devices.reshape(SIZES), DP + EXPERT)
    return jax.shard_map(
        on_device,
        mesh=fine,
        in_specs=(
            P(DP + EXPERT, None),
            P(DP + EXPERT),
            P(DP, None, EXPERT),
            P(EXPERT, None),
            P(DP, None, None),
            P(DP, None),
            P(DP, None, None),
        ),
        out_specs=(P(DP, None, EXPERT), P(EXPERT, None), P(DP + EXPERT, None)),
        check_vma=False,
    )
```

```python
import jax
import jax.numpy as jnp
from jax import lax
from jax.experimental import pallas as pl
from jax.experimental.pallas import tpu as pltpu
from jax.sharding import PartitionSpec as P

BF, F32, I32 = jnp.bfloat16, jnp.float32, jnp.int32
DP, EXPERT = ("h", "l", "c"), ("e", "m", "n", "x")
H, L, C, E, M, N, X = SIZES = (4, 2, 2, 2, 2, 2, 4)
QUARTERS, PARTS = L * C, L * C * X
LANES, TILES = 128, 4
WIDTH, SLOTS, UNITS, ROWS = 7168, 128, 128, 8
GROUP = E * M * N * X * ROWS
COLS, WIDE = WIDTH // PARTS, TILES * LANES
PAIR = 2 * COLS
SHARE = UNITS // L
CHUNK = UNITS // H
EXTRA = 16
PACK = SLOTS + EXTRA
FULL, TAIL = TILES - 1, COLS % LANES
TOKS = N * X * ROWS
BACK = FULL * CHUNK + CHUNK // 2
W_PART = FULL * SHARE + SHARE // 2
DENSE = FULL * TOKS + TOKS // 2
FLAT = ROWS * WIDTH // LANES
OWNED = E * M * N * ROWS


def lanes(shape):
    return lax.broadcasted_iota(I32, shape, len(shape) - 1)


def column(row):
    n = row.shape[1]
    across, down = lanes((n, n)), lax.broadcasted_iota(I32, (n, n), 0)
    return jnp.sum(jnp.where(across == down, row, jnp.zeros_like(row)), axis=1, keepdims=True)


def slice_of(a, n, l):
    start = n * PAIR
    if l == 0:
        a = a[:, start : start + WIDE]
    else:
        a = pltpu.roll(a[:, start + PAIR - WIDE : start + PAIR], COLS, 1)
    return jnp.where(lanes(a.shape) < COLS, a, 0.0)


def dense(a):
    half = a.shape[0] // 2
    last = a[:, FULL * LANES :]
    last = last[:half] + pltpu.roll(last[half:], TAIL, 1)
    return jnp.concatenate([a[:, t * LANES : (t + 1) * LANES] for t in range(FULL)] + [last], axis=0)


def last_tile(a):
    return jnp.concatenate([a, pltpu.roll(a, TAIL, 1)], axis=0)


def own_slots(where_ref, tok_ref, count_ref):
    owner = where_ref[0]
    tok = jnp.where(owner == 0, tok_ref[0:1, :], tok_ref[1:2, :])
    return jnp.where(lanes((1, SLOTS)) < count_ref[0, owner], tok, GROUP)


def own_gate(where_ref, gate_ref):
    return column(jnp.where(where_ref[0] == 0, gate_ref[0:1, :], gate_ref[1:2, :]))


def split3(a):
    high = a.astype(BF)
    rest = a - high.astype(F32)
    mid = rest.astype(BF)
    return high.astype(F32), mid.astype(F32), rest - mid.astype(F32)


def stack_rows(rows):
    shape = (EXTRA, rows[0].shape[1])
    at, out = lax.broadcasted_iota(I32, shape, 0), jnp.zeros(shape, F32)
    for i, row in enumerate(rows):
        out = jnp.where(at == i, row, out)
    return out.astype(BF)


def first_kernel(where_ref, count_ref, tok_ref, gate_ref, hidden_ref, values_ref, scales_ref, out_ref):
    scaled = values_ref[...].astype(F32) * column(scales_ref[...].astype(F32))
    for t in range(0, WIDTH // LANES, 2):
        two = [scaled[:, i * LANES : (i + 1) * LANES] for i in (t, t + 1)]
        out_ref[t * ROWS : (t + 2) * ROWS, :] = jnp.concatenate(two, axis=0).astype(BF)
    gate = jnp.where(where_ref[0] == 0, gate_ref[0:1, :], gate_ref[1:2, :])
    tok = own_slots(where_ref, tok_ref, count_ref).astype(F32)
    out_ref[FLAT : FLAT + SLOTS, :] = hidden_ref[...]
    out_ref[FLAT + SLOTS :, :] = stack_rows((tok,) + split3(gate))


def tokens_kernel(core_ref, both_ref, out_ref):
    half = FLAT // C
    rows = []
    for c in range(C):
        a = both_ref[c, pl.ds(pl.multiple_of(core_ref[0] * half, EXTRA), half), :].astype(F32)
        rows.append(jnp.concatenate([a[i : i + ROWS] for i in range(0, half, ROWS)], axis=1))
    rows = jnp.concatenate(rows, axis=0)
    for l in range(L):
        for x in range(X):
            part = slice_of(rows, x, l).astype(BF)
            for i in range(N):
                out_ref[(l * N + i) * X + x] = part


def send_kernel(both_ref, w_ref, out_ref):
    w = w_ref[...].astype(F32)
    for l in range(L):
        for x in range(X):
            for c in range(C):
                out_ref[l * X + x, c * PACK : (c + 1) * PACK, :] = both_ref[c, FLAT:, :]
            out_ref[l * X + x, C * PACK :, :] = dense(slice_of(w, x, l)).astype(BF)


def dense_kernel(rows_ref, out_ref):
    for l in range(L):
        rows = [rows_ref[l * N * X + i].astype(F32) for i in range(N * X)]
        for c in range(C):
            part = jnp.concatenate([a[c * ROWS : (c + 1) * ROWS] for a in rows], axis=0)
            out_ref[l * C + c] = dense(part).astype(BF)


def weight_kernel(mine_ref, pack_ref, part_ref, routed_ref):
    ids = lax.broadcasted_iota(I32, (GROUP, SLOTS), 0)
    first = (((0,), (0,)), ((), ()))
    gates = []
    for g in range(QUARTERS):
        extra = pack_ref[g // C * X, g % C * PACK + SLOTS : (g % C + 1) * PACK, :].astype(F32)
        gates.append(column(extra[1:2] + extra[2:3] + extra[3:4]))
        picks = jnp.where(ids == extra[0:1].astype(I32), 1.0, 0.0).astype(BF)
        rows = [mine_ref[:, g, t * TOKS : (t + 1) * TOKS, :].reshape(GROUP, LANES) for t in range(FULL)]
        rows += [
            jnp.concatenate(
                [last_tile(mine_ref[i, g, FULL * TOKS :, :].astype(F32)).astype(BF) for i in range(E * M)],
                axis=0,
            )
        ]
        rows = jnp.concatenate(rows, axis=1)
        rows = lax.dot_general(picks, rows, first, preferred_element_type=F32)
        rows = jnp.where(lanes(rows.shape) < COLS, rows, 0.0)
        routed_ref[g * SLOTS : (g + 1) * SLOTS, :] = rows.astype(BF)
    routed = routed_ref[...]

    for x in range(X):
        weighted = [
            (gates[g] * pack_ref[g // C * X + x, pl.ds(g % C * PACK, SLOTS), :].astype(F32)).astype(BF)
            for g in range(QUARTERS)
        ]
        weighted = jnp.concatenate(weighted, axis=0)
        part = lax.dot_general(weighted, routed, first, preferred_element_type=F32)
        for h in range(H):
            part_ref[h, x] = dense(part[h * CHUNK : (h + 1) * CHUNK]).astype(BF)


def project_kernel(core_ref, routed_ref, pack_ref, keep_ref, send_ref):
    core = core_ref[0]
    groups = [(l, c) for c in (core, 1 - core) for l in range(L)]
    outs = [(ref, l) for ref in (keep_ref, send_ref) for l in range(L)]
    routed = jnp.concatenate(
        [routed_ref[pl.ds(pl.multiple_of((l * C + c) * SLOTS, SLOTS), SLOTS), :] for l, c in groups], axis=0
    )
    sums = [jnp.zeros((SLOTS, 1), F32)] * QUARTERS
    for x in range(X):
        w = []
        for l in range(L):
            rows = pack_ref[l * X + x, C * PACK :, :]
            rows = [rows[t * SHARE : (t + 1) * SHARE] for t in range(FULL)] + [
                last_tile(rows[FULL * SHARE :].astype(F32)).astype(BF)
            ]
            w.append(jnp.concatenate(rows, axis=1))
        w = jnp.concatenate(w, axis=0)
        proj = lax.dot_general(routed, w, (((1,), (1,)), ((), ())), preferred_element_type=F32)
        for i, (ref, l) in enumerate(outs):
            rows = proj[i * SLOTS : (i + 1) * SLOTS]
            ref[l * X + x, 0:SLOTS, :] = rows.astype(BF)
            at = pl.multiple_of(groups[i][1] * PACK, EXTRA)
            hidden = pack_ref[l * X + x, pl.ds(at, SLOTS), :].astype(F32)
            sums[i] = sums[i] + jnp.sum(hidden * rows, axis=1, keepdims=True)
    at = lanes((SLOTS, LANES))
    for i, (ref, l) in enumerate(outs):
        row = pl.multiple_of(groups[i][1] * PACK + SLOTS, EXTRA)
        tok = column(pack_ref[l * X, pl.ds(row, EXTRA), :].astype(F32)[0:1]).astype(I32)
        device, spot = tok // ROWS, tok % ROWS
        spot = jnp.where(tok < GROUP, device // X * ROWS + spot, LANES)
        for x in range(X):
            here = (at == spot) & (device % X == x)
            row = jnp.sum(jnp.where(here, sums[i], 0.0), axis=0, keepdims=True)
            ref[l * X + x, SLOTS:PACK, :] = terms(row)


def terms(row):
    high, mid, low = split3(row)
    return stack_rows((high + pltpu.roll(mid, OWNED, 1), low))


def row_of(tile):
    row = tile[0:1] + (pltpu.roll(tile[0:1], OWNED, 1) + tile[1:2])
    return jnp.where(lanes(row.shape) < OWNED, row, 0.0)


def back_kernel(sums_ref, keep_ref, other_ref, out_ref):
    for x in range(X):
        total = sums_ref[0, x].astype(F32)
        for h in range(1, H):
            total = total + sums_ref[h, x].astype(F32)
        for l in range(L):
            out_ref[l * X + x, 0:BACK, :] = total.astype(BF)
    for n in range(L * X):
        both = keep_ref[n].astype(F32) + other_ref[n].astype(F32)
        out_ref[n, BACK : BACK + SLOTS, :] = both[:SLOTS].astype(BF)
        out_ref[n, BACK + SLOTS :, :] = terms(row_of(both[SLOTS:]))


def finish_kernel(where_ref, gate_ref, got_ref, grad_ref, spread_ref, block_ref):
    both = got_ref[0, BACK:, :].astype(F32)
    for n in range(1, L * X):
        both = both + got_ref[n, BACK:, :].astype(F32)
    grad_ref[...] = (own_gate(where_ref, gate_ref) * both[:SLOTS]).astype(BF)
    shape = (E * M * N, LANES)
    row = jnp.where(lanes(shape) // ROWS == lax.broadcasted_iota(I32, shape, 0), row_of(both[SLOTS:]), 0.0)
    shape = (LANES, ROWS)
    fold = jnp.where(lax.broadcasted_iota(I32, shape, 0) % ROWS == lanes(shape), 1.0, 0.0)
    spread_ref[...] = jnp.dot(
        row, fold, precision=lax.Precision.HIGHEST, preferred_element_type=F32
    )
    low = lanes((CHUNK, LANES)) < TAIL
    for x in range(X):
        a, b = (got_ref[l * X + x, 0:BACK, :].astype(F32) for l in range(L))
        a, b = (
            [p[t * CHUNK : (t + 1) * CHUNK] for t in range(FULL)] + [last_tile(p[FULL * CHUNK :])]
            for p in (a, b)
        )
        b = [pltpu.roll(p, TAIL, 1) for p in b]
        tiles = a[:-1] + [jnp.where(low, p, r) for p, r in zip([a[-1]] + b[:-1], b)]
        block_ref[:, x * PAIR : (x + 1) * PAIR] = jnp.concatenate(tiles, axis=1).astype(BF)


def put_columns(half_ref, out_ref, core, sem):
    width = X * PAIR
    copy = pltpu.make_async_copy(
        half_ref, out_ref.at[:, pl.ds(pl.multiple_of(core * width, LANES), width)], sem
    )
    copy.start()
    return copy


def own_half_kernel(core_ref, half_ref, out_ref, sem):
    put_columns(half_ref, out_ref, core_ref[0], sem).wait()


def other_half_kernel(core_ref, half_ref, spread_ref, out_in_ref, out_ref, gate_ref, sem):
    copy = put_columns(half_ref, out_ref, 1 - core_ref[0], sem)
    for e in range(E):
        gate_ref[e : e + 1, :] = jnp.sum(spread_ref[e * M * N : (e + 1) * M * N, :], axis=0, keepdims=True)
    copy.wait()


VM, SM, HBM = (pl.BlockSpec(memory_space=m) for m in (pltpu.VMEM, pltpu.SMEM, pl.ANY))


def call(kernel, places, outs, *args, scratch=(), flops=0, vmem=32, out_places=None, aliases={}):
    outs = [jax.ShapeDtypeStruct(s, d) for s, d in outs]
    nbytes = sum(a.size * a.dtype.itemsize for a in list(args) + outs)
    return pl.pallas_call(
        kernel,
        out_shape=outs,
        in_specs=places,
        out_specs=out_places or [VM] * len(outs),
        input_output_aliases=aliases,
        scratch_shapes=scratch,
        cost_estimate=pl.CostEstimate(flops=flops, bytes_accessed=nbytes, transcendentals=0),
        compiler_params=pltpu.CompilerParams(vmem_limit_bytes=vmem * 1024 * 1024),
    )(*args)


def on_device(grad_values, grad_scales, hidden_act, down_weight, slot_token, slot_count, slot_gate):
    low, core, owner = (lax.axis_index(a) for a in "lce")
    hidden, tok, gate = hidden_act[0], slot_token[0], slot_gate[0]
    where = owner[None].astype(I32)

    (both,) = call(
        first_kernel,
        [SM, SM, VM, VM, VM, VM, VM],
        [((FLAT + PACK, LANES), BF)],
        where, slot_count, tok, gate, hidden, grad_values, grad_scales.reshape(1, ROWS),
        vmem=60,
    )
    both = lax.all_gather(both, "c", axis=0)

    (send,) = call(
        tokens_kernel,
        [SM, VM],
        [((L * N * X, C * ROWS, WIDE), BF)],
        core[None].astype(I32), both,
    )
    mine = lax.all_to_all(send, ("l", "n", "x"), 0, 0)

    width = X * PAIR
    w_part = lax.dynamic_slice(down_weight, (low * SHARE, core * width), (SHARE, width))
    (pack,) = call(send_kernel, [VM, VM], [((L * X, C * PACK + W_PART, LANES), BF)], both, w_part)
    pack, mine = lax.optimization_barrier((pack, mine))
    pack = lax.all_to_all(pack, ("l", "x"), 0, 0)
    (mine,) = call(
        dense_kernel, [VM], [((QUARTERS, DENSE, LANES), BF)], mine
    )
    mine = lax.all_gather(mine, ("e", "m"), axis=0)

    part, routed = call(
        weight_kernel,
        [VM, VM],
        [((H, X, BACK, LANES), BF), ((QUARTERS * SLOTS, WIDE), BF)],
        mine, pack,
        flops=2 * QUARTERS * SLOTS * WIDE * (GROUP + X * UNITS),
    )
    keep, other = call(
        project_kernel,
        [SM, VM, VM],
        [((L * X, PACK, LANES), BF), ((L * X, PACK, LANES), BF)],
        core[None].astype(I32), routed, pack,
        flops=2 * QUARTERS * SLOTS * WIDE * X * UNITS,
    )
    other = lax.ppermute(other, "c", [(i, C - 1 - i) for i in range(C)])
    sums = lax.all_to_all(part, "h", 0, 0)

    (send,) = call(
        back_kernel,
        [VM, VM, VM],
        [((L * X, BACK + PACK, LANES), BF)],
        sums, keep, other,
    )
    got = lax.all_to_all(send, ("l", "x"), 0, 0)
    hidden_grad, spread, block = call(
        finish_kernel,
        [SM, VM, VM],
        [((SLOTS, UNITS), BF), ((E * M * N, ROWS), F32), ((CHUNK, X * PAIR), BF)],
        where, gate, got,
    )
    spread = lax.all_to_all(spread, ("e", "m", "n"), 0, 0, tiled=True)

    block = lax.all_gather(block, "h", axis=0, tiled=True)
    block, spread = lax.optimization_barrier((block, spread))
    other = lax.ppermute(block, "c", [(i, C - 1 - i) for i in range(C)])
    where = core[None].astype(I32)
    sem = [pltpu.SemaphoreType.DMA(())]
    (whole,) = call(
        own_half_kernel, [SM, VM], [((UNITS, WIDTH), BF)], where, block, scratch=sem, out_places=[HBM]
    )
    weight_grad, gate_grad = call(
        other_half_kernel,
        [SM, HBM, VM, HBM],
        [((UNITS, WIDTH), BF), ((E, ROWS), F32)],
        where, other, spread, whole,
        scratch=sem,
        out_places=[HBM, VM],
        aliases={3: 0},
    )
    return hidden_grad[None], weight_grad, gate_grad.T


def solution(mesh):
    fine = jax.sharding.Mesh(mesh.devices.reshape(SIZES), DP + EXPERT)
    return jax.shard_map(
        on_device,
        mesh=fine,
        in_specs=(
            P(DP + EXPERT, None),
            P(DP + EXPERT),
            P(DP, None, EXPERT),
            P(EXPERT, None),
            P(DP, None, None),
            P(DP, None),
            P(DP, None, None),
        ),
        out_specs=(P(DP, None, EXPERT), P(EXPERT, None), P(DP + EXPERT, None)),
        check_vma=False,
    )
```

```python
import jax
import jax.numpy as jnp
from jax import lax
from jax.experimental import pallas as pl
from jax.experimental.pallas import tpu as pltpu
from jax.sharding import PartitionSpec as P

BF, F32, I32 = jnp.bfloat16, jnp.float32, jnp.int32
DP, EXPERT = ("h", "l", "c"), ("e", "m", "n", "x")
H, L, C, E, M, N, X = SIZES = (4, 2, 2, 2, 2, 2, 4)
QUARTERS, PARTS = L * C, L * C * X
LANES, TILES = 128, 4
WIDTH, SLOTS, UNITS, ROWS = 7168, 128, 128, 8
GROUP = E * M * N * X * ROWS
COLS, WIDE = WIDTH // PARTS, TILES * LANES
PAIR = 2 * COLS
SHARE = UNITS // L
CHUNK = UNITS // H
EXTRA = 16
PACK = SLOTS + EXTRA
FULL, TAIL = TILES - 1, COLS % LANES
TOKS = N * X * ROWS
BACK = FULL * CHUNK + CHUNK // 2
W_PART = FULL * SHARE + SHARE // 2
DENSE = FULL * TOKS + TOKS // 2
FLAT = ROWS * WIDTH // LANES
OWNED = E * M * N * ROWS


def lanes(shape):
    return lax.broadcasted_iota(I32, shape, len(shape) - 1)


def column(row):
    n = row.shape[1]
    across, down = lanes((n, n)), lax.broadcasted_iota(I32, (n, n), 0)
    return jnp.sum(jnp.where(across == down, row, jnp.zeros_like(row)), axis=1, keepdims=True)


def slice_of(a, n, l):
    start = n * PAIR
    if l == 0:
        a = a[:, start : start + WIDE]
    else:
        a = pltpu.roll(a[:, start + PAIR - WIDE : start + PAIR], COLS, 1)
    return jnp.where(lanes(a.shape) < COLS, a, 0.0)


def dense(a):
    half = a.shape[0] // 2
    last = a[:, FULL * LANES :]
    last = last[:half] + pltpu.roll(last[half:], TAIL, 1)
    return jnp.concatenate([a[:, t * LANES : (t + 1) * LANES] for t in range(FULL)] + [last], axis=0)


def last_tile(a):
    return jnp.concatenate([a, pltpu.roll(a, TAIL, 1)], axis=0)


def own_slots(where_ref, tok_ref, count_ref):
    owner = where_ref[0]
    tok = jnp.where(owner == 0, tok_ref[0:1, :], tok_ref[1:2, :])
    return jnp.where(lanes((1, SLOTS)) < count_ref[0, owner], tok, GROUP)


def own_gate(where_ref, gate_ref):
    return column(jnp.where(where_ref[0] == 0, gate_ref[0:1, :], gate_ref[1:2, :]))


def split3(a):
    high = a.astype(BF)
    rest = a - high.astype(F32)
    mid = rest.astype(BF)
    return high.astype(F32), mid.astype(F32), rest - mid.astype(F32)


def stack_rows(rows):
    shape = (EXTRA, rows[0].shape[1])
    at, out = lax.broadcasted_iota(I32, shape, 0), jnp.zeros(shape, F32)
    for i, row in enumerate(rows):
        out = jnp.where(at == i, row, out)
    return out.astype(BF)


def first_kernel(where_ref, count_ref, tok_ref, gate_ref, hidden_ref, values_ref, scales_ref, out_ref):
    scaled = values_ref[...].astype(F32) * column(scales_ref[...].astype(F32))
    for t in range(0, WIDTH // LANES, 2):
        two = [scaled[:, i * LANES : (i + 1) * LANES] for i in (t, t + 1)]
        out_ref[t * ROWS : (t + 2) * ROWS, :] = jnp.concatenate(two, axis=0).astype(BF)
    gate = jnp.where(where_ref[0] == 0, gate_ref[0:1, :], gate_ref[1:2, :])
    tok = own_slots(where_ref, tok_ref, count_ref).astype(F32)
    out_ref[FLAT : FLAT + SLOTS, :] = hidden_ref[...]
    out_ref[FLAT + SLOTS :, :] = stack_rows((tok,) + split3(gate))


def tokens_kernel(core_ref, both_ref, out_ref):
    half = FLAT // C
    rows = []
    for c in range(C):
        a = both_ref[c, pl.ds(pl.multiple_of(core_ref[0] * half, EXTRA), half), :].astype(F32)
        rows.append(jnp.concatenate([a[i : i + ROWS] for i in range(0, half, ROWS)], axis=1))
    rows = jnp.concatenate(rows, axis=0)
    for l in range(L):
        for x in range(X):
            part = slice_of(rows, x, l).astype(BF)
            for i in range(N):
                out_ref[(l * N + i) * X + x] = part


def send_kernel(both_ref, w_ref, out_ref):
    w = w_ref[...].astype(F32)
    for l in range(L):
        for x in range(X):
            for c in range(C):
                out_ref[l * X + x, c * PACK : (c + 1) * PACK, :] = both_ref[c, FLAT:, :]
            out_ref[l * X + x, C * PACK :, :] = dense(slice_of(w, x, l)).astype(BF)


def dense_kernel(rows_ref, out_ref):
    for l in range(L):
        rows = [rows_ref[l * N * X + i].astype(F32) for i in range(N * X)]
        for c in range(C):
            part = jnp.concatenate([a[c * ROWS : (c + 1) * ROWS] for a in rows], axis=0)
            out_ref[l * C + c] = dense(part).astype(BF)


def weight_kernel(mine_ref, pack_ref, part_ref, routed_ref):
    ids = lax.broadcasted_iota(I32, (GROUP, SLOTS), 0)
    first = (((0,), (0,)), ((), ()))
    gates = []
    for g in range(QUARTERS):
        extra = pack_ref[g // C * X, g % C * PACK + SLOTS : (g % C + 1) * PACK, :].astype(F32)
        gates.append(column(extra[1:2] + extra[2:3] + extra[3:4]))
        picks = jnp.where(ids == extra[0:1].astype(I32), 1.0, 0.0).astype(BF)
        rows = [mine_ref[:, g, t * TOKS : (t + 1) * TOKS, :].reshape(GROUP, LANES) for t in range(FULL)]
        rows += [
            jnp.concatenate(
                [last_tile(mine_ref[i, g, FULL * TOKS :, :].astype(F32)).astype(BF) for i in range(E * M)],
                axis=0,
            )
        ]
        rows = jnp.concatenate(rows, axis=1)
        rows = lax.dot_general(picks, rows, first, preferred_element_type=F32)
        rows = jnp.where(lanes(rows.shape) < COLS, rows, 0.0)
        routed_ref[g * SLOTS : (g + 1) * SLOTS, :] = rows.astype(BF)
    routed = routed_ref[...]

    for x in range(X):
        weighted = [
            (gates[g] * pack_ref[g // C * X + x, pl.ds(g % C * PACK, SLOTS), :].astype(F32)).astype(BF)
            for g in range(QUARTERS)
        ]
        weighted = jnp.concatenate(weighted, axis=0)
        part = lax.dot_general(weighted, routed, first, preferred_element_type=F32)
        for h in range(H):
            part_ref[h, x] = dense(part[h * CHUNK : (h + 1) * CHUNK]).astype(BF)


def project_kernel(core_ref, routed_ref, pack_ref, keep_ref, send_ref):
    core = core_ref[0]
    groups = [(l, c) for c in (core, 1 - core) for l in range(L)]
    outs = [(ref, l) for ref in (keep_ref, send_ref) for l in range(L)]
    routed = jnp.concatenate(
        [routed_ref[pl.ds(pl.multiple_of((l * C + c) * SLOTS, SLOTS), SLOTS), :] for l, c in groups], axis=0
    )
    sums = [jnp.zeros((SLOTS, 1), F32)] * QUARTERS
    for x in range(X):
        w = []
        for l in range(L):
            rows = pack_ref[l * X + x, C * PACK :, :]
            rows = [rows[t * SHARE : (t + 1) * SHARE] for t in range(FULL)] + [
                last_tile(rows[FULL * SHARE :].astype(F32)).astype(BF)
            ]
            w.append(jnp.concatenate(rows, axis=1))
        w = jnp.concatenate(w, axis=0)
        proj = lax.dot_general(routed, w, (((1,), (1,)), ((), ())), preferred_element_type=F32)
        for i, (ref, l) in enumerate(outs):
            rows = proj[i * SLOTS : (i + 1) * SLOTS]
            ref[l * X + x, 0:SLOTS, :] = rows.astype(BF)
            at = pl.multiple_of(groups[i][1] * PACK, EXTRA)
            hidden = pack_ref[l * X + x, pl.ds(at, SLOTS), :].astype(F32)
            sums[i] = sums[i] + jnp.sum(hidden * rows, axis=1, keepdims=True)
    at = lanes((SLOTS, LANES))
    for i, (ref, l) in enumerate(outs):
        row = pl.multiple_of(groups[i][1] * PACK + SLOTS, EXTRA)
        tok = column(pack_ref[l * X, pl.ds(row, EXTRA), :].astype(F32)[0:1]).astype(I32)
        device, spot = tok // ROWS, tok % ROWS
        spot = jnp.where(tok < GROUP, device // X * ROWS + spot, LANES)
        for x in range(X):
            here = (at == spot) & (device % X == x)
            row = jnp.sum(jnp.where(here, sums[i], 0.0), axis=0, keepdims=True)
            ref[l * X + x, SLOTS:PACK, :] = terms(row)


def terms(row):
    high, mid, low = split3(row)
    return stack_rows((high + pltpu.roll(mid, OWNED, 1), low))


def row_of(tile):
    row = tile[0:1] + (pltpu.roll(tile[0:1], OWNED, 1) + tile[1:2])
    return jnp.where(lanes(row.shape) < OWNED, row, 0.0)


def back_kernel(sums_ref, keep_ref, other_ref, out_ref):
    for x in range(X):
        total = sums_ref[0, x].astype(F32)
        for h in range(1, H):
            total = total + sums_ref[h, x].astype(F32)
        for l in range(L):
            out_ref[l * X + x, 0:BACK, :] = total.astype(BF)
    for n in range(L * X):
        both = keep_ref[n].astype(F32) + other_ref[n].astype(F32)
        out_ref[n, BACK : BACK + SLOTS, :] = both[:SLOTS].astype(BF)
        out_ref[n, BACK + SLOTS :, :] = terms(row_of(both[SLOTS:]))


def finish_kernel(where_ref, gate_ref, got_ref, grad_ref, spread_ref, block_ref):
    both = got_ref[0, BACK:, :].astype(F32)
    for n in range(1, L * X):
        both = both + got_ref[n, BACK:, :].astype(F32)
    grad_ref[...] = (own_gate(where_ref, gate_ref) * both[:SLOTS]).astype(BF)
    shape = (E * M * N, LANES)
    row = jnp.where(lanes(shape) // ROWS == lax.broadcasted_iota(I32, shape, 0), row_of(both[SLOTS:]), 0.0)
    shape = (LANES, ROWS)
    fold = jnp.where(lax.broadcasted_iota(I32, shape, 0) % ROWS == lanes(shape), 1.0, 0.0)
    spread_ref[...] = jnp.dot(
        row, fold, precision=lax.Precision.HIGHEST, preferred_element_type=F32
    )
    low = lanes((CHUNK, LANES)) < TAIL
    for x in range(X):
        a, b = (got_ref[l * X + x, 0:BACK, :].astype(F32) for l in range(L))
        a, b = (
            [p[t * CHUNK : (t + 1) * CHUNK] for t in range(FULL)] + [last_tile(p[FULL * CHUNK :])]
            for p in (a, b)
        )
        b = [pltpu.roll(p, TAIL, 1) for p in b]
        tiles = a[:-1] + [jnp.where(low, p, r) for p, r in zip([a[-1]] + b[:-1], b)]
        block_ref[:, x * PAIR : (x + 1) * PAIR] = jnp.concatenate(tiles, axis=1).astype(BF)


def put_columns(half_ref, out_ref, core, sem):
    width, step = X * PAIR, UNITS // 4
    columns = pl.ds(pl.multiple_of(core * width, LANES), width)
    copies = []
    for i in range(4):
        rows = pl.ds(i * step, step)
        copies.append(pltpu.make_async_copy(half_ref.at[rows], out_ref.at[rows, columns], sem.at[i]))
        copies[-1].start()
    return copies


def own_half_kernel(core_ref, half_ref, out_ref, sem):
    for copy in put_columns(half_ref, out_ref, core_ref[0], sem):
        copy.wait()


def other_half_kernel(core_ref, half_ref, spread_ref, out_in_ref, out_ref, gate_ref, sem):
    copies = put_columns(half_ref, out_ref, 1 - core_ref[0], sem)
    for e in range(E):
        gate_ref[e : e + 1, :] = jnp.sum(spread_ref[e * M * N : (e + 1) * M * N, :], axis=0, keepdims=True)
    for copy in copies:
        copy.wait()


VM, SM, HBM = (pl.BlockSpec(memory_space=m) for m in (pltpu.VMEM, pltpu.SMEM, pl.ANY))


def call(kernel, places, outs, *args, scratch=(), flops=0, vmem=32, out_places=None, aliases={}):
    outs = [jax.ShapeDtypeStruct(s, d) for s, d in outs]
    nbytes = sum(a.size * a.dtype.itemsize for a in list(args) + outs)
    return pl.pallas_call(
        kernel,
        out_shape=outs,
        in_specs=places,
        out_specs=out_places or [VM] * len(outs),
        input_output_aliases=aliases,
        scratch_shapes=scratch,
        cost_estimate=pl.CostEstimate(flops=flops, bytes_accessed=nbytes, transcendentals=0),
        compiler_params=pltpu.CompilerParams(vmem_limit_bytes=vmem * 1024 * 1024),
    )(*args)


def on_device(grad_values, grad_scales, hidden_act, down_weight, slot_token, slot_count, slot_gate):
    low, core, owner = (lax.axis_index(a) for a in "lce")
    hidden, tok, gate = hidden_act[0], slot_token[0], slot_gate[0]
    where = owner[None].astype(I32)

    (both,) = call(
        first_kernel,
        [SM, SM, VM, VM, VM, VM, VM],
        [((FLAT + PACK, LANES), BF)],
        where, slot_count, tok, gate, hidden, grad_values, grad_scales.reshape(1, ROWS),
        vmem=60,
    )
    both = lax.all_gather(both, "c", axis=0)

    (send,) = call(
        tokens_kernel,
        [SM, VM],
        [((L * N * X, C * ROWS, WIDE), BF)],
        core[None].astype(I32), both,
    )
    mine = lax.all_to_all(send, ("l", "n", "x"), 0, 0)

    width = X * PAIR
    w_part = lax.dynamic_slice(down_weight, (low * SHARE, core * width), (SHARE, width))
    (pack,) = call(send_kernel, [VM, VM], [((L * X, C * PACK + W_PART, LANES), BF)], both, w_part)
    pack, mine = lax.optimization_barrier((pack, mine))
    pack = lax.all_to_all(pack, ("l", "x"), 0, 0)
    (mine,) = call(
        dense_kernel, [VM], [((QUARTERS, DENSE, LANES), BF)], mine
    )
    mine = lax.all_gather(mine, ("e", "m"), axis=0)

    part, routed = call(
        weight_kernel,
        [VM, VM],
        [((H, X, BACK, LANES), BF), ((QUARTERS * SLOTS, WIDE), BF)],
        mine, pack,
        flops=2 * QUARTERS * SLOTS * WIDE * (GROUP + X * UNITS),
    )
    keep, other = call(
        project_kernel,
        [SM, VM, VM],
        [((L * X, PACK, LANES), BF), ((L * X, PACK, LANES), BF)],
        core[None].astype(I32), routed, pack,
        flops=2 * QUARTERS * SLOTS * WIDE * X * UNITS,
    )
    other = lax.ppermute(other, "c", [(i, C - 1 - i) for i in range(C)])
    sums = lax.all_to_all(part, "h", 0, 0)

    (send,) = call(
        back_kernel,
        [VM, VM, VM],
        [((L * X, BACK + PACK, LANES), BF)],
        sums, keep, other,
    )
    got = lax.all_to_all(send, ("l", "x"), 0, 0)
    hidden_grad, spread, block = call(
        finish_kernel,
        [SM, VM, VM],
        [((SLOTS, UNITS), BF), ((E * M * N, ROWS), F32), ((CHUNK, X * PAIR), BF)],
        where, gate, got,
    )
    spread = lax.all_to_all(spread, ("e", "m", "n"), 0, 0, tiled=True)

    block = lax.all_gather(block, "h", axis=0, tiled=True)
    block, spread = lax.optimization_barrier((block, spread))
    other = lax.ppermute(block, "c", [(i, C - 1 - i) for i in range(C)])
    where = core[None].astype(I32)
    sem = [pltpu.SemaphoreType.DMA((4,))]
    (whole,) = call(
        own_half_kernel, [SM, VM], [((UNITS, WIDTH), BF)], where, block, scratch=sem, out_places=[HBM]
    )
    weight_grad, gate_grad = call(
        other_half_kernel,
        [SM, HBM, VM, HBM],
        [((UNITS, WIDTH), BF), ((E, ROWS), F32)],
        where, other, spread, whole,
        scratch=sem,
        out_places=[HBM, VM],
        aliases={3: 0},
    )
    return hidden_grad[None], weight_grad, gate_grad.T


def solution(mesh):
    fine = jax.sharding.Mesh(mesh.devices.reshape(SIZES), DP + EXPERT)
    return jax.shard_map(
        on_device,
        mesh=fine,
        in_specs=(
            P(DP + EXPERT, None),
            P(DP + EXPERT),
            P(DP, None, EXPERT),
            P(EXPERT, None),
            P(DP, None, None),
            P(DP, None),
            P(DP, None, None),
        ),
        out_specs=(P(DP, None, EXPERT), P(EXPERT, None), P(DP + EXPERT, None)),
        check_vma=False,
    )
```
